32 devices in a mesh: rep: 2 (over y), gx: 4 (over z), gy: 2 (over x), gz: 2 (over core).
Axes of the slice: x: 2, y: 2, z: 4, core: 2. Of those that a mesh axis runs over, the one named last changes fastest.
Arguments:
- hidden: bfloat16 [128, 16384], P(('rep', 'gx'), ('gy', 'gz')), parts along dimension 0
- attention_norm_gain: bfloat16 [16384], P(('gy', 'gz')), may hold values from 0.099609375 to 1.8984375
- query_weight: bfloat16 [16384, 16384], P(('gy', 'gz'), 'gx'), may hold values from -0.046875 to 0.046875
- slot_down_factors: bfloat16 [4, 16384, 64], P('gx', ('gy', 'gz')), may hold values from -0.046875 to 0.046875
- adapter_up_factors: bfloat16 [4, 64, 16384], P(None, None, 'gx'), may hold values from -0.75 to 0.75
- adapter_of_row: int32 [128], P('rep'), parts along dimension 0, may hold values from 0 to 4, as said below
- padded_adapter_rank: int32 [4], replicated, may hold values from 16 to 64, as said below
- adapter_in_slot: int32 [4], replicated, may hold values from 0 to 3, each once
- segment_starts: int32 [10], P('rep'), parts along dimension 0, may hold values from 0 to 34, as said below
Outputs:
- query: bfloat16 [128, 16384], P(('rep', 'gy', 'gz'), 'gx'), parts along dimension 0
The draws below stay inside these ranges and needn't reach their ends.
There are 2 independent parts, one for each index of `rep`. The reference program is written for one: setup_inputs(seed, part) draws one part's arguments, and reference() takes and returns one part's arrays. A program takes and returns all parts, laid end to end along the dimension named above; an argument that names none is the same for every part. Nothing has to cross between parts.
Inputs may be any that keep to these rules, and one draw needn't show every extreme that they name: `adapter_of_row`: Non-decreasing; rows of adapter a lie from segment_starts[a] to segment_starts[a+1] - 1; rows from segment_starts[4] on have 4. Every adapter has 1 to 16 rows, one has exactly 16 and one exactly 1. `padded_adapter_rank`: multiples of 16; some adapter has 64 and some 16. segment_starts[0] = 0, increasing, consistent with adapter_of_row; segment_starts[4] is the number of adapted rows. `adapter_in_slot`: storage slot s lies on index s // 1 of gx.
All inputs are finite; a program needn't handle non-finite values.
Results may differ from the reference program's by a relative error of at most 0.0052.
Values may be sent and summed in bfloat16 or wider, within the bound.
No kernel may reach another device: no remote copies, remote signals or barrier semaphores. Data moves between devices by JAX's collectives and lax.ppermute only.
A program may use at most 128 MiB of HBM per device.

```python
import jax
import jax.numpy as jnp
from jax import lax

MODEL_WIDTH = 16384
QUERY_FEATURES = 16384
LARGEST_RANK = 64
RBLK = 16
ROWS = 64
ADAPTER_COUNT = 4
CAP = 16


def segment_counts(key):
    key_order, key_counts = jax.random.split(key)
    half = ADAPTER_COUNT // 2
    order = jax.random.permutation(key_order, ADAPTER_COUNT)
    first = jax.random.randint(key_counts, (half,), 1, CAP + 1)
    first = jnp.where(jnp.arange(half) == 0, CAP, first)
    paired = jnp.concatenate([first, CAP + 1 - first]).astype(jnp.int32)
    counts = jnp.zeros((ADAPTER_COUNT,), jnp.int32).at[order].set(paired)
    return counts.astype(jnp.int32)


def draw_adapter_of_row(key, part):
    counts = segment_counts(key)
    ends = jnp.cumsum(counts)
    row_index = jnp.arange(ROWS, dtype=jnp.int32)
    return jnp.sum((row_index[:, None] >= ends[None, :]).astype(jnp.int32), axis=1).astype(jnp.int32)


def draw_segment_starts(key, part):
    counts = segment_counts(key)
    return jnp.concatenate([jnp.zeros((1,), jnp.int32), jnp.cumsum(counts).astype(jnp.int32)])


def draw_padded_adapter_rank(key, part):
    key = jax.random.fold_in(key, 7)
    key_levels, key_high, key_low = jax.random.split(key, 3)
    levels = jax.random.randint(key_levels, (ADAPTER_COUNT,), 1, LARGEST_RANK // RBLK + 1)
    high_index = jax.random.randint(key_high, (), 0, ADAPTER_COUNT)
    low_index = (high_index + jax.random.randint(key_low, (), 1, ADAPTER_COUNT)) % ADAPTER_COUNT
    position = jnp.arange(ADAPTER_COUNT)
    levels = jnp.where(position == high_index, LARGEST_RANK // RBLK, levels)
    levels = jnp.where(position == low_index, 1, levels)
    return (levels * RBLK).astype(jnp.int32)


def draw_hidden(key, part):
    key = jax.random.fold_in(key, 5)
    key_base, key_rows = jax.random.split(key)
    columns = jnp.arange(MODEL_WIDTH, dtype=jnp.float32) / MODEL_WIDTH
    values = jax.random.normal(key_base, (ROWS, MODEL_WIDTH), jnp.float32)
    row_scale = jnp.exp(jax.random.uniform(key_rows, (ROWS, 1), jnp.float32) * jnp.log(10.0))
    col_scale = jnp.power(10.0, columns)
    return (values * row_scale * col_scale[None, :]).astype(jnp.bfloat16)


def block_scale(rng, shape, cuts, least, top_value):
    def one(axis_at, blocks):
        steps = jax.random.uniform(jax.random.fold_in(jax.random.fold_in(rng, 6), axis_at), (blocks,), jnp.float32, least / len(cuts), top_value / len(cuts))
        return jnp.repeat(jnp.exp(steps), shape[axis_at] // blocks).reshape((-1,) + (1,) * (len(shape) - axis_at - 1))

    factor_of = one(*cuts[0])
    for cut in cuts[1:]:
        factor_of = factor_of * one(*cut)
    return factor_of


def noise(stream_key, dims, width, most, cuts=(), held_as=jnp.bfloat16):
    level = block_scale(stream_key, dims, cuts, -0.22, 0.18) if cuts else 1.0
    drawn = jax.random.normal(stream_key, dims, jnp.float32) * width * level
    return jnp.minimum(jnp.maximum(drawn, -most), most).astype(held_as)


def setup_inputs(seed: int = 0, part: int = 0) -> dict:
    streams_of = jax.random.split(jax.random.key(seed), 10)
    own_keys = jax.random.split(jax.random.fold_in(streams_of[9], part), 10)
    hidden = draw_hidden(jax.random.fold_in(jax.random.fold_in(streams_of[9], part), 71), part)
    attention_norm_gain = jnp.clip(1.0 + 0.18 * jax.random.normal(streams_of[1], (MODEL_WIDTH,), jnp.float32), 0.099609375, 1.8984375).astype(jnp.bfloat16)
    query_weight = noise(streams_of[2], (MODEL_WIDTH, QUERY_FEATURES), MODEL_WIDTH ** -0.5, 0.046875, ((0, 4), (1, 4)))
    slot_down_factors = noise(streams_of[3], (ADAPTER_COUNT, MODEL_WIDTH, LARGEST_RANK), MODEL_WIDTH ** -0.5, 0.046875, ((0, 4), (1, 4)))
    adapter_up_factors = noise(streams_of[4], (ADAPTER_COUNT, LARGEST_RANK, QUERY_FEATURES), LARGEST_RANK ** -0.5, 0.75, ((2, 4),))
    adapter_of_row = draw_adapter_of_row(jax.random.fold_in(jax.random.fold_in(streams_of[9], part), 71), part)
    padded_adapter_rank = draw_padded_adapter_rank(jax.random.fold_in(streams_of[9], 71), part)
    adapter_in_slot = jax.random.permutation(streams_of[7], ADAPTER_COUNT).astype(jnp.int32)
    segment_starts = draw_segment_starts(jax.random.fold_in(jax.random.fold_in(streams_of[9], part), 71), part)
    return dict(hidden=hidden, attention_norm_gain=attention_norm_gain, query_weight=query_weight, slot_down_factors=slot_down_factors, adapter_up_factors=adapter_up_factors, adapter_of_row=adapter_of_row, padded_adapter_rank=padded_adapter_rank, adapter_in_slot=adapter_in_slot, segment_starts=segment_starts)


EPSILON = 1e-05
ADAPTER_ALPHA = 32.0

def reference(hidden, attention_norm_gain, query_weight, slot_down_factors, adapter_up_factors, adapter_of_row, padded_adapter_rank, adapter_in_slot, segment_starts):
    hidden_f32 = hidden.astype(jnp.float32)
    mean_sq = lax.optimization_barrier(jnp.mean(hidden_f32 * hidden_f32, axis=1, keepdims=True))
    normed = (hidden_f32 * lax.rsqrt(mean_sq + EPSILON) * attention_norm_gain.astype(jnp.float32)).astype(jnp.bfloat16)
    base_output = jnp.dot(normed, query_weight, preferred_element_type=jnp.float32)
    flattened_down = jnp.transpose(slot_down_factors, (1, 0, 2)).reshape(MODEL_WIDTH, ADAPTER_COUNT * LARGEST_RANK)
    query_projected = jnp.dot(normed, flattened_down, preferred_element_type=jnp.float32).reshape(ROWS, ADAPTER_COUNT, LARGEST_RANK)
    chosen = adapter_in_slot[None, :] == adapter_of_row[:, None]
    selected_rows = lax.optimization_barrier(jnp.sum(jnp.where(chosen[:, :, None], query_projected, jnp.zeros((), jnp.float32)), axis=1))
    clipped_ids = jnp.minimum(adapter_of_row, ADAPTER_COUNT - 1).astype(jnp.int32)
    rank_vector = jnp.take(padded_adapter_rank, clipped_ids)
    seg_first = jnp.take(segment_starts, clipped_ids)
    seg_after = jnp.take(segment_starts, clipped_ids + 1)
    row_index = jnp.arange(ROWS, dtype=jnp.int32)
    inside = (row_index >= seg_first) & (row_index < seg_after)
    col_index = jnp.arange(LARGEST_RANK, dtype=jnp.int32)
    keep_mask = (col_index[None, :] < rank_vector[:, None]) & inside[:, None]
    scaled_delta = selected_rows * (ADAPTER_ALPHA / rank_vector.astype(jnp.float32))[:, None]
    down = jnp.where(keep_mask, scaled_delta, jnp.zeros((), jnp.float32)).astype(jnp.bfloat16)
    onehot = adapter_of_row[:, None] == jnp.arange(ADAPTER_COUNT, dtype=jnp.int32)[None, :]
    spread_rows = jnp.where(onehot[:, :, None], down[:, None, :], jnp.zeros((), jnp.bfloat16)).reshape(ROWS, ADAPTER_COUNT * LARGEST_RANK)
    adapter_delta = jnp.dot(spread_rows, adapter_up_factors.reshape(ADAPTER_COUNT * LARGEST_RANK, QUERY_FEATURES), preferred_element_type=jnp.float32)
    return (base_output + adapter_delta).astype(jnp.bfloat16)
```

```python
import functools

import jax
import jax.numpy as jnp
from jax import lax
from jax.experimental import pallas as pl
from jax.experimental.pallas import tpu as pltpu
from jax.sharding import PartitionSpec as P

EPSILON = 1e-05
ADAPTER_ALPHA = 32.0
LANES = 128
MIB = 1 << 20

VMEM = pl.BlockSpec(memory_space=pltpu.VMEM)
SMEM = pl.BlockSpec(memory_space=pltpu.SMEM)
ANY = pl.BlockSpec(memory_space=pl.ANY)


def params(mib):
    return pltpu.CompilerParams(vmem_limit_bytes=mib * MIB)


def cost(flops, moved):
    return pl.CostEstimate(flops=flops, bytes_accessed=moved, transcendentals=0)


def fetch_kernel(pieces, w_hbm, gain_ref, *refs):
    gain_out, chunks, sems = refs[0], refs[1:-1], refs[-1]
    depth = w_hbm.shape[0] // pieces
    copies = []
    first = 0
    for c, chunk in enumerate(chunks):
        width = chunk.shape[1]
        for p in range(pieces):
            here = pl.ds(p * depth, depth)
            copies.append(
                pltpu.make_async_copy(
                    w_hbm.at[here, pl.ds(first, width)], chunk.at[here], sems.at[c, p]
                )
            )
        first += width
    for copy in copies:
        copy.start()
    gain_out[...] = gain_ref[...].astype(jnp.float32)
    for copy in copies:
        copy.wait()


def rows_kernel(n, *refs):
    place, rank_ref, slot_ref, start_ref, gain_ref, down_ref = refs[:6]
    blocks = refs[6 : 6 + n]
    x_ref, small_ref = refs[6 + n :]
    home = place[0]
    block_rows = blocks[0].shape[0]
    rows = n * block_rows
    gain = gain_ref[...]
    for k in range(n):
        source = lax.rem(home - k + n, n)
        begin = pl.multiple_of(source * block_rows, block_rows)
        values = blocks[k][...].astype(jnp.float32)
        squares = jnp.sum(values * values, axis=1, keepdims=True)
        x_ref[pl.ds(begin, block_rows), :] = (values * gain).astype(jnp.bfloat16)
        small_ref[pl.ds(begin, block_rows), LANES:] = jnp.broadcast_to(squares, (block_rows, LANES))
    slots, rank_columns = down_ref.shape[0], down_ref.shape[1]
    row = lax.broadcasted_iota(jnp.int32, (rows, rank_columns), 0)
    col = lax.broadcasted_iota(jnp.int32, (rows, rank_columns), 1)
    total = jnp.zeros((rows, rank_columns), jnp.float32)
    for s in range(slots):
        adapter = slot_ref[home * slots + s]
        rank = rank_ref[adapter]
        live = (row >= start_ref[adapter]) & (row < start_ref[adapter + 1]) & (col < rank)
        projected = lax.dot_general(
            x_ref[...], down_ref[s], (((1,), (1,)), ((), ())), preferred_element_type=jnp.float32
        )
        scale = ADAPTER_ALPHA / jnp.full((rows, rank_columns), rank, jnp.int32).astype(jnp.float32)
        total = total + jnp.where(live, projected * scale, 0.0)
    small_ref[:, :LANES] = jnp.zeros((rows, LANES), jnp.float32)
    small_ref[:, :rank_columns] = total


def slice_kernel(n, offset, place, small_ref, *outs):
    g = place[1]
    rows_here = outs[0].shape[0]
    for k in range(n):
        owner = offset(g, k)
        begin = pl.multiple_of(owner * rows_here, rows_here)
        outs[k][...] = small_ref[pl.ds(begin, rows_here), :]


def chunk_kernel(n, offset, step, place, x_ref, w_ref, *refs):
    outs, acc = refs[:n], refs[n]
    g = place[1]
    rows_here, width = outs[0].shape
    for c in range(0, width, step):
        acc[:, c : c + step] = jnp.dot(
            x_ref[...], w_ref[:, c : c + step], preferred_element_type=jnp.float32
        )
    for k in range(n):
        begin = pl.multiple_of(offset(g, k) * rows_here, rows_here)
        outs[k][...] = acc[pl.ds(begin, rows_here), :].astype(outs[k].dtype)


def final_kernel(n, n_small, n_down, chunks, width, *refs):
    place, start_ref, up_ref = refs[:3]
    refs = refs[3:]
    smalls, refs = refs[:n_small], refs[n_small:]
    downs, refs = refs[:n_down], refs[n_down:]
    parts, out_ref = refs[: n * chunks], refs[n * chunks]
    g = place[1]
    rows_here = out_ref.shape[0]
    adapters, rank_columns, _ = up_ref.shape
    own = smalls[0][...]
    for other in smalls[1:]:
        own = own + other[...]
    mean_sq = own[:, LANES : LANES + 1] / width
    scale = lax.rsqrt(mean_sq + EPSILON)
    down = own[:, :rank_columns]
    for other in downs:
        down = down + other[:, :rank_columns]
    live_rows = mean_sq < jnp.inf
    down = jnp.where(live_rows, down * scale, 0.0).astype(jnp.bfloat16)
    row = lax.broadcasted_iota(jnp.int32, (rows_here, rank_columns), 0) + g * rows_here
    spread = jnp.concatenate(
        [
            jnp.where((row >= start_ref[a]) & (row < start_ref[a + 1]), down, jnp.zeros_like(down))
            for a in range(adapters)
        ],
        axis=1,
    )
    columns = out_ref.shape[1] // chunks
    for c in range(chunks):
        here = slice(c * columns, (c + 1) * columns)
        delta = jnp.zeros((rows_here, columns), jnp.float32)
        total = parts[c * n][...]
        for k in range(1, n):
            total = total + parts[c * n + k][...].astype(jnp.float32)
        up = up_ref[:, :, here].reshape(adapters * rank_columns, columns)
        delta = jnp.dot(spread, up, preferred_element_type=jnp.float32)
        base = jnp.where(live_rows, total * scale, 0.0)
        out_ref[:, here] = (base + delta).astype(out_ref.dtype)


def body(
    hidden,
    attention_norm_gain,
    query_weight,
    slot_down_factors,
    adapter_up_factors,
    adapter_of_row,
    padded_adapter_rank,
    adapter_in_slot,
    segment_starts,
):
    n_x, n_y, n_z = lax.axis_size("gx"), lax.axis_size("gy"), lax.axis_size("gz")
    groups = n_y * n_z
    block_rows, depth = hidden.shape
    columns = query_weight.shape[1]
    rows = n_x * block_rows
    rows_here = rows // groups
    home = lax.axis_index("gx")
    place = jnp.stack([home, lax.axis_index(("gy", "gz"))]).astype(jnp.int32)

    def offset(g, k):
        y = lax.rem(g // n_z + k // n_z, n_y)
        z = lax.rem(lax.rem(g, n_z) + k % n_z, n_z)
        return y * n_z + z

    def send_x(value, k):
        return lax.ppermute(value, "gx", [(j, (j + k) % n_x) for j in range(n_x)])

    def send_g(value, k):
        pairs = []
        for g in range(groups):
            y, z = (g // n_z + k // n_z) % n_y, (g % n_z + k % n_z) % n_z
            pairs.append((g, y * n_z + z))
        return lax.ppermute(value, ("gy", "gz"), pairs)

    blocks = [hidden] + [send_x(hidden, k) for k in range(1, n_x)]

    chunks = 4
    width = columns // chunks
    pieces = 4
    gain, *weights = pl.pallas_call(
        functools.partial(fetch_kernel, pieces),
        out_shape=[jax.ShapeDtypeStruct((1, depth), jnp.float32)]
        + [pltpu.VMEM((depth, width), query_weight.dtype)] * chunks,
        in_specs=[ANY, VMEM],
        out_specs=[VMEM] * (1 + chunks),
        scratch_shapes=[pltpu.SemaphoreType.DMA((chunks, pieces))],
        cost_estimate=cost(0, 2 * query_weight.size),
        compiler_params=params(12),
        name="fetch_weight",
    )(query_weight, attention_norm_gain.reshape(1, depth))

    x, small = pl.pallas_call(
        functools.partial(rows_kernel, n_x),
        out_shape=(
            jax.ShapeDtypeStruct((rows, depth), jnp.bfloat16),
            jax.ShapeDtypeStruct((rows, 2 * LANES), jnp.float32),
        ),
        in_specs=[SMEM] * 4 + [VMEM] * (2 + n_x),
        out_specs=(VMEM, VMEM),
        compiler_params=params(12),
        name="scaled_rows",
    )(
        place,
        padded_adapter_rank,
        adapter_in_slot,
        segment_starts,
        gain,
        jnp.swapaxes(slot_down_factors, 1, 2),
        *blocks,
    )

    small_parts = pl.pallas_call(
        functools.partial(slice_kernel, groups, offset),
        out_shape=[jax.ShapeDtypeStruct((rows_here, 2 * LANES), jnp.float32)] * groups,
        in_specs=[SMEM, VMEM],
        out_specs=[VMEM] * groups,
        compiler_params=params(12),
        name="small_parts",
    )(place, small)
    smalls = [small_parts[0]] + [send_g(small_parts[k], k) for k in range(1, groups)]

    step = min(width, 512)
    parts = []
    for c in range(chunks):
        dtypes = [jnp.float32] + [jnp.bfloat16] * (groups - 1)
        made = pl.pallas_call(
            functools.partial(chunk_kernel, groups, offset, step),
            out_shape=[jax.ShapeDtypeStruct((rows_here, width), t) for t in dtypes],
            in_specs=[SMEM, VMEM, VMEM],
            out_specs=[VMEM] * groups,
            scratch_shapes=[pltpu.VMEM((rows, width), jnp.float32)],
            cost_estimate=cost(2 * rows * depth * width, 2 * depth * width),
            compiler_params=params(12),
        name="product",
        )(place, x, pltpu.with_memory_space_constraint(weights[c], pltpu.VMEM))
        parts += [made[0]] + [send_g(made[k], k) for k in range(1, groups)]
        if c == 0:
            down = smalls[0][:, :LANES]
            for other in smalls[1:]:
                down = down + other[:, :LANES]
            downs = [send_x(down, k) for k in range(1, n_x)]

    return pl.pallas_call(
        functools.partial(
            final_kernel, groups, groups, n_x - 1, chunks, depth * groups
        ),
        out_shape=jax.ShapeDtypeStruct((rows_here, columns), jnp.bfloat16),
        in_specs=[SMEM] * 2 + [VMEM] * (1 + groups + n_x - 1 + groups * chunks),
        out_specs=VMEM,
        compiler_params=params(12),
        name="query_rows",
    )(place, segment_starts, adapter_up_factors, *smalls, *downs, *parts)


def solution(mesh):
    return jax.shard_map(
        body,
        mesh=mesh,
        in_specs=(
            P(("rep", "gx"), ("gy", "gz")),
            P(("gy", "gz")),
            P(("gy", "gz"), "gx"),
            P("gx", ("gy", "gz"), None),
            P(None, None, "gx"),
            P("rep"),
            P(),
            P(),
            P("rep"),
        ),
        out_specs=P(("rep", "gy", "gz"), "gx"),
        check_vma=False,
    )
```

```python
import functools

import jax
import jax.numpy as jnp
from jax import lax
from jax.experimental import pallas as pl
from jax.experimental.pallas import tpu as pltpu
from jax.sharding import PartitionSpec as P

EPSILON = 1e-05
ADAPTER_ALPHA = 32.0
LANES = 128
MIB = 1 << 20

VMEM = pl.BlockSpec(memory_space=pltpu.VMEM)
SMEM = pl.BlockSpec(memory_space=pltpu.SMEM)
ANY = pl.BlockSpec(memory_space=pl.ANY)


def params(mib):
    return pltpu.CompilerParams(vmem_limit_bytes=mib * MIB)


def cost(flops, moved):
    return pl.CostEstimate(flops=flops, bytes_accessed=moved, transcendentals=0)


def weight_copies(w_hbm, first, w_vmem, sems):
    pieces = sems.shape[0]
    depth, width = w_vmem.shape
    step = depth // pieces
    return [
        pltpu.make_async_copy(
            w_hbm.at[pl.ds(p * step, step), pl.ds(first, width)],
            w_vmem.at[pl.ds(p * step, step)],
            sems.at[p],
        )
        for p in range(pieces)
    ]


def fetch_kernel(w_hbm, gain_ref, gain_out, w_vmem, sems):
    copies = weight_copies(w_hbm, 0, w_vmem, sems)
    for copy in copies:
        copy.start()
    gain_out[...] = gain_ref[...].astype(jnp.float32).reshape(gain_out.shape)
    for copy in copies:
        copy.wait()


def multiply(x_ref, w_ref, out_ref, first, step):
    width = w_ref.shape[1]
    for c in range(0, width, step):
        out_ref[:, first + c : first + c + step] = jnp.dot(
            x_ref[...], w_ref[:, c : c + step], preferred_element_type=jnp.float32
        )


def first_kernel(n, step, width, *refs):
    rank_ref, slot_ref, start_ref, gain_ref, down_ref, w_hbm, w_ref = refs[:7]
    blocks = refs[7 : 7 + n]
    x_ref, square_ref, down_out, base_ref, rest_ref, sems = refs[7 + n :]
    copies = weight_copies(w_hbm, w_ref.shape[1], rest_ref, sems)
    for copy in copies:
        copy.start()
    home = lax.axis_index("gx")
    block_rows = blocks[0].shape[0]
    rows = n * block_rows
    gain = gain_ref[...]
    for k in range(n):
        source = lax.rem(home - k + n, n)
        begin = pl.multiple_of(source * block_rows, block_rows)
        values = blocks[k][...].astype(jnp.float32)
        squares = jnp.sum(values * values, axis=1, keepdims=True) / width
        x_ref[pl.ds(begin, block_rows), :] = (values * gain).astype(jnp.bfloat16)
        square_ref[pl.ds(begin, block_rows), :] = jnp.broadcast_to(squares, (block_rows, LANES))
    slots, rank_columns = down_ref.shape[0], down_ref.shape[1]
    row = lax.broadcasted_iota(jnp.int32, (rows, rank_columns), 0)
    col = lax.broadcasted_iota(jnp.int32, (rows, rank_columns), 1)
    total = jnp.zeros((rows, rank_columns), jnp.float32)
    for s in range(slots):
        adapter = slot_ref[home * slots + s]
        rank = rank_ref[adapter]
        live = (row >= start_ref[adapter]) & (row < start_ref[adapter + 1]) & (col < rank)
        projected = lax.dot_general(
            x_ref[...], down_ref[s], (((1,), (1,)), ((), ())), preferred_element_type=jnp.float32
        )
        scale = ADAPTER_ALPHA / jnp.full((rows, rank_columns), rank, jnp.int32).astype(jnp.float32)
        total = total + jnp.where(live, projected * scale, 0.0)
    down_out[...] = jnp.zeros(down_out.shape, down_out.dtype)
    down_out[:, :rank_columns] = total.astype(down_out.dtype)
    multiply(x_ref, w_ref, base_ref, 0, step)
    for copy in copies:
        copy.wait()


def second_kernel(n_x, groups, step, offset, *refs):
    start_ref, x_ref, square_ref, base_ref, w_ref, up_ref = refs[:6]
    downs = refs[6 : 6 + n_x]
    outs, acc = refs[6 + n_x : -1], refs[-1]
    rows = x_ref.shape[0]
    done = base_ref.shape[1]
    columns = done + w_ref.shape[1]
    adapters, rank_columns, _ = up_ref.shape
    down = downs[0][:, :rank_columns]
    for other in downs[1:]:
        down = down + other[:, :rank_columns]
    row = lax.broadcasted_iota(jnp.int32, (rows, rank_columns), 0)
    spread = jnp.concatenate(
        [
            jnp.where((row >= start_ref[a]) & (row < start_ref[a + 1]), down, jnp.zeros_like(down))
            for a in range(adapters)
        ],
        axis=1,
    )
    for c in range(0, columns, step):
        here = slice(c, c + step)
        up = up_ref[:, :, here].reshape(adapters * rank_columns, step)
        delta = jnp.dot(spread, up, preferred_element_type=jnp.float32)
        if c < done:
            base = base_ref[:, here]
        else:
            base = jnp.dot(
                x_ref[...], w_ref[:, c - done : c - done + step], preferred_element_type=jnp.float32
            )
        acc[:, here] = base + delta
    square = square_ref[...]
    high = square.astype(jnp.bfloat16).astype(jnp.float32)
    low = jnp.where(high < jnp.inf, square - high, 0.0)
    lane = lax.broadcasted_iota(jnp.int32, square.shape, 1)
    acc[:, columns:] = jnp.where(lane < LANES // 2, high, low)
    g = lax.axis_index(("gy", "gz"))
    rows_here = outs[0].shape[0]
    for k in range(groups):
        begin = pl.multiple_of(offset(g, k) * rows_here, rows_here)
        outs[k][...] = acc[pl.ds(begin, rows_here), :].astype(outs[k].dtype)


def final_kernel(*refs):
    parts, out_ref = refs[:-1], refs[-1]
    columns = out_ref.shape[1]
    total = parts[0][...]
    for other in parts[1:]:
        total = total + other[...].astype(jnp.float32)
    mean_sq = total[:, columns : columns + 1] + total[:, columns + LANES - 1 :]
    scale = lax.rsqrt(mean_sq + EPSILON)
    value = jnp.where(mean_sq < jnp.inf, total[:, :columns] * scale, 0.0)
    out_ref[...] = value.astype(out_ref.dtype)


def body(
    hidden,
    attention_norm_gain,
    query_weight,
    slot_down_factors,
    adapter_up_factors,
    adapter_of_row,
    padded_adapter_rank,
    adapter_in_slot,
    segment_starts,
):
    n_x, n_y, n_z = lax.axis_size("gx"), lax.axis_size("gy"), lax.axis_size("gz")
    groups = n_y * n_z
    block_rows, depth = hidden.shape
    columns = query_weight.shape[1]
    rows = n_x * block_rows
    rows_here = rows // groups

    def offset(g, k):
        y = lax.rem(g // n_z + k // n_z, n_y)
        z = lax.rem(lax.rem(g, n_z) + k % n_z, n_z)
        return y * n_z + z

    def send_x(value, k):
        return lax.ppermute(value, "gx", [(j, (j + k) % n_x) for j in range(n_x)])

    def send_g(value, k):
        pairs = []
        for g in range(groups):
            y, z = (g // n_z + k // n_z) % n_y, (g % n_z + k % n_z) % n_z
            pairs.append((g, y * n_z + z))
        return lax.ppermute(value, ("gy", "gz"), pairs)

    blocks = [hidden] + [send_x(hidden, k) for k in range(1, n_x)]

    step = min(512, columns // 4)
    first = columns * 5 // 8 // step * step
    rest = columns - first
    pieces = 8
    f32, bf16 = jnp.float32, jnp.bfloat16
    gain, weight = pl.pallas_call(
        fetch_kernel,
        out_shape=(
            jax.ShapeDtypeStruct((1, depth), f32),
            pltpu.VMEM((depth, first), query_weight.dtype),
        ),
        in_specs=[ANY, VMEM],
        out_specs=(VMEM, VMEM),
        scratch_shapes=[pltpu.SemaphoreType.DMA((pieces,))],
        cost_estimate=cost(0, 2 * depth * first),
        compiler_params=params(12),
        name="fetch_weight",
    )(query_weight, attention_norm_gain)

    x, square, down, base, weight_rest = pl.pallas_call(
        functools.partial(first_kernel, n_x, step, depth * groups),
        out_shape=(
            jax.ShapeDtypeStruct((rows, depth), bf16),
            jax.ShapeDtypeStruct((rows, LANES), f32),
            jax.ShapeDtypeStruct((rows, LANES), bf16),
            jax.ShapeDtypeStruct((rows, first), f32),
            pltpu.VMEM((depth, rest), query_weight.dtype),
        ),
        in_specs=[SMEM] * 3 + [VMEM] * 2 + [ANY] + [VMEM] * (1 + n_x),
        out_specs=(VMEM,) * 5,
        scratch_shapes=[pltpu.SemaphoreType.DMA((pieces,))],
        cost_estimate=cost(2 * rows * depth * first, 2 * depth * rest),
        compiler_params=params(16),
        name="first_columns",
    )(
        padded_adapter_rank,
        adapter_in_slot,
        segment_starts,
        gain,
        jnp.swapaxes(slot_down_factors, 1, 2),
        query_weight,
        pltpu.with_memory_space_constraint(weight, pltpu.VMEM),
        *blocks,
    )

    downs = [down] + [send_x(down, k) for k in range(1, n_x)]

    dtypes = [f32] + [bf16] * (groups - 1)
    made = pl.pallas_call(
        functools.partial(second_kernel, n_x, groups, step, offset),
        out_shape=[jax.ShapeDtypeStruct((rows_here, columns + LANES), t) for t in dtypes],
        in_specs=[SMEM] + [VMEM] * (5 + n_x),
        out_specs=[VMEM] * groups,
        scratch_shapes=[pltpu.VMEM((rows, columns + LANES), f32)],
        cost_estimate=cost(2 * rows * depth * rest, 2 * depth * rest),
        compiler_params=params(16),
        name="last_columns",
    )(
        segment_starts,
        x,
        square,
        base,
        pltpu.with_memory_space_constraint(weight_rest, pltpu.VMEM),
        adapter_up_factors,
        *downs,
    )
    parts = [made[0]] + [send_g(made[k], k) for k in range(1, groups)]

    return pl.pallas_call(
        final_kernel,
        out_shape=jax.ShapeDtypeStruct((rows_here, columns), bf16),
        in_specs=[VMEM] * groups,
        out_specs=VMEM,
        compiler_params=params(12),
        name="query_rows",
    )(*parts)


def solution(mesh):
    return jax.shard_map(
        body,
        mesh=mesh,
        in_specs=(
            P(("rep", "gx"), ("gy", "gz")),
            P(("gy", "gz")),
            P(("gy", "gz"), "gx"),
            P("gx", ("gy", "gz"), None),
            P(None, None, "gx"),
            P("rep"),
            P(),
            P(),
            P("rep"),
        ),
        out_specs=P(("rep", "gy", "gz"), "gx"),
        check_vma=False,
    )
```

```python
import functools

import jax
import jax.numpy as jnp
from jax import lax
from jax.experimental import pallas as pl
from jax.experimental.pallas import tpu as pltpu
from jax.sharding import PartitionSpec as P

EPSILON = 1e-05
ADAPTER_ALPHA = 32.0
LANES = 128
MIB = 1 << 20

VMEM = pl.BlockSpec(memory_space=pltpu.VMEM)
SMEM = pl.BlockSpec(memory_space=pltpu.SMEM)
ANY = pl.BlockSpec(memory_space=pl.ANY)


def params(mib):
    return pltpu.CompilerParams(vmem_limit_bytes=mib * MIB)


def cost(flops, moved):
    return pl.CostEstimate(flops=flops, bytes_accessed=moved, transcendentals=0)


def weight_copies(w_hbm, first, w_vmem, sems):
    pieces = sems.shape[0]
    depth, width = w_vmem.shape
    step = depth // pieces
    return [
        pltpu.make_async_copy(
            w_hbm.at[pl.ds(p * step, step), pl.ds(first, width)],
            w_vmem.at[pl.ds(p * step, step)],
            sems.at[p],
        )
        for p in range(pieces)
    ]


def fetch_kernel(n, w_hbm, token_ref, *refs):
    weights, sems = refs[:n], refs[n]
    copies = []
    first = 0
    for j, w_vmem in enumerate(weights):
        copies += weight_copies(w_hbm, first, w_vmem, sems.at[j])
        first += w_vmem.shape[1]
    for copy in copies:
        copy.start()
    token_ref[...] = jnp.zeros(token_ref.shape, token_ref.dtype)
    for copy in copies:
        copy.wait()


def rows_kernel(n, width, *refs):
    rank_ref, slot_ref, start_ref, gain_ref, down_ref, _ = refs[:6]
    blocks = refs[6 : 6 + n]
    x_ref, square_ref, down_out = refs[6 + n :]
    home = lax.axis_index("gx")
    block_rows = blocks[0].shape[0]
    rows = n * block_rows
    gain = gain_ref[...].astype(jnp.float32).reshape(1, gain_ref.shape[0])
    for k in range(n):
        source = lax.rem(home - k + n, n)
        begin = pl.multiple_of(source * block_rows, block_rows)
        values = blocks[k][...].astype(jnp.float32)
        squares = jnp.sum(values * values, axis=1, keepdims=True) / width
        x_ref[pl.ds(begin, block_rows), :] = (values * gain).astype(jnp.bfloat16)
        square_ref[pl.ds(begin, block_rows), :] = jnp.broadcast_to(squares, (block_rows, LANES))
    slots, rank_columns = down_ref.shape[0], down_ref.shape[1]
    row = lax.broadcasted_iota(jnp.int32, (rows, rank_columns), 0)
    col = lax.broadcasted_iota(jnp.int32, (rows, rank_columns), 1)
    total = jnp.zeros((rows, rank_columns), jnp.float32)
    for s in range(slots):
        adapter = slot_ref[home * slots + s]
        rank = rank_ref[adapter]
        live = (row >= start_ref[adapter]) & (row < start_ref[adapter + 1]) & (col < rank)
        projected = lax.dot_general(
            x_ref[...], down_ref[s], (((1,), (1,)), ((), ())), preferred_element_type=jnp.float32
        )
        scale = ADAPTER_ALPHA / jnp.full((rows, rank_columns), rank, jnp.int32).astype(jnp.float32)
        total = total + jnp.where(live, projected * scale, 0.0)
    down_out[...] = jnp.zeros(down_out.shape, down_out.dtype)
    down_out[:, :rank_columns] = total.astype(down_out.dtype)


def product_kernel(n_x, n_w, groups, step, offset, *refs):
    start_ref, x_ref, square_ref, up_ref = refs[:4]
    downs, refs = refs[4 : 4 + n_x], refs[4 + n_x :]
    weights, outs, acc = refs[:n_w], refs[n_w:-1], refs[-1]
    rows = x_ref.shape[0]
    width = weights[0].shape[1]
    columns = width * n_w
    adapters, rank_columns, _ = up_ref.shape
    down = downs[0][:, :rank_columns]
    for other in downs[1:]:
        down = down + other[:, :rank_columns]
    row = lax.broadcasted_iota(jnp.int32, (rows, rank_columns), 0)
    spread = jnp.concatenate(
        [
            jnp.where((row >= start_ref[a]) & (row < start_ref[a + 1]), down, jnp.zeros_like(down))
            for a in range(adapters)
        ],
        axis=1,
    )
    for c in range(0, columns, step):
        here = slice(c, c + step)
        up = up_ref[:, :, here].reshape(adapters * rank_columns, step)
        inner = c % width
        base = jnp.dot(
            x_ref[...],
            weights[c // width][:, inner : inner + step],
            preferred_element_type=jnp.float32,
        )
        acc[:, here] = base + jnp.dot(spread, up, preferred_element_type=jnp.float32)
    square = square_ref[...]
    high = square.astype(jnp.bfloat16).astype(jnp.float32)
    low = jnp.where(high < jnp.inf, square - high, 0.0)
    lane = lax.broadcasted_iota(jnp.int32, square.shape, 1)
    acc[:, columns:] = jnp.where(lane < LANES // 2, high, low)
    g = lax.axis_index(("gy", "gz"))
    rows_here = outs[0].shape[0]
    for k in range(groups):
        begin = pl.multiple_of(offset(g, k) * rows_here, rows_here)
        outs[k][...] = acc[pl.ds(begin, rows_here), :].astype(outs[k].dtype)


def final_kernel(*refs):
    parts, out_ref = refs[:-1], refs[-1]
    columns = out_ref.shape[1]
    total = parts[0][...]
    for other in parts[1:]:
        total = total + other[...].astype(jnp.float32)
    mean_sq = total[:, columns : columns + 1] + total[:, columns + LANES - 1 :]
    scale = lax.rsqrt(mean_sq + EPSILON)
    value = jnp.where(mean_sq < jnp.inf, total[:, :columns] * scale, 0.0)
    out_ref[...] = value.astype(out_ref.dtype)


def body(
    hidden,
    attention_norm_gain,
    query_weight,
    slot_down_factors,
    adapter_up_factors,
    adapter_of_row,
    padded_adapter_rank,
    adapter_in_slot,
    segment_starts,
):
    n_x, n_y, n_z = lax.axis_size("gx"), lax.axis_size("gy"), lax.axis_size("gz")
    groups = n_y * n_z
    block_rows, depth = hidden.shape
    columns = query_weight.shape[1]
    rows = n_x * block_rows
    rows_here = rows // groups

    def offset(g, k):
        y = lax.rem(g // n_z + k // n_z, n_y)
        z = lax.rem(lax.rem(g, n_z) + k % n_z, n_z)
        return y * n_z + z

    def send_x(value, k):
        return lax.ppermute(value, "gx", [(j, (j + k) % n_x) for j in range(n_x)])

    def send_g(value, k):
        pairs = []
        for g in range(groups):
            y, z = (g // n_z + k // n_z) % n_y, (g % n_z + k % n_z) % n_z
            pairs.append((g, y * n_z + z))
        return lax.ppermute(value, ("gy", "gz"), pairs)

    blocks = [hidden] + [send_x(hidden, k) for k in range(1, n_x)]

    step = min(512, columns // 4)
    n_w, pieces = 4, 4
    f32, bf16 = jnp.float32, jnp.bfloat16
    token, *weights = pl.pallas_call(
        functools.partial(fetch_kernel, n_w),
        out_shape=[jax.ShapeDtypeStruct((8, LANES), f32)]
        + [pltpu.VMEM((depth, columns // n_w), query_weight.dtype)] * n_w,
        in_specs=[ANY],
        out_specs=[VMEM] * (1 + n_w),
        scratch_shapes=[pltpu.SemaphoreType.DMA((n_w, pieces))],
        cost_estimate=cost(0, 2 * query_weight.size),
        compiler_params=params(4),
        name="fetch_weight",
    )(query_weight)

    x, square, down = pl.pallas_call(
        functools.partial(rows_kernel, n_x, depth * groups),
        out_shape=(
            jax.ShapeDtypeStruct((rows, depth), bf16),
            jax.ShapeDtypeStruct((rows, LANES), f32),
            jax.ShapeDtypeStruct((rows, LANES), bf16),
        ),
        in_specs=[SMEM] * 3 + [VMEM] * 2 + [ANY] + [VMEM] * n_x,
        out_specs=(VMEM,) * 3,
        compiler_params=params(4 + (rows * depth >> 16)),
        name="scaled_rows",
    )(
        padded_adapter_rank,
        adapter_in_slot,
        segment_starts,
        attention_norm_gain,
        jnp.swapaxes(slot_down_factors, 1, 2),
        token,
        *blocks,
    )

    downs = [down] + [send_x(down, k) for k in range(1, n_x)]

    dtypes = [f32] + [bf16] * (groups - 1)
    made = pl.pallas_call(
        functools.partial(product_kernel, n_x, n_w, groups, step, offset),
        out_shape=[jax.ShapeDtypeStruct((rows_here, columns + LANES), t) for t in dtypes],
        in_specs=[SMEM] + [VMEM] * (3 + n_x + n_w),
        out_specs=[VMEM] * groups,
        scratch_shapes=[pltpu.VMEM((rows, columns + LANES), f32)],
        cost_estimate=cost(2 * rows * depth * columns, 2 * depth * columns),
        compiler_params=params(4 + (rows * depth >> 16)),
        name="product",
    )(
        segment_starts,
        x,
        square,
        adapter_up_factors,
        *downs,
        *[pltpu.with_memory_space_constraint(w, pltpu.VMEM) for w in weights],
    )
    parts = [made[0]] + [send_g(made[k], k) for k in range(1, groups)]

    return pl.pallas_call(
        final_kernel,
        out_shape=jax.ShapeDtypeStruct((rows_here, columns), bf16),
        in_specs=[VMEM] * groups,
        out_specs=VMEM,
        compiler_params=params(4 + (rows * depth >> 16)),
        name="query_rows",
    )(*parts)


def solution(mesh):
    return jax.shard_map(
        body,
        mesh=mesh,
        in_specs=(
            P(("rep", "gx"), ("gy", "gz")),
            P(("gy", "gz")),
            P(("gy", "gz"), "gx"),
            P("gx", ("gy", "gz"), None),
            P(None, None, "gx"),
            P("rep"),
            P(),
            P(),
            P("rep"),
        ),
        out_specs=P(("rep", "gy", "gz"), "gx"),
        check_vma=False,
    )
```

```python
import functools

import jax
import jax.numpy as jnp
from jax import lax
from jax.experimental import pallas as pl
from jax.experimental.pallas import tpu as pltpu
from jax.sharding import PartitionSpec as P

EPSILON = 1e-05
ADAPTER_ALPHA = 32.0
LANES = 128
MIB = 1 << 20

VMEM = pl.BlockSpec(memory_space=pltpu.VMEM)
SMEM = pl.BlockSpec(memory_space=pltpu.SMEM)
ANY = pl.BlockSpec(memory_space=pl.ANY)


def params(mib):
    return pltpu.CompilerParams(vmem_limit_bytes=mib * MIB)


def cost(flops, moved):
    return pl.CostEstimate(flops=flops, bytes_accessed=moved, transcendentals=0)


def weight_copies(w_hbm, first, w_vmem, sems):
    pieces = sems.shape[0]
    depth, width = w_vmem.shape
    step = depth // pieces
    return [
        pltpu.make_async_copy(
            w_hbm.at[pl.ds(p * step, step), pl.ds(first, width)],
            w_vmem.at[pl.ds(p * step, step)],
            sems.at[p],
        )
        for p in range(pieces)
    ]


def fetch_kernel(n, w_hbm, token_ref, *refs):
    weights, sems = refs[:n], refs[n]
    copies = []
    first = 0
    for j, w_vmem in enumerate(weights):
        copies += weight_copies(w_hbm, first, w_vmem, sems.at[j])
        first += w_vmem.shape[1]
    for copy in copies:
        copy.start()
    token_ref[...] = jnp.zeros(token_ref.shape, token_ref.dtype)
    for copy in copies:
        copy.wait()


def rows_kernel(n, width, *refs):
    rank_ref, slot_ref, start_ref, gain_ref, down_ref, _ = refs[:6]
    blocks = refs[6 : 6 + n]
    x_ref, square_ref, down_out = refs[6 + n :]
    home = lax.axis_index("gx")
    block_rows = blocks[0].shape[0]
    rows = n * block_rows
    gain = gain_ref[...].astype(jnp.float32).reshape(1, gain_ref.shape[0])
    for k in range(n):
        source = lax.rem(home - k + n, n)
        begin = pl.multiple_of(source * block_rows, block_rows)
        values = blocks[k][...].astype(jnp.float32)
        squares = jnp.sum(values * values, axis=1, keepdims=True) / width
        x_ref[pl.ds(begin, block_rows), :] = (values * gain).astype(jnp.bfloat16)
        square_ref[pl.ds(begin, block_rows), :] = jnp.broadcast_to(squares, (block_rows, LANES))
    slots, rank_columns = down_ref.shape[0], down_ref.shape[1]
    row = lax.broadcasted_iota(jnp.int32, (rows, rank_columns), 0)
    col = lax.broadcasted_iota(jnp.int32, (rows, rank_columns), 1)
    total = jnp.zeros((rows, rank_columns), jnp.float32)
    for s in range(slots):
        adapter = slot_ref[home * slots + s]
        rank = rank_ref[adapter]
        live = (row >= start_ref[adapter]) & (row < start_ref[adapter + 1]) & (col < rank)
        projected = lax.dot_general(
            x_ref[...], down_ref[s], (((1,), (1,)), ((), ())), preferred_element_type=jnp.float32
        )
        scale = ADAPTER_ALPHA / jnp.full((rows, rank_columns), rank, jnp.int32).astype(jnp.float32)
        total = total + jnp.where(live, projected * scale, 0.0)
    down_out[...] = jnp.zeros(down_out.shape, down_out.dtype)
    for k in range(n):
        down_out[k, :, :rank_columns] = total.astype(down_out.dtype)


def product_kernel(n_w, step, *refs):
    start_ref, x_ref, square_ref, up_ref, downs = refs[:5]
    weights, out_ref = refs[5 : 5 + n_w], refs[5 + n_w]
    rows = x_ref.shape[0]
    width = weights[0].shape[1]
    columns = width * n_w
    adapters, rank_columns, _ = up_ref.shape
    down = downs[0, :, :rank_columns]
    for k in range(1, downs.shape[0]):
        down = down + downs[k, :, :rank_columns]
    groups, rows_here, _ = out_ref.shape
    row = lax.broadcasted_iota(jnp.int32, (rows, rank_columns), 0)
    spread = jnp.concatenate(
        [
            jnp.where((row >= start_ref[a]) & (row < start_ref[a + 1]), down, jnp.zeros_like(down))
            for a in range(adapters)
        ],
        axis=1,
    )
    for c in range(0, columns, step):
        here = slice(c, c + step)
        up = up_ref[:, :, here].reshape(adapters * rank_columns, step)
        inner = c % width
        base = jnp.dot(
            x_ref[...],
            weights[c // width][:, inner : inner + step],
            preferred_element_type=jnp.float32,
        )
        total = base + jnp.dot(spread, up, preferred_element_type=jnp.float32)
        out_ref[:, :, here] = total.reshape(groups, rows_here, step).astype(out_ref.dtype)
    square = square_ref[...]
    high = square.astype(jnp.bfloat16).astype(jnp.float32)
    low = jnp.where(high < jnp.inf, square - high, 0.0)
    lane = lax.broadcasted_iota(jnp.int32, square.shape, 1)
    both = jnp.where(lane < LANES // 2, high, low)
    out_ref[:, :, columns:] = both.reshape(groups, rows_here, LANES).astype(out_ref.dtype)


def final_kernel(parts, out_ref):
    columns = out_ref.shape[1]
    total = parts[0].astype(jnp.float32)
    for k in range(1, parts.shape[0]):
        total = total + parts[k].astype(jnp.float32)
    mean_sq = total[:, columns : columns + 1] + total[:, columns + LANES - 1 :]
    scale = lax.rsqrt(mean_sq + EPSILON)
    value = jnp.where(mean_sq < jnp.inf, total[:, :columns] * scale, 0.0)
    out_ref[...] = value.astype(out_ref.dtype)


def body(
    hidden,
    attention_norm_gain,
    query_weight,
    slot_down_factors,
    adapter_up_factors,
    adapter_of_row,
    padded_adapter_rank,
    adapter_in_slot,
    segment_starts,
):
    n_x, n_y, n_z = lax.axis_size("gx"), lax.axis_size("gy"), lax.axis_size("gz")
    groups = n_y * n_z
    block_rows, depth = hidden.shape
    columns = query_weight.shape[1]
    rows = n_x * block_rows
    rows_here = rows // groups

    def send_x(value, k):
        return lax.ppermute(value, "gx", [(j, (j + k) % n_x) for j in range(n_x)])

    blocks = [hidden] + [send_x(hidden, k) for k in range(1, n_x)]

    step = min(512, columns // 4)
    n_w, pieces = 4, 4
    f32, bf16 = jnp.float32, jnp.bfloat16
    token, *weights = pl.pallas_call(
        functools.partial(fetch_kernel, n_w),
        out_shape=[jax.ShapeDtypeStruct((8, LANES), f32)]
        + [pltpu.VMEM((depth, columns // n_w), query_weight.dtype)] * n_w,
        in_specs=[ANY],
        out_specs=[VMEM] * (1 + n_w),
        scratch_shapes=[pltpu.SemaphoreType.DMA((n_w, pieces))],
        cost_estimate=cost(0, 2 * query_weight.size),
        compiler_params=params(4),
        name="fetch_weight",
    )(query_weight)

    x, square, down = pl.pallas_call(
        functools.partial(rows_kernel, n_x, depth * groups),
        out_shape=(
            jax.ShapeDtypeStruct((rows, depth), bf16),
            jax.ShapeDtypeStruct((rows, LANES), f32),
            jax.ShapeDtypeStruct((n_x, rows, LANES), bf16),
        ),
        in_specs=[SMEM] * 3 + [VMEM] * 2 + [ANY] + [VMEM] * n_x,
        out_specs=(VMEM,) * 3,
        compiler_params=params(4 + (rows * depth >> 16)),
        name="scaled_rows",
    )(
        padded_adapter_rank,
        adapter_in_slot,
        segment_starts,
        attention_norm_gain,
        jnp.swapaxes(slot_down_factors, 1, 2),
        token,
        *blocks,
    )

    downs = lax.all_to_all(down, "gx", 0, 0)

    made = pl.pallas_call(
        functools.partial(product_kernel, n_w, step),
        out_shape=jax.ShapeDtypeStruct((groups, rows_here, columns + LANES), bf16),
        in_specs=[SMEM] + [VMEM] * (4 + n_w),
        out_specs=VMEM,
        cost_estimate=cost(2 * rows * depth * columns, 2 * depth * columns),
        compiler_params=params(4 + (rows * depth >> 16)),
        name="product",
    )(
        segment_starts,
        x,
        square,
        adapter_up_factors,
        downs,
        *[pltpu.with_memory_space_constraint(w, pltpu.VMEM) for w in weights],
    )
    parts = lax.all_to_all(made, ("gy", "gz"), 0, 0)

    return pl.pallas_call(
        final_kernel,
        out_shape=jax.ShapeDtypeStruct((rows_here, columns), bf16),
        in_specs=[VMEM],
        out_specs=VMEM,
        compiler_params=params(4 + (rows * depth >> 16)),
        name="query_rows",
    )(parts)


def solution(mesh):
    return jax.shard_map(
        body,
        mesh=mesh,
        in_specs=(
            P(("rep", "gx"), ("gy", "gz")),
            P(("gy", "gz")),
            P(("gy", "gz"), "gx"),
            P("gx", ("gy", "gz"), None),
            P(None, None, "gx"),
            P("rep"),
            P(),
            P(),
            P("rep"),
        ),
        out_specs=P(("rep", "gy", "gz"), "gx"),
        check_vma=False,
    )
```

```python
import functools

import jax
import jax.numpy as jnp
from jax import lax
from jax.experimental import pallas as pl
from jax.experimental.pallas import tpu as pltpu
from jax.sharding import PartitionSpec as P

EPSILON = 1e-05
ADAPTER_ALPHA = 32.0
LANES = 128
MIB = 1 << 20

VMEM = pl.BlockSpec(memory_space=pltpu.VMEM)
SMEM = pl.BlockSpec(memory_space=pltpu.SMEM)
ANY = pl.BlockSpec(memory_space=pl.ANY)


def params(mib):
    return pltpu.CompilerParams(vmem_limit_bytes=mib * MIB)


def cost(flops, moved):
    return pl.CostEstimate(flops=flops, bytes_accessed=moved, transcendentals=0)


def weight_copies(w_hbm, first, w_vmem, sems):
    pieces = sems.shape[0]
    depth, width = w_vmem.shape
    step = depth // pieces
    return [
        pltpu.make_async_copy(
            w_hbm.at[pl.ds(p * step, step), pl.ds(first, width)],
            w_vmem.at[pl.ds(p * step, step)],
            sems.at[p],
        )
        for p in range(pieces)
    ]


def fetch_kernel(n, w_hbm, token_ref, *refs):
    weights, sems = refs[:n], refs[n]
    copies = []
    first = 0
    for j, w_vmem in enumerate(weights):
        copies += weight_copies(w_hbm, first, w_vmem, sems.at[j])
        first += w_vmem.shape[1]
    for copy in copies:
        copy.start()
    token_ref[...] = jnp.zeros(token_ref.shape, token_ref.dtype)
    for copy in copies:
        copy.wait()


def rows_kernel(n, width, *refs):
    rank_ref, slot_ref, start_ref, gain_ref, down_ref, _ = refs[:6]
    blocks = refs[6 : 6 + n]
    x_ref, square_ref, down_out = refs[6 + n :]
    home = lax.axis_index("gx")
    block_rows = blocks[0].shape[0]
    rows = n * block_rows
    gain = gain_ref[...].astype(jnp.float32).reshape(1, gain_ref.shape[0])
    for k in range(n):
        source = lax.rem(home - k + n, n)
        begin = pl.multiple_of(source * block_rows, block_rows)
        values = blocks[k][...].astype(jnp.float32)
        squares = jnp.sum(values * values, axis=1, keepdims=True) / width
        x_ref[pl.ds(begin, block_rows), :] = (values * gain).astype(jnp.bfloat16)
        square_ref[pl.ds(begin, block_rows), :] = jnp.broadcast_to(squares, (block_rows, LANES))
    slots, rank_columns = down_ref.shape[0], down_ref.shape[1]
    row = lax.broadcasted_iota(jnp.int32, (rows, rank_columns), 0)
    col = lax.broadcasted_iota(jnp.int32, (rows, rank_columns), 1)
    total = jnp.zeros((rows, rank_columns), jnp.float32)
    for s in range(slots):
        adapter = slot_ref[home * slots + s]
        rank = rank_ref[adapter]
        live = (row >= start_ref[adapter]) & (row < start_ref[adapter + 1]) & (col < rank)
        projected = lax.dot_general(
            x_ref[...], down_ref[s], (((1,), (1,)), ((), ())), preferred_element_type=jnp.float32
        )
        scale = ADAPTER_ALPHA / jnp.full((rows, rank_columns), rank, jnp.int32).astype(jnp.float32)
        total = total + jnp.where(live, projected * scale, 0.0)
    down_out[...] = jnp.zeros(down_out.shape, down_out.dtype)
    down_out[:, :rank_columns] = total.astype(down_out.dtype)


def base_kernel(n_w, step, x_ref, *refs):
    weights, out_ref = refs[:n_w], refs[n_w]
    width = weights[0].shape[1]
    for c in range(0, out_ref.shape[1], step):
        inner = c % width
        out_ref[:, c : c + step] = jnp.dot(
            x_ref[...],
            weights[c // width][:, inner : inner + step],
            preferred_element_type=jnp.float32,
        )


def product_kernel(n_x, n_w, groups, step, offset, *refs):
    start_ref, x_ref, square_ref, up_ref, base_ref = refs[:5]
    downs, refs = refs[5 : 5 + n_x], refs[5 + n_x :]
    weights, outs, acc = refs[:n_w], refs[n_w:-1], refs[-1]
    rows = x_ref.shape[0]
    width = weights[0].shape[1]
    done = base_ref.shape[1]
    columns = done + width * n_w
    adapters, rank_columns, _ = up_ref.shape
    down = downs[0][:, :rank_columns]
    for other in downs[1:]:
        down = down + other[:, :rank_columns]
    row = lax.broadcasted_iota(jnp.int32, (rows, rank_columns), 0)
    spread = jnp.concatenate(
        [
            jnp.where((row >= start_ref[a]) & (row < start_ref[a + 1]), down, jnp.zeros_like(down))
            for a in range(adapters)
        ],
        axis=1,
    )
    for c in range(0, columns, step):
        here = slice(c, c + step)
        up = up_ref[:, :, here].reshape(adapters * rank_columns, step)
        if c < done:
            base = base_ref[:, here]
        else:
            inner = (c - done) % width
            base = jnp.dot(
                x_ref[...],
                weights[(c - done) // width][:, inner : inner + step],
                preferred_element_type=jnp.float32,
            )
        acc[:, here] = base + jnp.dot(spread, up, preferred_element_type=jnp.float32)
    square = square_ref[...]
    high = square.astype(jnp.bfloat16).astype(jnp.float32)
    low = jnp.where(high < jnp.inf, square - high, 0.0)
    lane = lax.broadcasted_iota(jnp.int32, square.shape, 1)
    acc[:, columns:] = jnp.where(lane < LANES // 2, high, low)
    g = lax.axis_index(("gy", "gz"))
    rows_here = outs[0].shape[0]
    for k in range(groups):
        begin = pl.multiple_of(offset(g, k) * rows_here, rows_here)
        outs[k][...] = acc[pl.ds(begin, rows_here), :].astype(outs[k].dtype)


def final_kernel(*refs):
    parts, out_ref = refs[:-1], refs[-1]
    columns = out_ref.shape[1]
    total = parts[0][...]
    for other in parts[1:]:
        total = total + other[...].astype(jnp.float32)
    mean_sq = total[:, columns : columns + 1] + total[:, columns + LANES - 1 :]
    scale = lax.rsqrt(mean_sq + EPSILON)
    value = jnp.where(mean_sq < jnp.inf, total[:, :columns] * scale, 0.0)
    out_ref[...] = value.astype(out_ref.dtype)


def body(
    hidden,
    attention_norm_gain,
    query_weight,
    slot_down_factors,
    adapter_up_factors,
    adapter_of_row,
    padded_adapter_rank,
    adapter_in_slot,
    segment_starts,
):
    n_x, n_y, n_z = lax.axis_size("gx"), lax.axis_size("gy"), lax.axis_size("gz")
    groups = n_y * n_z
    block_rows, depth = hidden.shape
    columns = query_weight.shape[1]
    rows = n_x * block_rows
    rows_here = rows // groups

    def offset(g, k):
        y = lax.rem(g // n_z + k // n_z, n_y)
        z = lax.rem(lax.rem(g, n_z) + k % n_z, n_z)
        return y * n_z + z

    def send_x(value, k):
        return lax.ppermute(value, "gx", [(j, (j + k) % n_x) for j in range(n_x)])

    def send_g(value, k):
        pairs = []
        for g in range(groups):
            y, z = (g // n_z + k // n_z) % n_y, (g % n_z + k % n_z) % n_z
            pairs.append((g, y * n_z + z))
        return lax.ppermute(value, ("gy", "gz"), pairs)

    blocks = [hidden] + [send_x(hidden, k) for k in range(1, n_x)]

    step = min(512, columns // 4)
    n_w, pieces = 4, 4
    f32, bf16 = jnp.float32, jnp.bfloat16
    token, *weights = pl.pallas_call(
        functools.partial(fetch_kernel, n_w),
        out_shape=[jax.ShapeDtypeStruct((8, LANES), f32)]
        + [pltpu.VMEM((depth, columns // n_w), query_weight.dtype)] * n_w,
        in_specs=[ANY],
        out_specs=[VMEM] * (1 + n_w),
        scratch_shapes=[pltpu.SemaphoreType.DMA((n_w, pieces))],
        cost_estimate=cost(0, 2 * query_weight.size),
        compiler_params=params(4),
        name="fetch_weight",
    )(query_weight)

    x, square, down = pl.pallas_call(
        functools.partial(rows_kernel, n_x, depth * groups),
        out_shape=(
            jax.ShapeDtypeStruct((rows, depth), bf16),
            jax.ShapeDtypeStruct((rows, LANES), f32),
            jax.ShapeDtypeStruct((rows, LANES), bf16),
        ),
        in_specs=[SMEM] * 3 + [VMEM] * 2 + [ANY] + [VMEM] * n_x,
        out_specs=(VMEM,) * 3,
        compiler_params=params(4 + (rows * depth >> 16)),
        name="scaled_rows",
    )(
        padded_adapter_rank,
        adapter_in_slot,
        segment_starts,
        attention_norm_gain,
        jnp.swapaxes(slot_down_factors, 1, 2),
        token,
        *blocks,
    )

    downs = [down] + [send_x(down, k) for k in range(1, n_x)]

    weights = [pltpu.with_memory_space_constraint(w, pltpu.VMEM) for w in weights]
    early = n_w // 2
    base_columns = early * (columns // n_w)
    base = pl.pallas_call(
        functools.partial(base_kernel, early, step),
        out_shape=jax.ShapeDtypeStruct((rows, base_columns), f32),
        in_specs=[VMEM] * (1 + early),
        out_specs=VMEM,
        cost_estimate=cost(2 * rows * depth * base_columns, 2 * depth * base_columns),
        compiler_params=params(4 + (rows * depth >> 16)),
        name="first_columns",
    )(x, *weights[:early])

    late = n_w - early
    late_columns = columns - base_columns
    dtypes = [f32] + [bf16] * (groups - 1)
    made = pl.pallas_call(
        functools.partial(product_kernel, n_x, late, groups, step, offset),
        out_shape=[jax.ShapeDtypeStruct((rows_here, columns + LANES), t) for t in dtypes],
        in_specs=[SMEM] + [VMEM] * (4 + n_x + late),
        out_specs=[VMEM] * groups,
        scratch_shapes=[pltpu.VMEM((rows, columns + LANES), f32)],
        cost_estimate=cost(2 * rows * depth * late_columns, 2 * depth * late_columns),
        compiler_params=params(4 + (rows * depth >> 16)),
        name="last_columns",
    )(segment_starts, x, square, adapter_up_factors, base, *downs, *weights[early:])
    parts = [made[0]] + [send_g(made[k], k) for k in range(groups - 1, 0, -1)]

    return pl.pallas_call(
        final_kernel,
        out_shape=jax.ShapeDtypeStruct((rows_here, columns), bf16),
        in_specs=[VMEM] * groups,
        out_specs=VMEM,
        compiler_params=params(4 + (rows * depth >> 16)),
        name="query_rows",
    )(*parts)


def solution(mesh):
    return jax.shard_map(
        body,
        mesh=mesh,
        in_specs=(
            P(("rep", "gx"), ("gy", "gz")),
            P(("gy", "gz")),
            P(("gy", "gz"), "gx"),
            P("gx", ("gy", "gz"), None),
            P(None, None, "gx"),
            P("rep"),
            P(),
            P(),
            P("rep"),
        ),
        out_specs=P(("rep", "gy", "gz"), "gx"),
        check_vma=False,
    )
```

```python
import functools

import jax
import jax.numpy as jnp
from jax import lax
from jax.experimental import pallas as pl
from jax.experimental.pallas import tpu as pltpu
from jax.sharding import PartitionSpec as P

EPSILON = 1e-05
ADAPTER_ALPHA = 32.0
LANES = 128
MIB = 1 << 20

VMEM = pl.BlockSpec(memory_space=pltpu.VMEM)
SMEM = pl.BlockSpec(memory_space=pltpu.SMEM)
ANY = pl.BlockSpec(memory_space=pl.ANY)


def params(mib):
    return pltpu.CompilerParams(vmem_limit_bytes=mib * MIB)


def cost(flops, moved):
    return pl.CostEstimate(flops=flops, bytes_accessed=moved, transcendentals=0)


def weight_copies(w_hbm, first, w_vmem, sems):
    pieces = sems.shape[0]
    depth, width = w_vmem.shape
    step = depth // pieces
    return [
        pltpu.make_async_copy(
            w_hbm.at[pl.ds(p * step, step), pl.ds(first, width)],
            w_vmem.at[pl.ds(p * step, step)],
            sems.at[p],
        )
        for p in range(pieces)
    ]


def fetch_kernel(n, w_hbm, token_ref, *refs):
    weights, sems = refs[:n], refs[n]
    copies = []
    first = 0
    for j, w_vmem in enumerate(weights):
        copies += weight_copies(w_hbm, first, w_vmem, sems.at[j])
        first += w_vmem.shape[1]
    for copy in copies:
        copy.start()
    token_ref[...] = jnp.zeros(token_ref.shape, token_ref.dtype)
    for copy in copies:
        copy.wait()


def rows_kernel(n, width, *refs):
    rank_ref, slot_ref, start_ref, gain_ref, down_ref, _ = refs[:6]
    blocks = refs[6 : 6 + n]
    x_ref, square_ref, down_out = refs[6 + n :]
    home = lax.axis_index("gx")
    block_rows = blocks[0].shape[0]
    rows = n * block_rows
    gain = gain_ref[...].astype(jnp.float32).reshape(1, gain_ref.shape[0])
    for k in range(n):
        source = lax.rem(home - k + n, n)
        begin = pl.multiple_of(source * block_rows, block_rows)
        values = blocks[k][...].astype(jnp.float32)
        squares = jnp.sum(values * values, axis=1, keepdims=True) / width
        x_ref[pl.ds(begin, block_rows), :] = (values * gain).astype(jnp.bfloat16)
        square_ref[pl.ds(begin, block_rows), :] = jnp.broadcast_to(squares, (block_rows, LANES))
    slots, rank_columns = down_ref.shape[0], down_ref.shape[1]
    row = lax.broadcasted_iota(jnp.int32, (rows, rank_columns), 0)
    col = lax.broadcasted_iota(jnp.int32, (rows, rank_columns), 1)
    total = jnp.zeros((rows, rank_columns), jnp.float32)
    for s in range(slots):
        adapter = slot_ref[home * slots + s]
        rank = rank_ref[adapter]
        live = (row >= start_ref[adapter]) & (row < start_ref[adapter + 1]) & (col < rank)
        projected = lax.dot_general(
            x_ref[...], down_ref[s], (((1,), (1,)), ((), ())), preferred_element_type=jnp.float32
        )
        scale = ADAPTER_ALPHA / jnp.full((rows, rank_columns), rank, jnp.int32).astype(jnp.float32)
        total = total + jnp.where(live, projected * scale, 0.0)
    down_out[...] = jnp.zeros(down_out.shape, down_out.dtype)
    down_out[:, :rank_columns] = total.astype(down_out.dtype)


def base_kernel(n_w, step, x_ref, *refs):
    weights, out_ref = refs[:n_w], refs[n_w]
    width = weights[0].shape[1]
    for c in range(0, out_ref.shape[1], step):
        inner = c % width
        out_ref[:, c : c + step] = jnp.dot(
            x_ref[...],
            weights[c // width][:, inner : inner + step],
            preferred_element_type=jnp.float32,
        )


def product_kernel(n_x, n_w, groups, step, offset, *refs):
    start_ref, x_ref, square_ref, up_ref, base_ref = refs[:5]
    downs, refs = refs[5 : 5 + n_x], refs[5 + n_x :]
    weights, outs, acc = refs[:n_w], refs[n_w:-1], refs[-1]
    rows = x_ref.shape[0]
    width = weights[0].shape[1]
    done = base_ref.shape[1]
    columns = done + width * n_w
    adapters, rank_columns, _ = up_ref.shape
    down = downs[0][:, :rank_columns]
    for other in downs[1:]:
        down = down + other[:, :rank_columns]
    row = lax.broadcasted_iota(jnp.int32, (rows, rank_columns), 0)
    spread = jnp.concatenate(
        [
            jnp.where((row >= start_ref[a]) & (row < start_ref[a + 1]), down, jnp.zeros_like(down))
            for a in range(adapters)
        ],
        axis=1,
    )
    for c in range(0, columns, step):
        here = slice(c, c + step)
        up = up_ref[:, :, here].reshape(adapters * rank_columns, step)
        if c < done:
            base = base_ref[:, here]
        else:
            inner = (c - done) % width
            base = jnp.dot(
                x_ref[...],
                weights[(c - done) // width][:, inner : inner + step],
                preferred_element_type=jnp.float32,
            )
        acc[:, here] = base + jnp.dot(spread, up, preferred_element_type=jnp.float32)
    square = square_ref[...]
    high = square.astype(jnp.bfloat16).astype(jnp.float32)
    low = jnp.where(high < jnp.inf, square - high, 0.0)
    lane = lax.broadcasted_iota(jnp.int32, square.shape, 1)
    acc[:, columns:] = jnp.where(lane < LANES // 2, high, low)
    g = lax.axis_index(("gy", "gz"))
    rows_here = outs[0].shape[0]
    for k in range(groups):
        begin = pl.multiple_of(offset(g, k) * rows_here, rows_here)
        outs[k][...] = acc[pl.ds(begin, rows_here), :].astype(outs[k].dtype)


def final_kernel(*refs):
    parts, out_ref = refs[:-1], refs[-1]
    columns = out_ref.shape[1]
    total = parts[0][...]
    for other in parts[1:]:
        total = total + other[...].astype(jnp.float32)
    mean_sq = total[:, columns : columns + 1] + total[:, columns + LANES - 1 :]
    scale = lax.rsqrt(mean_sq + EPSILON)
    value = jnp.where(mean_sq < jnp.inf, total[:, :columns] * scale, 0.0)
    out_ref[...] = value.astype(out_ref.dtype)


def body(
    hidden,
    attention_norm_gain,
    query_weight,
    slot_down_factors,
    adapter_up_factors,
    adapter_of_row,
    padded_adapter_rank,
    adapter_in_slot,
    segment_starts,
):
    n_x, n_y, n_z = lax.axis_size("gx"), lax.axis_size("gy"), lax.axis_size("gz")
    groups = n_y * n_z
    block_rows, depth = hidden.shape
    columns = query_weight.shape[1]
    rows = n_x * block_rows
    rows_here = rows // groups

    def offset(g, k):
        y = lax.rem(g // n_z + k // n_z, n_y)
        z = lax.rem(lax.rem(g, n_z) + k % n_z, n_z)
        return y * n_z + z

    def send_x(value, k):
        return lax.ppermute(value, "gx", [(j, (j + k) % n_x) for j in range(n_x)])

    def send_g(value, k):
        pairs = []
        for g in range(groups):
            y, z = (g // n_z + k // n_z) % n_y, (g % n_z + k % n_z) % n_z
            pairs.append((g, y * n_z + z))
        return lax.ppermute(value, ("gy", "gz"), pairs)

    blocks = [hidden] + [send_x(hidden, k) for k in range(1, n_x)]

    step = min(512, columns // 4)
    n_w, pieces = 4, 4
    f32, bf16 = jnp.float32, jnp.bfloat16
    token, *weights = pl.pallas_call(
        functools.partial(fetch_kernel, n_w - 1),
        out_shape=[jax.ShapeDtypeStruct((8, LANES), f32)]
        + [pltpu.VMEM((depth, columns // n_w), query_weight.dtype)] * (n_w - 1),
        in_specs=[ANY],
        out_specs=[VMEM] * n_w,
        scratch_shapes=[pltpu.SemaphoreType.DMA((n_w - 1, pieces))],
        cost_estimate=cost(0, 2 * query_weight.size),
        compiler_params=params(4),
        name="fetch_weight",
    )(query_weight)

    x, square, down = pl.pallas_call(
        functools.partial(rows_kernel, n_x, depth * groups),
        out_shape=(
            jax.ShapeDtypeStruct((rows, depth), bf16),
            jax.ShapeDtypeStruct((rows, LANES), f32),
            jax.ShapeDtypeStruct((rows, LANES), bf16),
        ),
        in_specs=[SMEM] * 3 + [VMEM] * 2 + [ANY] + [VMEM] * n_x,
        out_specs=(VMEM,) * 3,
        compiler_params=params(4 + (rows * depth >> 16)),
        name="scaled_rows",
    )(
        padded_adapter_rank,
        adapter_in_slot,
        segment_starts,
        attention_norm_gain,
        jnp.swapaxes(slot_down_factors, 1, 2),
        token,
        *blocks,
    )

    downs = [down] + [send_x(down, k) for k in range(1, n_x)]

    weights.append(query_weight[:, columns - columns // n_w :])
    weights = [pltpu.with_memory_space_constraint(w, pltpu.VMEM) for w in weights]
    early = n_w // 2
    base_columns = early * (columns // n_w)
    base = pl.pallas_call(
        functools.partial(base_kernel, early, step),
        out_shape=jax.ShapeDtypeStruct((rows, base_columns), f32),
        in_specs=[VMEM] * (1 + early),
        out_specs=VMEM,
        cost_estimate=cost(2 * rows * depth * base_columns, 2 * depth * base_columns),
        compiler_params=params(4 + (rows * depth >> 16)),
        name="first_columns",
    )(x, *weights[:early])

    late = n_w - early
    late_columns = columns - base_columns
    dtypes = [f32] + [bf16] * (groups - 1)
    made = pl.pallas_call(
        functools.partial(product_kernel, n_x, late, groups, step, offset),
        out_shape=[jax.ShapeDtypeStruct((rows_here, columns + LANES), t) for t in dtypes],
        in_specs=[SMEM] + [VMEM] * (4 + n_x + late),
        out_specs=[VMEM] * groups,
        scratch_shapes=[pltpu.VMEM((rows, columns + LANES), f32)],
        cost_estimate=cost(2 * rows * depth * late_columns, 2 * depth * late_columns),
        compiler_params=params(4 + (rows * depth >> 16)),
        name="last_columns",
    )(segment_starts, x, square, adapter_up_factors, base, *downs, *weights[early:])
    parts = [made[0]] + [send_g(made[k], k) for k in range(groups - 1, 0, -1)]

    return pl.pallas_call(
        final_kernel,
        out_shape=jax.ShapeDtypeStruct((rows_here, columns), bf16),
        in_specs=[VMEM] * groups,
        out_specs=VMEM,
        compiler_params=params(4 + (rows * depth >> 16)),
        name="query_rows",
    )(*parts)


def solution(mesh):
    return jax.shard_map(
        body,
        mesh=mesh,
        in_specs=(
            P(("rep", "gx"), ("gy", "gz")),
            P(("gy", "gz")),
            P(("gy", "gz"), "gx"),
            P("gx", ("gy", "gz"), None),
            P(None, None, "gx"),
            P("rep"),
            P(),
            P(),
            P("rep"),
        ),
        out_specs=P(("rep", "gy", "gz"), "gx"),
        check_vma=False,
    )
```

```python
import functools

import jax
import jax.numpy as jnp
from jax import lax
from jax.experimental import pallas as pl
from jax.experimental.pallas import tpu as pltpu
from jax.sharding import PartitionSpec as P

EPSILON = 1e-05
ADAPTER_ALPHA = 32.0
LANES = 128
MIB = 1 << 20

VMEM = pl.BlockSpec(memory_space=pltpu.VMEM)
SMEM = pl.BlockSpec(memory_space=pltpu.SMEM)
ANY = pl.BlockSpec(memory_space=pl.ANY)


def params(mib):
    return pltpu.CompilerParams(vmem_limit_bytes=mib * MIB)


def cost(flops, moved):
    return pl.CostEstimate(flops=flops, bytes_accessed=moved, transcendentals=0)


def weight_copies(w_hbm, first, w_vmem, sems):
    pieces = sems.shape[0]
    depth, width = w_vmem.shape
    step = depth // pieces
    return [
        pltpu.make_async_copy(
            w_hbm.at[pl.ds(p * step, step), pl.ds(first, width)],
            w_vmem.at[pl.ds(p * step, step)],
            sems.at[p],
        )
        for p in range(pieces)
    ]


def fetch_kernel(n, w_hbm, token_ref, *refs):
    weights, sems = refs[:n], refs[n]
    copies = []
    first = 0
    for j, w_vmem in enumerate(weights):
        copies += weight_copies(w_hbm, first, w_vmem, sems.at[j])
        first += w_vmem.shape[1]
    for copy in copies:
        copy.start()
    token_ref[...] = jnp.zeros(token_ref.shape, token_ref.dtype)
    for copy in copies:
        copy.wait()


def rows_kernel(n, width, *refs):
    rank_ref, slot_ref, start_ref, gain_ref, down_ref, _ = refs[:6]
    blocks = refs[6 : 6 + n]
    x_ref, square_ref, down_out = refs[6 + n :]
    home = lax.axis_index("gx")
    block_rows = blocks[0].shape[0]
    rows = n * block_rows
    gain = gain_ref[...].astype(jnp.float32).reshape(1, gain_ref.shape[0])
    for k in range(n):
        source = lax.rem(home - k + n, n)
        begin = pl.multiple_of(source * block_rows, block_rows)
        values = blocks[k][...].astype(jnp.float32)
        squares = jnp.sum(values * values, axis=1, keepdims=True) / width
        x_ref[pl.ds(begin, block_rows), :] = (values * gain).astype(jnp.bfloat16)
        square_ref[pl.ds(begin, block_rows), :] = jnp.broadcast_to(squares, (block_rows, LANES))
    slots, rank_columns = down_ref.shape[0], down_ref.shape[1]
    row = lax.broadcasted_iota(jnp.int32, (rows, rank_columns), 0)
    col = lax.broadcasted_iota(jnp.int32, (rows, rank_columns), 1)
    total = jnp.zeros((rows, rank_columns), jnp.float32)
    for s in range(slots):
        adapter = slot_ref[home * slots + s]
        rank = rank_ref[adapter]
        live = (row >= start_ref[adapter]) & (row < start_ref[adapter + 1]) & (col < rank)
        projected = lax.dot_general(
            x_ref[...], down_ref[s], (((1,), (1,)), ((), ())), preferred_element_type=jnp.float32
        )
        scale = ADAPTER_ALPHA / jnp.full((rows, rank_columns), rank, jnp.int32).astype(jnp.float32)
        total = total + jnp.where(live, projected * scale, 0.0)
    down_out[...] = jnp.zeros(down_out.shape, down_out.dtype)
    down_out[:, :rank_columns] = total.astype(down_out.dtype)


def split_wide(value):
    high = value.astype(jnp.bfloat16).astype(jnp.float32)
    low = jnp.where(high < jnp.inf, value - high, 0.0)
    lane = lax.broadcasted_iota(jnp.int32, value.shape, 1)
    return jnp.where(lane < LANES // 2, high, low)


def join_wide(value):
    return value[:, :1] + value[:, LANES - 1 :]


def write_rows(acc, outs, n_y, n_z):
    z = lax.axis_index("gz")
    rows_here = outs[0].shape[0] // n_y
    for k in range(n_z):
        for y in range(n_y):
            owner = y * n_z + lax.rem(z + k, n_z)
            begin = pl.multiple_of(owner * rows_here, rows_here)
            outs[k][y * rows_here : (y + 1) * rows_here, :] = acc[
                pl.ds(begin, rows_here), :
            ].astype(outs[k].dtype)


def multiply(x_ref, weights, step, acc):
    width = weights[0].shape[1]
    for c in range(0, width * len(weights), step):
        inner = c % width
        acc[:, c : c + step] = jnp.dot(
            x_ref[...],
            weights[c // width][:, inner : inner + step],
            preferred_element_type=jnp.float32,
        )


def first_kernel(n_w, n_y, n_z, step, x_ref, *refs):
    weights, outs, acc = refs[:n_w], refs[n_w:-1], refs[-1]
    multiply(x_ref, weights, step, acc)
    write_rows(acc, outs, n_y, n_z)


def last_kernel(n_w, n_x, n_y, n_z, step, x_ref, square_ref, *refs):
    downs, refs = refs[:n_x], refs[n_x:]
    weights, outs, acc = refs[:n_w], refs[n_w:-1], refs[-1]
    multiply(x_ref, weights, step, acc)
    columns = weights[0].shape[1] * n_w
    down = downs[0][...].astype(jnp.float32)
    for other in downs[1:]:
        down = down + other[...].astype(jnp.float32)
    acc[:, columns : columns + LANES] = down
    acc[:, columns + LANES :] = split_wide(square_ref[...])
    write_rows(acc, outs, n_y, n_z)


def pair_kernel(n_y, n_z, step, start_ref, up_ref, *refs):
    firsts, lasts = refs[:n_z], refs[n_z : 2 * n_z]
    outs, acc = refs[2 * n_z : -1], refs[-1]
    rows, done = firsts[0].shape
    rows_here = rows // n_y
    columns = done + lasts[0].shape[1] - 2 * LANES
    adapters, rank_columns, _ = up_ref.shape
    z = lax.axis_index("gz")

    def added(parts, here):
        total = parts[0][:, here]
        for part in parts[1:]:
            total = total + part[:, here].astype(jnp.float32)
        return total

    late = columns - done
    square = join_wide(lasts[0][:, late + LANES :])
    for part in lasts[1:]:
        square = square + join_wide(part[:, late + LANES :].astype(jnp.float32))
    down = added(lasts, slice(late, late + rank_columns)).astype(jnp.bfloat16)
    row = lax.broadcasted_iota(jnp.int32, (rows, rank_columns), 0)
    row = (row // rows_here * n_z + z) * rows_here + lax.rem(row, rows_here)
    spread = jnp.concatenate(
        [
            jnp.where((row >= start_ref[a]) & (row < start_ref[a + 1]), down, jnp.zeros_like(down))
            for a in range(adapters)
        ],
        axis=1,
    )
    for c in range(0, columns, step):
        if c < done:
            base = added(firsts, slice(c, c + step))
        else:
            base = added(lasts, slice(c - done, c - done + step))
        up = up_ref[:, :, c : c + step].reshape(adapters * rank_columns, step)
        acc[:, c : c + step] = base + jnp.dot(spread, up, preferred_element_type=jnp.float32)
    acc[:, columns:] = split_wide(jnp.broadcast_to(square, (rows, LANES)))
    y = lax.axis_index("gy")
    for k in range(n_y):
        begin = pl.multiple_of(lax.rem(y + k, n_y) * rows_here, rows_here)
        outs[k][...] = acc[pl.ds(begin, rows_here), :].astype(outs[k].dtype)


def final_kernel(*refs):
    parts, out_ref = refs[:-1], refs[-1]
    columns = out_ref.shape[1]
    total = parts[0][...]
    for other in parts[1:]:
        total = total + other[...].astype(jnp.float32)
    mean_sq = join_wide(total[:, columns:])
    scale = lax.rsqrt(mean_sq + EPSILON)
    value = jnp.where(mean_sq < jnp.inf, total[:, :columns] * scale, 0.0)
    out_ref[...] = value.astype(out_ref.dtype)


def body(
    hidden,
    attention_norm_gain,
    query_weight,
    slot_down_factors,
    adapter_up_factors,
    adapter_of_row,
    padded_adapter_rank,
    adapter_in_slot,
    segment_starts,
):
    n_x, n_y, n_z = lax.axis_size("gx"), lax.axis_size("gy"), lax.axis_size("gz")
    groups = n_y * n_z
    block_rows, depth = hidden.shape
    columns = query_weight.shape[1]
    rows = n_x * block_rows
    rows_here = rows // groups

    def send(value, axis, n, k):
        return lax.ppermute(value, axis, [(j, (j + k) % n) for j in range(n)])

    def spread_out(made, axis, n):
        return [made[0]] + [send(made[k], axis, n, k) for k in range(1, n)]

    blocks = [hidden] + [send(hidden, "gx", n_x, k) for k in range(1, n_x)]

    step = min(512, columns // 4)
    n_w, pieces = 4, 4
    f32, bf16 = jnp.float32, jnp.bfloat16
    token, *weights = pl.pallas_call(
        functools.partial(fetch_kernel, n_w),
        out_shape=[jax.ShapeDtypeStruct((8, LANES), f32)]
        + [pltpu.VMEM((depth, columns // n_w), query_weight.dtype)] * n_w,
        in_specs=[ANY],
        out_specs=[VMEM] * (1 + n_w),
        scratch_shapes=[pltpu.SemaphoreType.DMA((n_w, pieces))],
        cost_estimate=cost(0, 2 * query_weight.size),
        compiler_params=params(4),
        name="fetch_weight",
    )(query_weight)

    x, square, down = pl.pallas_call(
        functools.partial(rows_kernel, n_x, depth * groups),
        out_shape=(
            jax.ShapeDtypeStruct((rows, depth), bf16),
            jax.ShapeDtypeStruct((rows, LANES), f32),
            jax.ShapeDtypeStruct((rows, LANES), bf16),
        ),
        in_specs=[SMEM] * 3 + [VMEM] * 2 + [ANY] + [VMEM] * n_x,
        out_specs=(VMEM,) * 3,
        compiler_params=params(4 + (rows * depth >> 16)),
        name="scaled_rows",
    )(
        padded_adapter_rank,
        adapter_in_slot,
        segment_starts,
        attention_norm_gain,
        jnp.swapaxes(slot_down_factors, 1, 2),
        token,
        *blocks,
    )

    downs = [down] + [send(down, "gx", n_x, k) for k in range(1, n_x)]

    weights = [pltpu.with_memory_space_constraint(w, pltpu.VMEM) for w in weights]
    early, late = n_w - 1, 1
    early_columns, late_columns = (n * (columns // n_w) for n in (early, late))
    kept = n_y * rows_here

    def shapes(n, shape):
        return [jax.ShapeDtypeStruct(shape, f32 if k == 0 else bf16) for k in range(n)]

    made = pl.pallas_call(
        functools.partial(first_kernel, early, n_y, n_z, step),
        out_shape=shapes(n_z, (kept, early_columns)),
        in_specs=[VMEM] * (1 + early),
        out_specs=[VMEM] * n_z,
        scratch_shapes=[pltpu.VMEM((rows, early_columns), f32)],
        cost_estimate=cost(2 * rows * depth * early_columns, 2 * depth * early_columns),
        compiler_params=params(4 + (rows * depth >> 16)),
        name="first_columns",
    )(x, *weights[:early])
    firsts = spread_out(made, "gz", n_z)

    made = pl.pallas_call(
        functools.partial(last_kernel, late, n_x, n_y, n_z, step),
        out_shape=shapes(n_z, (kept, late_columns + 2 * LANES)),
        in_specs=[VMEM] * (2 + n_x + late),
        out_specs=[VMEM] * n_z,
        scratch_shapes=[pltpu.VMEM((rows, late_columns + 2 * LANES), f32)],
        cost_estimate=cost(2 * rows * depth * columns, 4 * depth * columns),
        compiler_params=params(4 + (rows * depth >> 16)),
        name="last_columns",
    )(x, square, *downs, *weights[early:])
    lasts = spread_out(made, "gz", n_z)

    made = pl.pallas_call(
        functools.partial(pair_kernel, n_y, n_z, step),
        out_shape=shapes(n_y, (rows_here, columns + LANES)),
        in_specs=[SMEM] + [VMEM] * (1 + 2 * n_z),
        out_specs=[VMEM] * n_y,
        scratch_shapes=[pltpu.VMEM((kept, columns + LANES), f32)],
        compiler_params=params(4 + (rows * depth >> 16)),
        name="chip_sums",
    )(segment_starts, adapter_up_factors, *firsts, *lasts)
    parts = spread_out(made, "gy", n_y)

    return pl.pallas_call(
        final_kernel,
        out_shape=jax.ShapeDtypeStruct((rows_here, columns), bf16),
        in_specs=[VMEM] * n_y,
        out_specs=VMEM,
        compiler_params=params(4 + (rows * depth >> 16)),
        name="query_rows",
    )(*parts)


def solution(mesh):
    return jax.shard_map(
        body,
        mesh=mesh,
        in_specs=(
            P(("rep", "gx"), ("gy", "gz")),
            P(("gy", "gz")),
            P(("gy", "gz"), "gx"),
            P("gx", ("gy", "gz"), None),
            P(None, None, "gx"),
            P("rep"),
            P(),
            P(),
            P("rep"),
        ),
        out_specs=P(("rep", "gy", "gz"), "gx"),
        check_vma=False,
    )
```

```python
import functools

import jax
import jax.numpy as jnp
from jax import lax
from jax.experimental import pallas as pl
from jax.experimental.pallas import tpu as pltpu
from jax.sharding import PartitionSpec as P

EPSILON = 1e-05
ADAPTER_ALPHA = 32.0
LANES = 128
MIB = 1 << 20

VMEM = pl.BlockSpec(memory_space=pltpu.VMEM)
SMEM = pl.BlockSpec(memory_space=pltpu.SMEM)
ANY = pl.BlockSpec(memory_space=pl.ANY)


def params(mib):
    return pltpu.CompilerParams(vmem_limit_bytes=mib * MIB)


def cost(flops, moved):
    return pl.CostEstimate(flops=flops, bytes_accessed=moved, transcendentals=0)


def weight_copies(w_hbm, first, w_vmem, sems):
    pieces = sems.shape[0]
    depth, width = w_vmem.shape
    step = depth // pieces
    return [
        pltpu.make_async_copy(
            w_hbm.at[pl.ds(p * step, step), pl.ds(first, width)],
            w_vmem.at[pl.ds(p * step, step)],
            sems.at[p],
        )
        for p in range(pieces)
    ]


def fetch_kernel(n, w_hbm, token_ref, *refs):
    weights, sems = refs[:n], refs[n]
    copies = []
    first = 0
    for j, w_vmem in enumerate(weights):
        copies += weight_copies(w_hbm, first, w_vmem, sems.at[j])
        first += w_vmem.shape[1]
    for copy in copies:
        copy.start()
    token_ref[...] = jnp.zeros(token_ref.shape, token_ref.dtype)
    for copy in copies:
        copy.wait()


def split_wide(value):
    high = value.astype(jnp.bfloat16).astype(jnp.float32)
    low = jnp.where(high < jnp.inf, value - high, 0.0)
    lane = lax.broadcasted_iota(jnp.int32, value.shape, 1)
    return jnp.where(lane < LANES // 2, high, low)


def join_wide(value):
    return value[:, :1] + value[:, LANES - 1 :]


def rows_kernel(n, width, *refs):
    rank_ref, slot_ref, start_ref, gain_ref, down_ref, _ = refs[:6]
    blocks = refs[6 : 6 + n]
    x_ref, small_ref = refs[6 + n :]
    home = lax.axis_index("gx")
    block_rows = blocks[0].shape[0]
    rows = n * block_rows
    gain = gain_ref[...].astype(jnp.float32).reshape(1, gain_ref.shape[0])
    small_ref[...] = jnp.zeros(small_ref.shape, small_ref.dtype)
    for k in range(n):
        begin = pl.multiple_of(jnp.bitwise_xor(home, k) * block_rows, block_rows)
        values = blocks[k][...].astype(jnp.float32)
        x_ref[pl.ds(begin, block_rows), :] = (values * gain).astype(jnp.bfloat16)
        if k == 0:
            squares = jnp.sum(values * values, axis=1, keepdims=True) / width
            squares = split_wide(jnp.broadcast_to(squares, (block_rows, LANES)))
            small_ref[pl.ds(begin, block_rows), LANES:] = squares.astype(jnp.bfloat16)
    slots, rank_columns = down_ref.shape[0], down_ref.shape[1]
    row = lax.broadcasted_iota(jnp.int32, (rows, rank_columns), 0)
    col = lax.broadcasted_iota(jnp.int32, (rows, rank_columns), 1)
    total = jnp.zeros((rows, rank_columns), jnp.float32)
    for s in range(slots):
        adapter = slot_ref[home * slots + s]
        rank = rank_ref[adapter]
        live = (row >= start_ref[adapter]) & (row < start_ref[adapter + 1]) & (col < rank)
        projected = lax.dot_general(
            x_ref[...], down_ref[s], (((1,), (1,)), ((), ())), preferred_element_type=jnp.float32
        )
        scale = ADAPTER_ALPHA / jnp.full((rows, rank_columns), rank, jnp.int32).astype(jnp.float32)
        total = total + jnp.where(live, projected * scale, 0.0)
    small_ref[:, :rank_columns] = total.astype(small_ref.dtype)


def write_rows(acc, outs, n_y, n_z):
    z = lax.axis_index("gz")
    rows_here = outs[0].shape[0] // n_y
    for k in range(n_z):
        for y in range(n_y):
            owner = y * n_z + jnp.bitwise_xor(z, k)
            begin = pl.multiple_of(owner * rows_here, rows_here)
            outs[k][y * rows_here : (y + 1) * rows_here, :] = acc[
                pl.ds(begin, rows_here), :
            ].astype(outs[k].dtype)


def multiply(x_ref, weights, step, acc):
    width = weights[0].shape[1]
    for c in range(0, width * len(weights), step):
        inner = c % width
        acc[:, c : c + step] = jnp.dot(
            x_ref[...],
            weights[c // width][:, inner : inner + step],
            preferred_element_type=jnp.float32,
        )


def product_kernel(n_w, n_y, n_z, step, _, x_ref, *refs):
    weights, outs, acc = refs[:n_w], refs[n_w:-1], refs[-1]
    multiply(x_ref, weights, step, acc)
    write_rows(acc, outs, n_y, n_z)


def pair_kernel(n_y, n_z, step, start_ref, up_ref, *refs):
    smalls, refs = refs[:n_z], refs[n_z:]
    firsts, lasts = refs[:n_z], refs[n_z : 2 * n_z]
    outs, acc = refs[2 * n_z : -1], refs[-1]
    rows, done = firsts[0].shape
    rows_here = rows // n_y
    columns = done + lasts[0].shape[1]
    adapters, rank_columns, _ = up_ref.shape
    z = lax.axis_index("gz")

    def added(parts, here):
        total = parts[0][:, here]
        for part in parts[1:]:
            total = total + part[:, here].astype(jnp.float32)
        return total

    small = jnp.zeros((rows, 2 * LANES), jnp.float32)
    for part in smalls:
        blocks = []
        for y in range(n_y):
            begin = pl.multiple_of((y * n_z + z) * rows_here, rows_here)
            blocks.append(part[pl.ds(begin, rows_here), :].astype(jnp.float32))
        small = small + jnp.concatenate(blocks, axis=0)
    square = join_wide(small[:, LANES:])
    down = small[:, :rank_columns].astype(jnp.bfloat16)
    row = lax.broadcasted_iota(jnp.int32, (rows, rank_columns), 0)
    row = (row // rows_here * n_z + z) * rows_here + lax.rem(row, rows_here)
    spread = jnp.concatenate(
        [
            jnp.where((row >= start_ref[a]) & (row < start_ref[a + 1]), down, jnp.zeros_like(down))
            for a in range(adapters)
        ],
        axis=1,
    )
    for c in range(0, columns, step):
        if c < done:
            base = added(firsts, slice(c, c + step))
        else:
            base = added(lasts, slice(c - done, c - done + step))
        up = up_ref[:, :, c : c + step].reshape(adapters * rank_columns, step)
        acc[:, c : c + step] = base + jnp.dot(spread, up, preferred_element_type=jnp.float32)
    acc[:, columns:] = split_wide(jnp.broadcast_to(square, (rows, LANES)))
    y = lax.axis_index("gy")
    for k in range(n_y):
        begin = pl.multiple_of(jnp.bitwise_xor(y, k) * rows_here, rows_here)
        outs[k][...] = acc[pl.ds(begin, rows_here), :].astype(outs[k].dtype)


def final_kernel(*refs):
    parts, out_ref = refs[:-1], refs[-1]
    columns = out_ref.shape[1]
    total = parts[0][...]
    for other in parts[1:]:
        total = total + other[...].astype(jnp.float32)
    mean_sq = join_wide(total[:, columns:])
    scale = lax.rsqrt(mean_sq + EPSILON)
    value = jnp.where(mean_sq < jnp.inf, total[:, :columns] * scale, 0.0)
    out_ref[...] = value.astype(out_ref.dtype)


def body(
    hidden,
    attention_norm_gain,
    query_weight,
    slot_down_factors,
    adapter_up_factors,
    adapter_of_row,
    padded_adapter_rank,
    adapter_in_slot,
    segment_starts,
):
    n_x, n_y, n_z = lax.axis_size("gx"), lax.axis_size("gy"), lax.axis_size("gz")
    groups = n_y * n_z
    block_rows, depth = hidden.shape
    columns = query_weight.shape[1]
    rows = n_x * block_rows
    rows_here = rows // groups

    def send(value, axis, n, k):
        return lax.ppermute(value, axis, [(j, j ^ k) for j in range(n)])

    def spread_out(made, axis, n):
        return [made[0]] + [send(made[k], axis, n, k) for k in range(1, n)]

    blocks = [hidden] + [send(hidden, "gx", n_x, k) for k in range(1, n_x)]

    step = min(512, columns // 4)
    n_w, pieces = 4, 4
    f32, bf16 = jnp.float32, jnp.bfloat16
    token, *weights = pl.pallas_call(
        functools.partial(fetch_kernel, n_w),
        out_shape=[jax.ShapeDtypeStruct((8, LANES), f32)]
        + [pltpu.VMEM((depth, columns // n_w), query_weight.dtype)] * n_w,
        in_specs=[ANY],
        out_specs=[VMEM] * (1 + n_w),
        scratch_shapes=[pltpu.SemaphoreType.DMA((n_w, pieces))],
        cost_estimate=cost(0, 2 * query_weight.size),
        compiler_params=params(4),
        name="fetch_weight",
    )(query_weight)

    x, small = pl.pallas_call(
        functools.partial(rows_kernel, n_x, depth * groups),
        out_shape=(
            jax.ShapeDtypeStruct((rows, depth), bf16),
            jax.ShapeDtypeStruct((rows, 2 * LANES), bf16),
        ),
        in_specs=[SMEM] * 3 + [VMEM] * 2 + [ANY] + [VMEM] * n_x,
        out_specs=(VMEM,) * 2,
        compiler_params=params(4 + (rows * depth >> 16)),
        name="scaled_rows",
    )(
        padded_adapter_rank,
        adapter_in_slot,
        segment_starts,
        attention_norm_gain,
        jnp.swapaxes(slot_down_factors, 1, 2),
        token,
        *blocks,
    )

    half = small + send(small, "gx", n_x, 1)
    hop = 2
    small = half
    while hop < n_x:
        small = small + send(small, "gx", n_x, hop)
        hop *= 2
    smalls = [small] + [send(small, "gz", n_z, k) for k in range(1, n_z)]

    weights = [pltpu.with_memory_space_constraint(w, pltpu.VMEM) for w in weights]
    kept = n_y * rows_here

    def shapes(n, shape):
        return [jax.ShapeDtypeStruct(shape, f32 if k == 0 else bf16) for k in range(n)]

    def product(some, after, weight_of_time):
        wide = len(some) * (columns // n_w)
        made = pl.pallas_call(
            functools.partial(product_kernel, len(some), n_y, n_z, step),
            out_shape=shapes(n_z, (kept, wide)),
            in_specs=[ANY] + [VMEM] * (1 + len(some)),
            out_specs=[VMEM] * n_z,
            scratch_shapes=[pltpu.VMEM((rows, wide), f32)],
            cost_estimate=cost(2 * rows * depth * wide * weight_of_time, 2 * depth * wide),
            compiler_params=params(4 + (rows * depth >> 16)),
            name="product",
        )(after, x, *some)
        return spread_out(made, "gz", n_z)

    firsts = product(weights[:-1], token, 1)
    lasts = product(weights[-1:], half, 8)

    made = pl.pallas_call(
        functools.partial(pair_kernel, n_y, n_z, step),
        out_shape=shapes(n_y, (rows_here, columns + LANES)),
        in_specs=[SMEM] + [VMEM] * (1 + 3 * n_z),
        out_specs=[VMEM] * n_y,
        scratch_shapes=[pltpu.VMEM((kept, columns + LANES), f32)],
        compiler_params=params(4 + (rows * depth >> 16)),
        name="chip_sums",
    )(segment_starts, adapter_up_factors, *smalls, *firsts, *lasts)
    parts = spread_out(made, "gy", n_y)

    return pl.pallas_call(
        final_kernel,
        out_shape=jax.ShapeDtypeStruct((rows_here, columns), bf16),
        in_specs=[VMEM] * n_y,
        out_specs=VMEM,
        compiler_params=params(4 + (rows * depth >> 16)),
        name="query_rows",
    )(*parts)


def solution(mesh):
    return jax.shard_map(
        body,
        mesh=mesh,
        in_specs=(
            P(("rep", "gx"), ("gy", "gz")),
            P(("gy", "gz")),
            P(("gy", "gz"), "gx"),
            P("gx", ("gy", "gz"), None),
            P(None, None, "gx"),
            P("rep"),
            P(),
            P(),
            P("rep"),
        ),
        out_specs=P(("rep", "gy", "gz"), "gx"),
        check_vma=False,
    )
```

```python
import functools

import jax
import jax.numpy as jnp
from jax import lax
from jax.experimental import pallas as pl
from jax.experimental.pallas import tpu as pltpu
from jax.sharding import PartitionSpec as P

EPSILON = 1e-05
ADAPTER_ALPHA = 32.0
LANES = 128
MIB = 1 << 20

VMEM = pl.BlockSpec(memory_space=pltpu.VMEM)
SMEM = pl.BlockSpec(memory_space=pltpu.SMEM)
ANY = pl.BlockSpec(memory_space=pl.ANY)


def params(mib):
    return pltpu.CompilerParams(vmem_limit_bytes=mib * MIB)


def cost(flops, moved):
    return pl.CostEstimate(flops=flops, bytes_accessed=moved, transcendentals=0)


def weight_copies(w_hbm, first, w_vmem, sems):
    pieces = sems.shape[0]
    depth, width = w_vmem.shape
    step = depth // pieces
    return [
        pltpu.make_async_copy(
            w_hbm.at[pl.ds(p * step, step), pl.ds(first, width)],
            w_vmem.at[pl.ds(p * step, step)],
            sems.at[p],
        )
        for p in range(pieces)
    ]


def fetch_kernel(n, w_hbm, token_ref, *refs):
    weights, sems = refs[:n], refs[n]
    copies = []
    first = 0
    for j, w_vmem in enumerate(weights):
        copies += weight_copies(w_hbm, first, w_vmem, sems.at[j])
        first += w_vmem.shape[1]
    for copy in copies:
        copy.start()
    token_ref[...] = jnp.zeros(token_ref.shape, token_ref.dtype)
    for copy in copies:
        copy.wait()


def split_wide(value):
    high = value.astype(jnp.bfloat16).astype(jnp.float32)
    low = jnp.where(high < jnp.inf, value - high, 0.0)
    lane = lax.broadcasted_iota(jnp.int32, value.shape, 1)
    return jnp.where(lane < LANES // 2, high, low)


def join_wide(value):
    return value[:, :1] + value[:, LANES - 1 :]


def rows_kernel(n, width, *refs):
    rank_ref, slot_ref, start_ref, gain_ref, down_ref, _ = refs[:6]
    blocks = refs[6 : 6 + n]
    x_ref, small_ref = refs[6 + n :]
    home = lax.axis_index("gx")
    block_rows = blocks[0].shape[0]
    rows = n * block_rows
    gain = gain_ref[...].astype(jnp.float32).reshape(1, gain_ref.shape[0])
    small_ref[...] = jnp.zeros(small_ref.shape, small_ref.dtype)
    for k in range(n):
        begin = pl.multiple_of(jnp.bitwise_xor(home, k) * block_rows, block_rows)
        values = blocks[k][...].astype(jnp.float32)
        x_ref[pl.ds(begin, block_rows), :] = (values * gain).astype(jnp.bfloat16)
        if k == 0:
            squares = jnp.sum(values * values, axis=1, keepdims=True) / width
            squares = split_wide(jnp.broadcast_to(squares, (block_rows, LANES)))
            small_ref[pl.ds(begin, block_rows), LANES:] = squares.astype(jnp.bfloat16)
    slots, rank_columns = down_ref.shape[0], down_ref.shape[1]
    row = lax.broadcasted_iota(jnp.int32, (rows, rank_columns), 0)
    col = lax.broadcasted_iota(jnp.int32, (rows, rank_columns), 1)
    total = jnp.zeros((rows, rank_columns), jnp.float32)
    for s in range(slots):
        adapter = slot_ref[home * slots + s]
        rank = rank_ref[adapter]
        live = (row >= start_ref[adapter]) & (row < start_ref[adapter + 1]) & (col < rank)
        projected = lax.dot_general(
            x_ref[...], down_ref[s], (((1,), (1,)), ((), ())), preferred_element_type=jnp.float32
        )
        scale = ADAPTER_ALPHA / jnp.full((rows, rank_columns), rank, jnp.int32).astype(jnp.float32)
        total = total + jnp.where(live, projected * scale, 0.0)
    small_ref[:, :rank_columns] = total.astype(small_ref.dtype)


def write_rows(acc, outs, n_y, n_z):
    z = lax.axis_index("gz")
    rows_here = outs[0].shape[0] // n_y
    for k in range(n_z):
        for y in range(n_y):
            owner = y * n_z + jnp.bitwise_xor(z, k)
            begin = pl.multiple_of(owner * rows_here, rows_here)
            outs[k][y * rows_here : (y + 1) * rows_here, :] = acc[
                pl.ds(begin, rows_here), :
            ].astype(outs[k].dtype)


def multiply(x_ref, weights, step, out, first):
    width = weights[0].shape[1]
    for c in range(0, width * len(weights), step):
        inner = c % width
        out[:, first + c : first + c + step] = jnp.dot(
            x_ref[...],
            weights[c // width][:, inner : inner + step],
            preferred_element_type=jnp.float32,
        )


def base_kernel(n_w, step, _, x_ref, *refs):
    multiply(x_ref, refs[:n_w], step, refs[n_w], 0)


def product_kernel(n_w, n_y, n_z, step, first, x_ref, side_ref, *refs):
    weights, outs, acc = refs[:n_w], refs[n_w:-1], refs[-1]
    wide = weights[0].shape[1] * n_w
    multiply(x_ref, weights, step, acc, first)
    begin = 0 if first else wide
    acc[:, begin : begin + side_ref.shape[1]] = side_ref[...].astype(jnp.float32)
    write_rows(acc, outs, n_y, n_z)


def pair_kernel(n_y, n_z, step, start_ref, up_ref, *refs):
    firsts, lasts = refs[:n_z], refs[n_z : 2 * n_z]
    outs, acc = refs[2 * n_z : -1], refs[-1]
    rows, done = firsts[0].shape
    rows_here = rows // n_y
    late = lasts[0].shape[1] - 2 * LANES
    columns = done + late
    adapters, rank_columns, _ = up_ref.shape
    z = lax.axis_index("gz")

    def added(parts, here):
        total = parts[0][:, here]
        for part in parts[1:]:
            total = total + part[:, here].astype(jnp.float32)
        return total

    square = join_wide(lasts[0][:, late + LANES :])
    for part in lasts[1:]:
        square = square + join_wide(part[:, late + LANES :].astype(jnp.float32))
    down = added(lasts, slice(late, late + rank_columns)).astype(jnp.bfloat16)
    row = lax.broadcasted_iota(jnp.int32, (rows, rank_columns), 0)
    row = (row // rows_here * n_z + z) * rows_here + lax.rem(row, rows_here)
    spread = jnp.concatenate(
        [
            jnp.where((row >= start_ref[a]) & (row < start_ref[a + 1]), down, jnp.zeros_like(down))
            for a in range(adapters)
        ],
        axis=1,
    )
    for c in range(0, columns, step):
        if c < done:
            base = added(firsts, slice(c, c + step))
        else:
            base = added(lasts, slice(c - done, c - done + step))
        up = up_ref[:, :, c : c + step].reshape(adapters * rank_columns, step)
        acc[:, c : c + step] = base + jnp.dot(spread, up, preferred_element_type=jnp.float32)
    acc[:, columns:] = split_wide(jnp.broadcast_to(square, (rows, LANES)))
    y = lax.axis_index("gy")
    for k in range(n_y):
        begin = pl.multiple_of(jnp.bitwise_xor(y, k) * rows_here, rows_here)
        outs[k][...] = acc[pl.ds(begin, rows_here), :].astype(outs[k].dtype)


def final_kernel(*refs):
    parts, out_ref = refs[:-1], refs[-1]
    columns = out_ref.shape[1]
    total = parts[0][...]
    for other in parts[1:]:
        total = total + other[...].astype(jnp.float32)
    mean_sq = join_wide(total[:, columns:])
    scale = lax.rsqrt(mean_sq + EPSILON)
    value = jnp.where(mean_sq < jnp.inf, total[:, :columns] * scale, 0.0)
    out_ref[...] = value.astype(out_ref.dtype)


def body(
    hidden,
    attention_norm_gain,
    query_weight,
    slot_down_factors,
    adapter_up_factors,
    adapter_of_row,
    padded_adapter_rank,
    adapter_in_slot,
    segment_starts,
):
    n_x, n_y, n_z = lax.axis_size("gx"), lax.axis_size("gy"), lax.axis_size("gz")
    groups = n_y * n_z
    block_rows, depth = hidden.shape
    columns = query_weight.shape[1]
    rows = n_x * block_rows
    rows_here = rows // groups

    def send(value, axis, n, k):
        return lax.ppermute(value, axis, [(j, j ^ k) for j in range(n)])

    def spread_out(made, axis, n):
        return [made[0]] + [send(made[k], axis, n, k) for k in range(1, n)]

    blocks = [hidden] + [send(hidden, "gx", n_x, k) for k in range(1, n_x)]

    step = min(512, columns // 4)
    n_w, pieces = 4, 8
    f32, bf16 = jnp.float32, jnp.bfloat16
    token, *weights = pl.pallas_call(
        functools.partial(fetch_kernel, n_w),
        out_shape=[jax.ShapeDtypeStruct((8, LANES), f32)]
        + [pltpu.VMEM((depth, columns // n_w), query_weight.dtype)] * n_w,
        in_specs=[ANY],
        out_specs=[VMEM] * (1 + n_w),
        scratch_shapes=[pltpu.SemaphoreType.DMA((n_w, pieces))],
        cost_estimate=cost(0, 2 * query_weight.size),
        compiler_params=params(4),
        name="fetch_weight",
    )(query_weight)

    x, small = pl.pallas_call(
        functools.partial(rows_kernel, n_x, depth * groups),
        out_shape=(
            jax.ShapeDtypeStruct((rows, depth), bf16),
            jax.ShapeDtypeStruct((rows, 2 * LANES), bf16),
        ),
        in_specs=[SMEM] * 3 + [VMEM] * 2 + [ANY] + [VMEM] * n_x,
        out_specs=(VMEM,) * 2,
        compiler_params=params(4 + (rows * depth >> 16)),
        name="scaled_rows",
    )(
        padded_adapter_rank,
        adapter_in_slot,
        segment_starts,
        attention_norm_gain,
        jnp.swapaxes(slot_down_factors, 1, 2),
        token,
        *blocks,
    )

    hop = 1
    while hop < n_x:
        small = small + send(small, "gx", n_x, hop)
        hop *= 2

    weights = [pltpu.with_memory_space_constraint(w, pltpu.VMEM) for w in weights]
    kept = n_y * rows_here

    def shapes(n, shape):
        return [jax.ShapeDtypeStruct(shape, f32 if k == 0 else bf16) for k in range(n)]

    quarter = columns // n_w
    base = pl.pallas_call(
        functools.partial(base_kernel, 1, step),
        out_shape=jax.ShapeDtypeStruct((rows, quarter), f32),
        in_specs=[ANY] + [VMEM] * 2,
        out_specs=VMEM,
        cost_estimate=cost(2 * rows * depth * quarter, 2 * depth * quarter),
        compiler_params=params(4 + (rows * depth >> 16)),
        name="first_columns",
    )(token, x, weights[0])

    def product(some, first, side, times, name):
        wide = first + len(some) * quarter + (0 if first else side.shape[1])
        made = pl.pallas_call(
            functools.partial(product_kernel, len(some), n_y, n_z, step, first),
            out_shape=shapes(n_z, (kept, wide)),
            in_specs=[VMEM] * (2 + len(some)),
            out_specs=[VMEM] * n_z,
            scratch_shapes=[pltpu.VMEM((rows, wide), f32)],
            cost_estimate=cost(2 * rows * depth * wide * times, 2 * depth * wide),
            compiler_params=params(4 + (rows * depth >> 16)),
            name=name,
        )(x, side, *some)
        return spread_out(made, "gz", n_z)

    firsts = product(weights[1:-1], quarter, base, 4, "middle_columns")
    lasts = product(weights[-1:], 0, small, 8, "last_columns")

    made = pl.pallas_call(
        functools.partial(pair_kernel, n_y, n_z, step),
        out_shape=shapes(n_y, (rows_here, columns + LANES)),
        in_specs=[SMEM] + [VMEM] * (1 + 2 * n_z),
        out_specs=[VMEM] * n_y,
        scratch_shapes=[pltpu.VMEM((kept, columns + LANES), f32)],
        compiler_params=params(4 + (rows * depth >> 16)),
        name="chip_sums",
    )(segment_starts, adapter_up_factors, *firsts, *lasts)
    parts = spread_out(made, "gy", n_y)

    return pl.pallas_call(
        final_kernel,
        out_shape=jax.ShapeDtypeStruct((rows_here, columns), bf16),
        in_specs=[VMEM] * n_y,
        out_specs=VMEM,
        compiler_params=params(4 + (rows * depth >> 16)),
        name="query_rows",
    )(*parts)


def solution(mesh):
    return jax.shard_map(
        body,
        mesh=mesh,
        in_specs=(
            P(("rep", "gx"), ("gy", "gz")),
            P(("gy", "gz")),
            P(("gy", "gz"), "gx"),
            P("gx", ("gy", "gz"), None),
            P(None, None, "gx"),
            P("rep"),
            P(),
            P(),
            P("rep"),
        ),
        out_specs=P(("rep", "gy", "gz"), "gx"),
        check_vma=False,
    )
```

```python
import functools

import jax
import jax.numpy as jnp
from jax import lax
from jax.experimental import pallas as pl
from jax.experimental.pallas import tpu as pltpu
from jax.sharding import PartitionSpec as P

EPSILON = 1e-05
ADAPTER_ALPHA = 32.0
LANES = 128
MIB = 1 << 20

VMEM = pl.BlockSpec(memory_space=pltpu.VMEM)
SMEM = pl.BlockSpec(memory_space=pltpu.SMEM)
ANY = pl.BlockSpec(memory_space=pl.ANY)


def params(mib):
    return pltpu.CompilerParams(vmem_limit_bytes=mib * MIB)


def cost(flops, moved):
    return pl.CostEstimate(flops=flops, bytes_accessed=moved, transcendentals=0)


def weight_copies(w_hbm, first, w_vmem, sems):
    pieces = sems.shape[0]
    depth, width = w_vmem.shape
    step = depth // pieces
    return [
        pltpu.make_async_copy(
            w_hbm.at[pl.ds(p * step, step), pl.ds(first, width)],
            w_vmem.at[pl.ds(p * step, step)],
            sems.at[p],
        )
        for p in range(pieces)
    ]


def fetch_kernel(n, w_hbm, token_ref, *refs):
    weights, sems = refs[:n], refs[n]
    copies = []
    first = 0
    for j, w_vmem in enumerate(weights):
        copies += weight_copies(w_hbm, first, w_vmem, sems.at[j])
        first += w_vmem.shape[1]
    for copy in copies:
        copy.start()
    token_ref[...] = jnp.zeros(token_ref.shape, token_ref.dtype)
    for copy in copies:
        copy.wait()


def split_wide(value):
    high = value.astype(jnp.bfloat16).astype(jnp.float32)
    low = jnp.where(high < jnp.inf, value - high, 0.0)
    lane = lax.broadcasted_iota(jnp.int32, value.shape, 1)
    return jnp.where(lane < LANES // 2, high, low)


def join_wide(value):
    return value[:, :1] + value[:, LANES - 1 :]


def rows_kernel(order, width, *refs):
    n = len(order)
    rank_ref, slot_ref, start_ref, gain_ref, down_ref, _ = refs[:6]
    blocks = refs[6 : 6 + n]
    x_ref, small_ref = refs[6 + n :]
    home = lax.axis_index("gx")
    block_rows = blocks[0].shape[0]
    rows = n * block_rows
    gain = gain_ref[...].astype(jnp.float32).reshape(1, gain_ref.shape[0])
    small_ref[...] = jnp.zeros(small_ref.shape, small_ref.dtype)
    for k, block in zip(order, blocks):
        begin = pl.multiple_of(jnp.bitwise_xor(home, k) * block_rows, block_rows)
        values = block[...].astype(jnp.float32)
        x_ref[pl.ds(begin, block_rows), :] = (values * gain).astype(jnp.bfloat16)
        if k == 0:
            squares = jnp.sum(values * values, axis=1, keepdims=True) / width
            squares = split_wide(jnp.broadcast_to(squares, (block_rows, LANES)))
            small_ref[pl.ds(begin, block_rows), LANES:] = squares.astype(jnp.bfloat16)
    slots, rank_columns = down_ref.shape[0], down_ref.shape[1]
    row = lax.broadcasted_iota(jnp.int32, (rows, rank_columns), 0)
    col = lax.broadcasted_iota(jnp.int32, (rows, rank_columns), 1)
    total = jnp.zeros((rows, rank_columns), jnp.float32)
    for s in range(slots):
        adapter = slot_ref[home * slots + s]
        rank = rank_ref[adapter]
        live = (row >= start_ref[adapter]) & (row < start_ref[adapter + 1]) & (col < rank)
        projected = lax.dot_general(
            x_ref[...], down_ref[s], (((1,), (1,)), ((), ())), preferred_element_type=jnp.float32
        )
        scale = ADAPTER_ALPHA / jnp.full((rows, rank_columns), rank, jnp.int32).astype(jnp.float32)
        total = total + jnp.where(live, projected * scale, 0.0)
    small_ref[:, :rank_columns] = total.astype(small_ref.dtype)


def write_rows(acc, outs, n_y, n_z):
    z = lax.axis_index("gz")
    rows_here = outs[0].shape[0] // n_y
    for k in range(n_z):
        for y in range(n_y):
            owner = y * n_z + jnp.bitwise_xor(z, k)
            begin = pl.multiple_of(owner * rows_here, rows_here)
            outs[k][y * rows_here : (y + 1) * rows_here, :] = acc[
                pl.ds(begin, rows_here), :
            ].astype(outs[k].dtype)


def multiply(x_ref, weights, step, out, first):
    width = weights[0].shape[1]
    for c in range(0, width * len(weights), step):
        inner = c % width
        out[:, first + c : first + c + step] = jnp.dot(
            x_ref[...],
            weights[c // width][:, inner : inner + step],
            preferred_element_type=jnp.float32,
        )


def base_kernel(n_w, step, _, x_ref, *refs):
    multiply(x_ref, refs[:n_w], step, refs[n_w], 0)


def product_kernel(n_w, n_y, n_z, step, first, x_ref, side_ref, *refs):
    weights, outs, acc = refs[:n_w], refs[n_w:-1], refs[-1]
    wide = weights[0].shape[1] * n_w
    multiply(x_ref, weights, step, acc, first)
    begin = 0 if first else wide
    acc[:, begin : begin + side_ref.shape[1]] = side_ref[...].astype(jnp.float32)
    write_rows(acc, outs, n_y, n_z)


def pair_kernel(n_y, side, *refs):
    parts, outs = refs[:-n_y], refs[-n_y:]
    rows_here, columns = outs[0].shape
    y = lax.axis_index("gy")
    for k in range(n_y):
        begin = pl.multiple_of(jnp.bitwise_xor(y, k) * rows_here, rows_here)
        here = pl.ds(begin, rows_here)
        total = parts[0][here, :]
        for part in parts[1:]:
            total = total + part[here, :].astype(jnp.float32)
        if side:
            late = columns - LANES
            square = join_wide(total[:, late:])
            outs[k][:, late:] = split_wide(jnp.broadcast_to(square, (rows_here, LANES))).astype(
                outs[k].dtype
            )
            outs[k][:, :late] = total[:, :late].astype(outs[k].dtype)
        else:
            outs[k][...] = total.astype(outs[k].dtype)


def final_kernel(n, n_z, step, start_ref, up_ref, *refs):
    firsts, lasts, out_ref = refs[:n], refs[n : 2 * n], refs[2 * n]
    rows_here, columns = out_ref.shape
    done = firsts[0].shape[1]
    late = columns - done
    adapters, rank_columns, _ = up_ref.shape

    def added(parts, begin, end):
        total = parts[0][:, begin:end]
        for part in parts[1:]:
            total = total + part[:, begin:end].astype(jnp.float32)
        return total

    side = added(lasts, late, late + 2 * LANES)
    mean_sq = join_wide(side[:, LANES:])
    scale = lax.rsqrt(mean_sq + EPSILON)
    down = side[:, :rank_columns].astype(jnp.bfloat16)
    first_row = (lax.axis_index("gy") * n_z + lax.axis_index("gz")) * rows_here
    row = lax.broadcasted_iota(jnp.int32, (rows_here, rank_columns), 0) + first_row
    spread = jnp.concatenate(
        [
            jnp.where((row >= start_ref[a]) & (row < start_ref[a + 1]), down, jnp.zeros_like(down))
            for a in range(adapters)
        ],
        axis=1,
    )
    for c in range(0, columns, step):
        if c < done:
            base = added(firsts, c, c + step)
        else:
            base = added(lasts, c - done, c - done + step)
        up = up_ref[:, :, c : c + step].reshape(adapters * rank_columns, step)
        total = base + jnp.dot(spread, up, preferred_element_type=jnp.float32)
        value = jnp.where(mean_sq < jnp.inf, total * scale, 0.0)
        out_ref[:, c : c + step] = value.astype(out_ref.dtype)


def body(
    hidden,
    attention_norm_gain,
    query_weight,
    slot_down_factors,
    adapter_up_factors,
    adapter_of_row,
    padded_adapter_rank,
    adapter_in_slot,
    segment_starts,
):
    n_x, n_y, n_z = lax.axis_size("gx"), lax.axis_size("gy"), lax.axis_size("gz")
    groups = n_y * n_z
    block_rows, depth = hidden.shape
    columns = query_weight.shape[1]
    rows = n_x * block_rows
    rows_here = rows // groups

    def send(value, axis, n, k):
        return lax.ppermute(value, axis, [(j, j ^ k) for j in range(n)])

    def spread_out(made, axis, n):
        return [made[0]] + [send(made[k], axis, n, k) for k in range(1, n)]

    near_last = [0] + sorted(range(1, n_x), reverse=True)
    blocks = [hidden] + [send(hidden, "gx", n_x, k) for k in near_last[1:]]

    step = min(512, columns // 4)
    n_w, pieces = 4, 8
    f32, bf16 = jnp.float32, jnp.bfloat16
    token, *weights = pl.pallas_call(
        functools.partial(fetch_kernel, n_w),
        out_shape=[jax.ShapeDtypeStruct((8, LANES), f32)]
        + [pltpu.VMEM((depth, columns // n_w), query_weight.dtype)] * n_w,
        in_specs=[ANY],
        out_specs=[VMEM] * (1 + n_w),
        scratch_shapes=[pltpu.SemaphoreType.DMA((n_w, pieces))],
        cost_estimate=cost(0, 2 * query_weight.size),
        compiler_params=params(4),
        name="fetch_weight",
    )(query_weight)

    x, small = pl.pallas_call(
        functools.partial(rows_kernel, near_last, depth * groups),
        out_shape=(
            jax.ShapeDtypeStruct((rows, depth), bf16),
            jax.ShapeDtypeStruct((rows, 2 * LANES), bf16),
        ),
        in_specs=[SMEM] * 3 + [VMEM] * 2 + [ANY] + [VMEM] * n_x,
        out_specs=(VMEM,) * 2,
        compiler_params=params(4 + (rows * depth >> 16)),
        name="scaled_rows",
    )(
        padded_adapter_rank,
        adapter_in_slot,
        segment_starts,
        attention_norm_gain,
        jnp.swapaxes(slot_down_factors, 1, 2),
        token,
        *blocks,
    )

    hop = 1
    while hop < n_x:
        small = small + send(small, "gx", n_x, hop)
        hop *= 2

    weights = [pltpu.with_memory_space_constraint(w, pltpu.VMEM) for w in weights]
    kept = n_y * rows_here

    def shapes(n, shape):
        return [jax.ShapeDtypeStruct(shape, f32 if k == 0 else bf16) for k in range(n)]

    quarter = columns // n_w
    base = pl.pallas_call(
        functools.partial(base_kernel, 1, step),
        out_shape=jax.ShapeDtypeStruct((rows, quarter), f32),
        in_specs=[ANY] + [VMEM] * 2,
        out_specs=VMEM,
        cost_estimate=cost(2 * rows * depth * quarter, 2 * depth * quarter),
        compiler_params=params(4 + (rows * depth >> 16)),
        name="first_columns",
    )(token, x, weights[0])

    def product(some, first, side, times, name):
        wide = first + len(some) * quarter + (0 if first else side.shape[1])
        made = pl.pallas_call(
            functools.partial(product_kernel, len(some), n_y, n_z, step, first),
            out_shape=shapes(n_z, (kept, wide)),
            in_specs=[VMEM] * (2 + len(some)),
            out_specs=[VMEM] * n_z,
            scratch_shapes=[pltpu.VMEM((rows, wide), f32)],
            cost_estimate=cost(2 * rows * depth * wide * times, 2 * depth * wide),
            compiler_params=params(4 + (rows * depth >> 16)),
            name=name,
        )(x, side, *some)
        return spread_out(made, "gz", n_z)

    firsts = product(weights[1:-1], quarter, base, 4, "middle_columns")
    lasts = product(weights[-1:], 0, small, 8, "last_columns")

    def chip_sums(parts, side, name):
        wide = parts[0].shape[1]
        made = pl.pallas_call(
            functools.partial(pair_kernel, n_y, side),
            out_shape=shapes(n_y, (rows_here, wide)),
            in_specs=[VMEM] * n_z,
            out_specs=[VMEM] * n_y,
            cost_estimate=cost(2 * rows * depth * quarter, 2 * depth * quarter),
            compiler_params=params(4 + (rows * depth >> 16)),
            name=name,
        )(*parts)
        return spread_out(made, "gy", n_y)

    first_parts = chip_sums(firsts, False, "first_sums")
    last_parts = chip_sums(lasts, True, "last_sums")

    return pl.pallas_call(
        functools.partial(final_kernel, n_y, n_z, step),
        out_shape=jax.ShapeDtypeStruct((rows_here, columns), bf16),
        in_specs=[SMEM] + [VMEM] * (1 + 2 * n_y),
        out_specs=VMEM,
        compiler_params=params(4 + (rows * depth >> 16)),
        name="query_rows",
    )(segment_starts, adapter_up_factors, *first_parts, *last_parts)


def solution(mesh):
    return jax.shard_map(
        body,
        mesh=mesh,
        in_specs=(
            P(("rep", "gx"), ("gy", "gz")),
            P(("gy", "gz")),
            P(("gy", "gz"), "gx"),
            P("gx", ("gy", "gz"), None),
            P(None, None, "gx"),
            P("rep"),
            P(),
            P(),
            P("rep"),
        ),
        out_specs=P(("rep", "gy", "gz"), "gx"),
        check_vma=False,
    )
```

```python
import functools

import jax
import jax.numpy as jnp
from jax import lax
from jax.experimental import pallas as pl
from jax.experimental.pallas import tpu as pltpu
from jax.sharding import PartitionSpec as P

EPSILON = 1e-05
ADAPTER_ALPHA = 32.0
LANES = 128
MIB = 1 << 20

VMEM = pl.BlockSpec(memory_space=pltpu.VMEM)
HBM = pl.BlockSpec(memory_space=pltpu.HBM)
ANY = pl.BlockSpec(memory_space=pl.ANY)


def params(mib):
    return pltpu.CompilerParams(vmem_limit_bytes=mib * MIB)


def cost(flops, moved):
    return pl.CostEstimate(flops=flops, bytes_accessed=moved, transcendentals=0)


def weight_copies(w_hbm, first, w_vmem, sems):
    pieces = sems.shape[0]
    depth, width = w_vmem.shape
    step = depth // pieces
    return [
        pltpu.make_async_copy(
            w_hbm.at[pl.ds(p * step, step), pl.ds(first, width)],
            w_vmem.at[pl.ds(p * step, step)],
            sems.at[p],
        )
        for p in range(pieces)
    ]


def fetch_kernel(n, w_hbm, rank_hbm, slot_hbm, start_hbm, factor_ref, spread_ref, *refs):
    weights, sems, scalar_sems = refs[:n], refs[n], refs[n + 1]
    rank_ref, slot_ref, start_ref = refs[n + 2 :]
    scalars = [
        pltpu.make_async_copy(source, target, scalar_sems.at[j])
        for j, (source, target) in enumerate(
            ((rank_hbm, rank_ref), (slot_hbm, slot_ref), (start_hbm, start_ref))
        )
    ]
    for copy in scalars:
        copy.start()
    copies = []
    first = 0
    for j, w_vmem in enumerate(weights):
        copies += weight_copies(w_hbm, first, w_vmem, sems.at[j])
        first += w_vmem.shape[1]
    for copy in copies:
        copy.start()
    for copy in scalars:
        copy.wait()
    slots, rows, rank_columns = factor_ref.shape
    home = lax.axis_index("gx")
    row = lax.broadcasted_iota(jnp.int32, (rows, rank_columns), 0)
    col = lax.broadcasted_iota(jnp.int32, (rows, rank_columns), 1)
    for s in range(slots):
        adapter = slot_ref[home * slots + s]
        rank = rank_ref[adapter]
        live = (row >= start_ref[adapter]) & (row < start_ref[adapter + 1]) & (col < rank)
        scale = ADAPTER_ALPHA / jnp.full((rows, rank_columns), rank, jnp.int32).astype(jnp.float32)
        factor_ref[s] = jnp.where(live, scale, 0.0)
    adapters = spread_ref.shape[1] // rank_columns
    for a in range(adapters):
        live = (row >= start_ref[a]) & (row < start_ref[a + 1])
        spread_ref[:, a * rank_columns : (a + 1) * rank_columns] = jnp.where(live, 1.0, 0.0)
    for copy in copies:
        copy.wait()


def split_wide(value):
    high = value.astype(jnp.bfloat16).astype(jnp.float32)
    low = jnp.where(high < jnp.inf, value - high, 0.0)
    lane = lax.broadcasted_iota(jnp.int32, value.shape, 1)
    return jnp.where(lane < LANES // 2, high, low)


def join_wide(value):
    return value[:, :1] + value[:, LANES - 1 :]


def rows_kernel(order, width, gain_ref, down_ref, factor_ref, *refs):
    n = len(order)
    blocks = refs[:n]
    x_ref, small_ref = refs[n:]
    home = lax.axis_index("gx")
    block_rows = blocks[0].shape[0]
    gain = gain_ref[...].astype(jnp.float32).reshape(1, gain_ref.shape[0])
    small_ref[...] = jnp.zeros(small_ref.shape, small_ref.dtype)
    for k, block in zip(order, blocks):
        begin = pl.multiple_of(jnp.bitwise_xor(home, k) * block_rows, block_rows)
        values = block[...].astype(jnp.float32)
        x_ref[pl.ds(begin, block_rows), :] = (values * gain).astype(jnp.bfloat16)
        if k == 0:
            squares = jnp.sum(values * values, axis=1, keepdims=True) / width
            squares = split_wide(jnp.broadcast_to(squares, (block_rows, LANES)))
            small_ref[pl.ds(begin, block_rows), LANES:] = squares.astype(jnp.bfloat16)
    slots, rows, rank_columns = factor_ref.shape
    total = jnp.zeros((rows, rank_columns), jnp.float32)
    for s in range(slots):
        projected = lax.dot_general(
            x_ref[...], down_ref[s], (((1,), (1,)), ((), ())), preferred_element_type=jnp.float32
        )
        factor = factor_ref[s]
        total = total + jnp.where(factor > 0, projected * factor, 0.0)
    small_ref[:, :rank_columns] = total.astype(small_ref.dtype)


def write_rows(acc, outs, n_y, n_z):
    z = lax.axis_index("gz")
    rows_here = outs[0].shape[0] // n_y
    for k in range(n_z):
        for y in range(n_y):
            owner = y * n_z + jnp.bitwise_xor(z, k)
            begin = pl.multiple_of(owner * rows_here, rows_here)
            outs[k][y * rows_here : (y + 1) * rows_here, :] = acc[
                pl.ds(begin, rows_here), :
            ].astype(outs[k].dtype)


def multiply(x_ref, weights, step, out, first):
    width = weights[0].shape[1]
    for c in range(0, width * len(weights), step):
        inner = c % width
        out[:, first + c : first + c + step] = jnp.dot(
            x_ref[...],
            weights[c // width][:, inner : inner + step],
            preferred_element_type=jnp.float32,
        )


def base_kernel(n_w, step, x_ref, *refs):
    multiply(x_ref, refs[:n_w], step, refs[n_w], 0)


def product_kernel(n_w, n_y, n_z, step, first, x_ref, *refs):
    if first:
        base_ref, refs = refs[0], refs[2:]
    weights, outs, acc = refs[:n_w], refs[n_w:-1], refs[-1]
    if first:
        acc[:, :first] = base_ref[...]
    multiply(x_ref, weights, step, acc, first)
    write_rows(acc, outs, n_y, n_z)


def chip_rows(parts, here):
    total = parts[0][here, :].astype(jnp.float32)
    for part in parts[1:]:
        total = total + part[here, :].astype(jnp.float32)
    return total


def pair_kernel(n_y, n_z, *refs):
    parts, smalls, outs = refs[:n_z], refs[n_z:-n_y], refs[-n_y:]
    rows_here = outs[0].shape[0]
    columns = parts[0].shape[1]
    y, z = lax.axis_index("gy"), lax.axis_index("gz")
    for k in range(n_y):
        other = jnp.bitwise_xor(y, k)
        here = pl.ds(pl.multiple_of(other * rows_here, rows_here), rows_here)
        outs[k][:, :columns] = chip_rows(parts, here).astype(outs[k].dtype)
        if smalls:
            owner = other * n_z + z
            here = pl.ds(pl.multiple_of(owner * rows_here, rows_here), rows_here)
            small = chip_rows(smalls, here)
            square = jnp.broadcast_to(join_wide(small[:, LANES:]), (rows_here, LANES))
            outs[k][:, columns : columns + LANES] = small[:, :LANES].astype(outs[k].dtype)
            outs[k][:, columns + LANES :] = split_wide(square).astype(outs[k].dtype)


def final_kernel(n, n_z, step, spread_ref, up_ref, *refs):
    firsts, lasts, out_ref = refs[:n], refs[n : 2 * n], refs[2 * n]
    rows_here, columns = out_ref.shape
    done = firsts[0].shape[1]
    late = columns - done
    adapters, rank_columns, _ = up_ref.shape

    def added(parts, begin, end):
        total = parts[0][:, begin:end]
        for part in parts[1:]:
            total = total + part[:, begin:end].astype(jnp.float32)
        return total

    side = added(lasts, late, late + 2 * LANES)
    mean_sq = join_wide(side[:, LANES:])
    scale = lax.rsqrt(mean_sq + EPSILON)
    owner = lax.axis_index("gy") * n_z + lax.axis_index("gz")
    live = spread_ref[pl.ds(pl.multiple_of(owner * rows_here, rows_here), rows_here), :]
    spread = jnp.concatenate([side[:, :rank_columns]] * adapters, axis=1)
    spread = jnp.where(live > 0, spread, 0.0).astype(jnp.bfloat16)
    for c in range(0, columns, step):
        if c < done:
            base = added(firsts, c, c + step)
        else:
            base = added(lasts, c - done, c - done + step)
        up = up_ref[:, :, c : c + step].reshape(adapters * rank_columns, step)
        total = base + jnp.dot(spread, up, preferred_element_type=jnp.float32)
        value = jnp.where(mean_sq < jnp.inf, total * scale, 0.0)
        out_ref[:, c : c + step] = value.astype(out_ref.dtype)


def body(
    hidden,
    attention_norm_gain,
    query_weight,
    slot_down_factors,
    adapter_up_factors,
    adapter_of_row,
    padded_adapter_rank,
    adapter_in_slot,
    segment_starts,
):
    n_x, n_y, n_z = lax.axis_size("gx"), lax.axis_size("gy"), lax.axis_size("gz")
    groups = n_y * n_z
    block_rows, depth = hidden.shape
    columns = query_weight.shape[1]
    rows = n_x * block_rows
    rows_here = rows // groups

    def send(value, axis, n, k):
        return lax.ppermute(value, axis, [(j, j ^ k) for j in range(n)])

    def spread_out(made, axis, n):
        return [made[0]] + [send(made[k], axis, n, k) for k in range(1, n)]

    half = n_x // 2
    order = [0, *range(half, n_x), *range(half - 1, 0, -1)]
    blocks = [hidden] + [send(hidden, "gx", n_x, k) for k in order[1:]]

    step = min(512, columns // 4)
    n_w, pieces = 4, 8
    f32, bf16 = jnp.float32, jnp.bfloat16
    slots, rank_columns = slot_down_factors.shape[0], slot_down_factors.shape[2]
    adapters = adapter_up_factors.shape[0]
    quarter = columns // n_w
    kept = n_y * rows_here
    roomy = params(4 + (rows * depth >> 16))

    scalars = (padded_adapter_rank, adapter_in_slot, segment_starts)
    factor, spread, *weights = pl.pallas_call(
        functools.partial(fetch_kernel, n_w),
        out_shape=[
            jax.ShapeDtypeStruct((slots, rows, rank_columns), f32),
            jax.ShapeDtypeStruct((rows, adapters * rank_columns), f32),
        ]
        + [pltpu.VMEM((depth, quarter), query_weight.dtype)] * n_w,
        in_specs=[ANY] + [HBM] * 3,
        out_specs=[VMEM] * (2 + n_w),
        scratch_shapes=[
            pltpu.SemaphoreType.DMA((n_w, pieces)),
            pltpu.SemaphoreType.DMA((len(scalars),)),
            *[pltpu.SMEM(value.shape, value.dtype) for value in scalars],
        ],
        cost_estimate=cost(0, 2 * query_weight.size),
        compiler_params=roomy,
        name="fetch_weight",
    )(query_weight, *[pltpu.with_memory_space_constraint(v, pltpu.HBM) for v in scalars])
    weights = [pltpu.with_memory_space_constraint(w, pltpu.VMEM) for w in weights]

    x, small = pl.pallas_call(
        functools.partial(rows_kernel, order, depth * groups),
        out_shape=(
            jax.ShapeDtypeStruct((rows, depth), bf16),
            jax.ShapeDtypeStruct((rows, 2 * LANES), bf16),
        ),
        in_specs=[VMEM] * (3 + n_x),
        out_specs=(VMEM,) * 2,
        compiler_params=roomy,
        name="scaled_rows",
    )(attention_norm_gain, jnp.swapaxes(slot_down_factors, 1, 2), factor, *blocks)

    one_hop = small = small + send(small, "gx", n_x, 1)
    hop = 2
    while hop < n_x:
        small = small + send(small, "gx", n_x, hop)
        hop *= 2

    def shapes(n, shape):
        return [jax.ShapeDtypeStruct(shape, f32 if k == 0 else bf16) for k in range(n)]

    early = n_w // 2
    base_columns = early * quarter
    base = pl.pallas_call(
        functools.partial(base_kernel, early, step),
        out_shape=jax.ShapeDtypeStruct((rows, base_columns), f32),
        in_specs=[VMEM] * (1 + early),
        out_specs=VMEM,
        cost_estimate=cost(2 * rows * depth * base_columns, 2 * depth * base_columns),
        compiler_params=roomy,
        name="first_columns",
    )(x, *weights[:early])

    def product(some, bases, times, name):
        first = sum(part.shape[1] for part in bases[:1])
        wide = first + len(some) * quarter
        made = pl.pallas_call(
            functools.partial(product_kernel, len(some), n_y, n_z, step, first),
            out_shape=shapes(n_z, (kept, wide)),
            in_specs=[VMEM] * (1 + len(bases) + len(some)),
            out_specs=[VMEM] * n_z,
            scratch_shapes=[pltpu.VMEM((rows, wide), f32)],
            cost_estimate=cost(2 * rows * depth * wide * times, 2 * depth * wide),
            compiler_params=roomy,
            name=name,
        )(x, *bases, *some)
        return spread_out(made, "gz", n_z)

    firsts = product(weights[early:-1], [base, one_hop], 4, "middle_columns")
    lasts = product(weights[-1:], [], 8, "last_columns")
    smalls = spread_out([small] * n_z, "gz", n_z)

    def chip_sums(parts, sides, name):
        wide = parts[0].shape[1] + (2 * LANES if sides else 0)
        made = pl.pallas_call(
            functools.partial(pair_kernel, n_y, n_z),
            out_shape=shapes(n_y, (rows_here, wide)),
            in_specs=[VMEM] * (n_z + len(sides)),
            out_specs=[VMEM] * n_y,
            cost_estimate=cost(2 * rows * depth * quarter, 2 * depth * quarter),
            compiler_params=roomy,
            name=name,
        )(*parts, *sides)
        return spread_out(made, "gy", n_y)

    first_parts = chip_sums(firsts, [], "first_sums")
    last_parts = chip_sums(lasts, smalls, "last_sums")

    return pl.pallas_call(
        functools.partial(final_kernel, n_y, n_z, step),
        out_shape=jax.ShapeDtypeStruct((rows_here, columns), bf16),
        in_specs=[VMEM] * (2 + 2 * n_y),
        out_specs=VMEM,
        compiler_params=roomy,
        name="query_rows",
    )(spread, adapter_up_factors, *first_parts, *last_parts)


def solution(mesh):
    return jax.shard_map(
        body,
        mesh=mesh,
        in_specs=(
            P(("rep", "gx"), ("gy", "gz")),
            P(("gy", "gz")),
            P(("gy", "gz"), "gx"),
            P("gx", ("gy", "gz"), None),
            P(None, None, "gx"),
            P("rep"),
            P(),
            P(),
            P("rep"),
        ),
        out_specs=P(("rep", "gy", "gz"), "gx"),
        check_vma=False,
    )
```

```python
import functools

import jax
import jax.numpy as jnp
from jax import lax
from jax.experimental import pallas as pl
from jax.experimental.pallas import tpu as pltpu
from jax.sharding import PartitionSpec as P

EPSILON = 1e-05
ADAPTER_ALPHA = 32.0
LANES = 128
MIB = 1 << 20

VMEM = pl.BlockSpec(memory_space=pltpu.VMEM)
HBM = pl.BlockSpec(memory_space=pltpu.HBM)
ANY = pl.BlockSpec(memory_space=pl.ANY)


def params(mib):
    return pltpu.CompilerParams(vmem_limit_bytes=mib * MIB)


def cost(flops, moved):
    return pl.CostEstimate(flops=flops, bytes_accessed=moved, transcendentals=0)


def weight_copies(w_hbm, first, w_vmem, sems):
    pieces = sems.shape[0]
    depth, width = w_vmem.shape
    step = depth // pieces
    return [
        pltpu.make_async_copy(
            w_hbm.at[pl.ds(p * step, step), pl.ds(first, width)],
            w_vmem.at[pl.ds(p * step, step)],
            sems.at[p],
        )
        for p in range(pieces)
    ]


def load(w_hbm, first, weights, sems, meanwhile):
    copies = []
    for j, w_vmem in enumerate(weights):
        copies += weight_copies(w_hbm, first, w_vmem, sems.at[j])
        first += w_vmem.shape[1]
    for copy in copies:
        copy.start()
    meanwhile()
    for copy in copies:
        copy.wait()


def first_load_kernel(n, w_hbm, rank_hbm, slot_hbm, start_hbm, factor_ref, spread_ref, *refs):
    weights, sems, scalar_sems = refs[:n], refs[n], refs[n + 1]
    rank_ref, slot_ref, start_ref = refs[n + 2 :]

    def masks():
        pairs = ((rank_hbm, rank_ref), (slot_hbm, slot_ref), (start_hbm, start_ref))
        scalars = [
            pltpu.make_async_copy(source, target, scalar_sems.at[j])
            for j, (source, target) in enumerate(pairs)
        ]
        for copy in scalars:
            copy.start()
        for copy in scalars:
            copy.wait()
        slots, rows, rank_columns = factor_ref.shape
        home = lax.axis_index("gx")
        row = lax.broadcasted_iota(jnp.int32, (rows, rank_columns), 0)
        col = lax.broadcasted_iota(jnp.int32, (rows, rank_columns), 1)
        for s in range(slots):
            adapter = slot_ref[home * slots + s]
            rank = rank_ref[adapter]
            live = (row >= start_ref[adapter]) & (row < start_ref[adapter + 1]) & (col < rank)
            ranks = jnp.full((rows, rank_columns), rank, jnp.int32).astype(jnp.float32)
            factor_ref[s] = jnp.where(live, ADAPTER_ALPHA / ranks, 0.0)
        adapters = spread_ref.shape[1] // rank_columns
        for a in range(adapters):
            live = (row >= start_ref[a]) & (row < start_ref[a + 1])
            spread_ref[:, a * rank_columns : (a + 1) * rank_columns] = jnp.where(live, 1.0, 0.0)

    load(w_hbm, 0, weights, sems, masks)


def last_load_kernel(n, first, w_hbm, _, __, *refs):
    load(w_hbm, first, refs[:n], refs[n], lambda: None)


def split_wide(value):
    high = value.astype(jnp.bfloat16).astype(jnp.float32)
    low = jnp.where(high < jnp.inf, value - high, 0.0)
    lane = lax.broadcasted_iota(jnp.int32, value.shape, 1)
    return jnp.where(lane < LANES // 2, high, low)


def join_wide(value):
    return value[:, :1] + value[:, LANES - 1 :]


def rows_kernel(order, width, gain_ref, down_ref, factor_ref, *refs):
    n = len(order)
    blocks = refs[:n]
    x_ref, small_ref = refs[n:]
    home = lax.axis_index("gx")
    block_rows = blocks[0].shape[0]
    gain = gain_ref[...].astype(jnp.float32).reshape(1, gain_ref.shape[0])
    small_ref[...] = jnp.zeros(small_ref.shape, small_ref.dtype)
    for k, block in zip(order, blocks):
        begin = pl.multiple_of(jnp.bitwise_xor(home, k) * block_rows, block_rows)
        values = block[...].astype(jnp.float32)
        x_ref[pl.ds(begin, block_rows), :] = (values * gain).astype(jnp.bfloat16)
        if k == 0:
            squares = jnp.sum(values * values, axis=1, keepdims=True) / width
            squares = split_wide(jnp.broadcast_to(squares, (block_rows, LANES)))
            small_ref[pl.ds(begin, block_rows), LANES:] = squares.astype(jnp.bfloat16)
    slots, rows, rank_columns = factor_ref.shape
    total = jnp.zeros((rows, rank_columns), jnp.float32)
    for s in range(slots):
        projected = lax.dot_general(
            x_ref[...], down_ref[s], (((1,), (1,)), ((), ())), preferred_element_type=jnp.float32
        )
        factor = factor_ref[s]
        total = total + jnp.where(factor > 0, projected * factor, 0.0)
    small_ref[:, :rank_columns] = total.astype(small_ref.dtype)


def write_rows(acc, outs, n_y, n_z):
    z = lax.axis_index("gz")
    rows_here = outs[0].shape[0] // n_y
    for k in range(n_z):
        for y in range(n_y):
            owner = y * n_z + jnp.bitwise_xor(z, k)
            begin = pl.multiple_of(owner * rows_here, rows_here)
            outs[k][y * rows_here : (y + 1) * rows_here, :] = acc[
                pl.ds(begin, rows_here), :
            ].astype(outs[k].dtype)


def multiply(x_ref, weights, step, out, first):
    width = weights[0].shape[1]
    for c in range(0, width * len(weights), step):
        inner = c % width
        out[:, first + c : first + c + step] = jnp.dot(
            x_ref[...],
            weights[c // width][:, inner : inner + step],
            preferred_element_type=jnp.float32,
        )


def base_kernel(n_w, step, x_ref, *refs):
    multiply(x_ref, refs[:n_w], step, refs[n_w], 0)


def product_kernel(n_w, n_y, n_z, step, first, x_ref, *refs):
    if first:
        base_ref, refs = refs[0], refs[2:]
    weights, outs, acc = refs[:n_w], refs[n_w:-1], refs[-1]
    if first:
        acc[:, :first] = base_ref[...]
    multiply(x_ref, weights, step, acc, first)
    write_rows(acc, outs, n_y, n_z)


def chip_rows(parts, here):
    total = parts[0][here, :].astype(jnp.float32)
    for part in parts[1:]:
        total = total + part[here, :].astype(jnp.float32)
    return total


def pair_kernel(n_y, n_z, *refs):
    parts, smalls, outs = refs[:n_z], refs[n_z:-n_y], refs[-n_y:]
    rows_here = outs[0].shape[0]
    columns = parts[0].shape[1]
    y, z = lax.axis_index("gy"), lax.axis_index("gz")
    for k in range(n_y):
        other = jnp.bitwise_xor(y, k)
        here = pl.ds(pl.multiple_of(other * rows_here, rows_here), rows_here)
        outs[k][:, :columns] = chip_rows(parts, here).astype(outs[k].dtype)
        if smalls:
            owner = other * n_z + z
            here = pl.ds(pl.multiple_of(owner * rows_here, rows_here), rows_here)
            small = chip_rows(smalls, here)
            square = jnp.broadcast_to(join_wide(small[:, LANES:]), (rows_here, LANES))
            outs[k][:, columns : columns + LANES] = small[:, :LANES].astype(outs[k].dtype)
            outs[k][:, columns + LANES :] = split_wide(square).astype(outs[k].dtype)


def final_kernel(n, n_z, step, spread_ref, up_ref, *refs):
    firsts, lasts, out_ref = refs[:n], refs[n : 2 * n], refs[2 * n]
    rows_here, columns = out_ref.shape
    done = firsts[0].shape[1]
    late = columns - done
    adapters, rank_columns, _ = up_ref.shape

    def added(parts, begin, end):
        total = parts[0][:, begin:end]
        for part in parts[1:]:
            total = total + part[:, begin:end].astype(jnp.float32)
        return total

    side = added(lasts, late, late + 2 * LANES)
    mean_sq = join_wide(side[:, LANES:])
    scale = lax.rsqrt(mean_sq + EPSILON)
    owner = lax.axis_index("gy") * n_z + lax.axis_index("gz")
    live = spread_ref[pl.ds(pl.multiple_of(owner * rows_here, rows_here), rows_here), :]
    spread = jnp.concatenate([side[:, :rank_columns]] * adapters, axis=1)
    spread = jnp.where(live > 0, spread, 0.0).astype(jnp.bfloat16)
    for c in range(0, columns, step):
        if c < done:
            base = added(firsts, c, c + step)
        else:
            base = added(lasts, c - done, c - done + step)
        up = up_ref[:, :, c : c + step].reshape(adapters * rank_columns, step)
        total = base + jnp.dot(spread, up, preferred_element_type=jnp.float32)
        value = jnp.where(mean_sq < jnp.inf, total * scale, 0.0)
        out_ref[:, c : c + step] = value.astype(out_ref.dtype)


def body(
    hidden,
    attention_norm_gain,
    query_weight,
    slot_down_factors,
    adapter_up_factors,
    adapter_of_row,
    padded_adapter_rank,
    adapter_in_slot,
    segment_starts,
):
    n_x, n_y, n_z = lax.axis_size("gx"), lax.axis_size("gy"), lax.axis_size("gz")
    groups = n_y * n_z
    block_rows, depth = hidden.shape
    columns = query_weight.shape[1]
    rows = n_x * block_rows
    rows_here = rows // groups

    def send(value, axis, n, k):
        return lax.ppermute(value, axis, [(j, j ^ k) for j in range(n)])

    def spread_out(made, axis, n):
        return [made[0]] + [send(made[k], axis, n, k) for k in range(1, n)]

    sent = {0: hidden}
    order = [0, *range(2, n_x, 2), 1, *range(3, n_x, 2)]
    for k in order[1:]:
        sent[k] = send(sent[k - 1], "gx", n_x, 1) if k % 2 else send(hidden, "gx", n_x, k)
    blocks = [sent[k] for k in order]

    step = min(512, columns // 4)
    n_w, pieces = 4, 8
    f32, bf16 = jnp.float32, jnp.bfloat16
    slots, rank_columns = slot_down_factors.shape[0], slot_down_factors.shape[2]
    adapters = adapter_up_factors.shape[0]
    quarter = columns // n_w
    kept = n_y * rows_here
    roomy = params(4 + (rows * depth >> 16))

    scalars = (padded_adapter_rank, adapter_in_slot, segment_starts)
    early = n_w // 2
    load_cost = cost(300 * query_weight.size, query_weight.size)
    factor, spread, *weights = pl.pallas_call(
        functools.partial(first_load_kernel, early),
        out_shape=[
            jax.ShapeDtypeStruct((slots, rows, rank_columns), f32),
            jax.ShapeDtypeStruct((rows, adapters * rank_columns), f32),
        ]
        + [pltpu.VMEM((depth, quarter), query_weight.dtype)] * early,
        in_specs=[ANY] + [HBM] * 3,
        out_specs=[VMEM] * (2 + early),
        scratch_shapes=[
            pltpu.SemaphoreType.DMA((early, pieces)),
            pltpu.SemaphoreType.DMA((len(scalars),)),
            *[pltpu.SMEM(value.shape, value.dtype) for value in scalars],
        ],
        cost_estimate=load_cost,
        compiler_params=roomy,
        name="first_load",
    )(query_weight, *[pltpu.with_memory_space_constraint(v, pltpu.HBM) for v in scalars])
    weights += pl.pallas_call(
        functools.partial(last_load_kernel, n_w - early, early * quarter),
        out_shape=[pltpu.VMEM((depth, quarter), query_weight.dtype)] * (n_w - early),
        in_specs=[ANY] * 3,
        out_specs=[VMEM] * (n_w - early),
        scratch_shapes=[pltpu.SemaphoreType.DMA((n_w - early, pieces))],
        cost_estimate=load_cost,
        compiler_params=roomy,
        name="last_load",
    )(query_weight, factor, blocks[1])
    weights = [pltpu.with_memory_space_constraint(w, pltpu.VMEM) for w in weights]

    x, small = pl.pallas_call(
        functools.partial(rows_kernel, order, depth * groups),
        out_shape=(
            jax.ShapeDtypeStruct((rows, depth), bf16),
            jax.ShapeDtypeStruct((rows, 2 * LANES), bf16),
        ),
        in_specs=[VMEM] * (3 + n_x),
        out_specs=(VMEM,) * 2,
        compiler_params=roomy,
        name="scaled_rows",
    )(attention_norm_gain, jnp.swapaxes(slot_down_factors, 1, 2), factor, *blocks)

    one_hop = small = small + send(small, "gx", n_x, 1)
    hop = 2
    while hop < n_x:
        small = small + send(small, "gx", n_x, hop)
        hop *= 2

    def shapes(n, shape):
        return [jax.ShapeDtypeStruct(shape, f32 if k == 0 else bf16) for k in range(n)]

    base_columns = early * quarter
    base = pl.pallas_call(
        functools.partial(base_kernel, early, step),
        out_shape=jax.ShapeDtypeStruct((rows, base_columns), f32),
        in_specs=[VMEM] * (1 + early),
        out_specs=VMEM,
        cost_estimate=cost(2 * rows * depth * base_columns, 2 * depth * base_columns),
        compiler_params=roomy,
        name="first_columns",
    )(x, *weights[:early])

    def product(some, bases, times, name):
        first = sum(part.shape[1] for part in bases[:1])
        wide = first + len(some) * quarter
        made = pl.pallas_call(
            functools.partial(product_kernel, len(some), n_y, n_z, step, first),
            out_shape=shapes(n_z, (kept, wide)),
            in_specs=[VMEM] * (1 + len(bases) + len(some)),
            out_specs=[VMEM] * n_z,
            scratch_shapes=[pltpu.VMEM((rows, wide), f32)],
            cost_estimate=cost(2 * rows * depth * wide * times, 2 * depth * wide),
            compiler_params=roomy,
            name=name,
        )(x, *bases, *some)
        return spread_out(made, "gz", n_z)

    firsts = product(weights[early:-1], [base, one_hop], 4, "middle_columns")
    lasts = product(weights[-1:], [], 8, "last_columns")
    smalls = spread_out([small] * n_z, "gz", n_z)

    def chip_sums(parts, sides, name):
        wide = parts[0].shape[1] + (2 * LANES if sides else 0)
        made = pl.pallas_call(
            functools.partial(pair_kernel, n_y, n_z),
            out_shape=shapes(n_y, (rows_here, wide)),
            in_specs=[VMEM] * (n_z + len(sides)),
            out_specs=[VMEM] * n_y,
            cost_estimate=cost(2 * rows * depth * quarter, 2 * depth * quarter),
            compiler_params=roomy,
            name=name,
        )(*parts, *sides)
        return spread_out(made, "gy", n_y)

    first_parts = chip_sums(firsts, [], "first_sums")
    last_parts = chip_sums(lasts, smalls, "last_sums")

    return pl.pallas_call(
        functools.partial(final_kernel, n_y, n_z, step),
        out_shape=jax.ShapeDtypeStruct((rows_here, columns), bf16),
        in_specs=[VMEM] * (2 + 2 * n_y),
        out_specs=VMEM,
        compiler_params=roomy,
        name="query_rows",
    )(spread, adapter_up_factors, *first_parts, *last_parts)


def solution(mesh):
    return jax.shard_map(
        body,
        mesh=mesh,
        in_specs=(
            P(("rep", "gx"), ("gy", "gz")),
            P(("gy", "gz")),
            P(("gy", "gz"), "gx"),
            P("gx", ("gy", "gz"), None),
            P(None, None, "gx"),
            P("rep"),
            P(),
            P(),
            P("rep"),
        ),
        out_specs=P(("rep", "gy", "gz"), "gx"),
        check_vma=False,
    )
```

```python
import functools

import jax
import jax.numpy as jnp
from jax import lax
from jax.experimental import pallas as pl
from jax.experimental.pallas import tpu as pltpu
from jax.sharding import PartitionSpec as P

EPSILON = 1e-05
ADAPTER_ALPHA = 32.0
LANES = 128
MIB = 1 << 20

VMEM = pl.BlockSpec(memory_space=pltpu.VMEM)
HBM = pl.BlockSpec(memory_space=pltpu.HBM)
ANY = pl.BlockSpec(memory_space=pl.ANY)


def params(mib):
    return pltpu.CompilerParams(vmem_limit_bytes=mib * MIB)


def cost(flops, moved):
    return pl.CostEstimate(flops=flops, bytes_accessed=moved, transcendentals=0)


def weight_copies(w_hbm, first, w_vmem, sems):
    pieces = sems.shape[0]
    depth, width = w_vmem.shape
    step = depth // pieces
    return [
        pltpu.make_async_copy(
            w_hbm.at[pl.ds(p * step, step), pl.ds(first, width)],
            w_vmem.at[pl.ds(p * step, step)],
            sems.at[p],
        )
        for p in range(pieces)
    ]


def load(w_hbm, first, weights, sems, meanwhile):
    copies = []
    for j, w_vmem in enumerate(weights):
        copies += weight_copies(w_hbm, first, w_vmem, sems.at[j])
        first += w_vmem.shape[1]
    for copy in copies:
        copy.start()
    meanwhile()
    for copy in copies:
        copy.wait()


def first_load_kernel(n, w_hbm, rank_hbm, slot_hbm, start_hbm, factor_ref, spread_ref, *refs):
    weights, sems, scalar_sems = refs[:n], refs[n], refs[n + 1]
    rank_ref, slot_ref, start_ref = refs[n + 2 :]

    def masks():
        pairs = ((rank_hbm, rank_ref), (slot_hbm, slot_ref), (start_hbm, start_ref))
        scalars = [
            pltpu.make_async_copy(source, target, scalar_sems.at[j])
            for j, (source, target) in enumerate(pairs)
        ]
        for copy in scalars:
            copy.start()
        for copy in scalars:
            copy.wait()
        slots, rows, rank_columns = factor_ref.shape
        home = lax.axis_index("gx")
        row = lax.broadcasted_iota(jnp.int32, (rows, rank_columns), 0)
        col = lax.broadcasted_iota(jnp.int32, (rows, rank_columns), 1)
        for s in range(slots):
            adapter = slot_ref[home * slots + s]
            rank = rank_ref[adapter]
            live = (row >= start_ref[adapter]) & (row < start_ref[adapter + 1]) & (col < rank)
            ranks = jnp.full((rows, rank_columns), rank, jnp.int32).astype(jnp.float32)
            factor_ref[s] = jnp.where(live, ADAPTER_ALPHA / ranks, 0.0)
        adapters = spread_ref.shape[1] // rank_columns
        for a in range(adapters):
            live = (row >= start_ref[a]) & (row < start_ref[a + 1])
            spread_ref[:, a * rank_columns : (a + 1) * rank_columns] = jnp.where(live, 1.0, 0.0)

    load(w_hbm, 0, weights, sems, masks)


def last_load_kernel(n, first, w_hbm, _, __, *refs):
    load(w_hbm, first, refs[:n], refs[n], lambda: None)


def split_wide(value):
    high = value.astype(jnp.bfloat16).astype(jnp.float32)
    low = jnp.where(high < jnp.inf, value - high, 0.0)
    lane = lax.broadcasted_iota(jnp.int32, value.shape, 1)
    return jnp.where(lane < LANES // 2, high, low)


def join_wide(value):
    return value[:, :1] + value[:, LANES - 1 :]


def rows_kernel(order, width, gain_ref, down_ref, factor_ref, *refs):
    n = len(order)
    blocks = refs[:n]
    x_ref, small_ref = refs[n:]
    home = lax.axis_index("gx")
    block_rows = blocks[0].shape[0]
    gain = gain_ref[...].astype(jnp.float32).reshape(1, gain_ref.shape[0])
    small_ref[...] = jnp.zeros(small_ref.shape, small_ref.dtype)
    for k, block in zip(order, blocks):
        begin = pl.multiple_of(jnp.bitwise_xor(home, k) * block_rows, block_rows)
        values = block[...].astype(jnp.float32)
        x_ref[pl.ds(begin, block_rows), :] = (values * gain).astype(jnp.bfloat16)
        if k == 0:
            squares = jnp.sum(values * values, axis=1, keepdims=True) / width
            squares = split_wide(jnp.broadcast_to(squares, (block_rows, LANES)))
            small_ref[pl.ds(begin, block_rows), LANES:] = squares.astype(jnp.bfloat16)
    slots, rows, rank_columns = factor_ref.shape
    total = jnp.zeros((rows, rank_columns), jnp.float32)
    for s in range(slots):
        projected = lax.dot_general(
            x_ref[...], down_ref[s], (((1,), (1,)), ((), ())), preferred_element_type=jnp.float32
        )
        factor = factor_ref[s]
        total = total + jnp.where(factor > 0, projected * factor, 0.0)
    small_ref[:, :rank_columns] = total.astype(small_ref.dtype)


def write_rows(acc, outs, n_y, n_z):
    z = lax.axis_index("gz")
    rows_here = outs[0].shape[0] // n_y
    for k in range(n_z):
        for y in range(n_y):
            owner = y * n_z + jnp.bitwise_xor(z, k)
            begin = pl.multiple_of(owner * rows_here, rows_here)
            outs[k][y * rows_here : (y + 1) * rows_here, :] = acc[
                pl.ds(begin, rows_here), :
            ].astype(outs[k].dtype)


def multiply(x_ref, weights, step, out, first):
    for weight in weights:
        width = weight.shape[1]
        for c in range(0, width, step):
            out[:, first + c : first + c + step] = jnp.dot(
                x_ref[...], weight[:, c : c + step], preferred_element_type=jnp.float32
            )
        first += width


def base_kernel(n_w, step, x_ref, *refs):
    multiply(x_ref, refs[:n_w], step, refs[n_w], 0)


def product_kernel(n_w, n_y, n_z, step, first, x_ref, *refs):
    if first:
        base_ref, refs = refs[0], refs[2:]
    weights, outs, acc = refs[:n_w], refs[n_w:-1], refs[-1]
    if first:
        acc[:, :first] = base_ref[...]
    multiply(x_ref, weights, step, acc, first)
    write_rows(acc, outs, n_y, n_z)


def chip_rows(parts, here):
    total = parts[0][here, :].astype(jnp.float32)
    for part in parts[1:]:
        total = total + part[here, :].astype(jnp.float32)
    return total


def pair_kernel(n_y, n_z, *refs):
    parts, smalls, outs = refs[:n_z], refs[n_z:-n_y], refs[-n_y:]
    rows_here = outs[0].shape[0]
    columns = parts[0].shape[1]
    y, z = lax.axis_index("gy"), lax.axis_index("gz")
    for k in range(n_y):
        other = jnp.bitwise_xor(y, k)
        here = pl.ds(pl.multiple_of(other * rows_here, rows_here), rows_here)
        outs[k][:, :columns] = chip_rows(parts, here).astype(outs[k].dtype)
        if smalls:
            owner = other * n_z + z
            here = pl.ds(pl.multiple_of(owner * rows_here, rows_here), rows_here)
            small = chip_rows(smalls, here)
            square = jnp.broadcast_to(join_wide(small[:, LANES:]), (rows_here, LANES))
            outs[k][:, columns : columns + LANES] = small[:, :LANES].astype(outs[k].dtype)
            outs[k][:, columns + LANES :] = split_wide(square).astype(outs[k].dtype)


def final_kernel(n, n_z, step, spread_ref, up_ref, *refs):
    firsts, lasts, out_ref = refs[:n], refs[n : 2 * n], refs[2 * n]
    rows_here, columns = out_ref.shape
    done = firsts[0].shape[1]
    late = columns - done
    adapters, rank_columns, _ = up_ref.shape

    def added(parts, begin, end):
        total = parts[0][:, begin:end]
        for part in parts[1:]:
            total = total + part[:, begin:end].astype(jnp.float32)
        return total

    side = added(lasts, late, late + 2 * LANES)
    mean_sq = join_wide(side[:, LANES:])
    scale = lax.rsqrt(mean_sq + EPSILON)
    owner = lax.axis_index("gy") * n_z + lax.axis_index("gz")
    live = spread_ref[pl.ds(pl.multiple_of(owner * rows_here, rows_here), rows_here), :]
    spread = jnp.concatenate([side[:, :rank_columns]] * adapters, axis=1)
    spread = jnp.where(live > 0, spread, 0.0).astype(jnp.bfloat16)
    for c in range(0, columns, step):
        if c < done:
            base = added(firsts, c, c + step)
        else:
            base = added(lasts, c - done, c - done + step)
        up = up_ref[:, :, c : c + step].reshape(adapters * rank_columns, step)
        total = base + jnp.dot(spread, up, preferred_element_type=jnp.float32)
        value = jnp.where(mean_sq < jnp.inf, total * scale, 0.0)
        out_ref[:, c : c + step] = value.astype(out_ref.dtype)


def body(
    hidden,
    attention_norm_gain,
    query_weight,
    slot_down_factors,
    adapter_up_factors,
    adapter_of_row,
    padded_adapter_rank,
    adapter_in_slot,
    segment_starts,
):
    n_x, n_y, n_z = lax.axis_size("gx"), lax.axis_size("gy"), lax.axis_size("gz")
    groups = n_y * n_z
    block_rows, depth = hidden.shape
    columns = query_weight.shape[1]
    rows = n_x * block_rows
    rows_here = rows // groups

    def send(value, axis, n, k):
        return lax.ppermute(value, axis, [(j, j ^ k) for j in range(n)])

    def spread_out(made, axis, n):
        return [made[0]] + [send(made[k], axis, n, k) for k in range(1, n)]

    sent = {0: hidden}
    order = [0, *range(2, n_x, 2), 1, *range(3, n_x, 2)]
    for k in order[1:]:
        sent[k] = send(sent[k - 1], "gx", n_x, 1) if k % 2 else send(hidden, "gx", n_x, k)
    blocks = [sent[k] for k in order]

    step = min(512, columns // 8 if columns >= 8 * LANES else columns // 4)
    pieces = 8
    f32, bf16 = jnp.float32, jnp.bfloat16
    slots, rank_columns = slot_down_factors.shape[0], slot_down_factors.shape[2]
    adapters = adapter_up_factors.shape[0]
    quarter = columns // 4
    if quarter % (2 * LANES) == 0:
        loads = [quarter, quarter, quarter // 2], [quarter // 2, quarter]
    else:
        loads = [quarter, quarter], [quarter, quarter]
    kept = n_y * rows_here
    roomy = params(4 + (rows * depth >> 16))

    scalars = (padded_adapter_rank, adapter_in_slot, segment_starts)
    weight_hbm = pltpu.with_memory_space_constraint(query_weight, pltpu.HBM)
    load_cost = cost(300 * query_weight.size, query_weight.size)
    factor, spread, *weights = pl.pallas_call(
        functools.partial(first_load_kernel, len(loads[0])),
        out_shape=[
            jax.ShapeDtypeStruct((slots, rows, rank_columns), f32),
            jax.ShapeDtypeStruct((rows, adapters * rank_columns), f32),
        ]
        + [pltpu.VMEM((depth, wide), query_weight.dtype) for wide in loads[0]],
        in_specs=[HBM] * 4,
        out_specs=[VMEM] * (2 + len(loads[0])),
        scratch_shapes=[
            pltpu.SemaphoreType.DMA((len(loads[0]), pieces)),
            pltpu.SemaphoreType.DMA((len(scalars),)),
            *[pltpu.SMEM(value.shape, value.dtype) for value in scalars],
        ],
        cost_estimate=load_cost,
        compiler_params=roomy,
        name="first_load",
    )(weight_hbm, *[pltpu.with_memory_space_constraint(v, pltpu.HBM) for v in scalars])
    weights += pl.pallas_call(
        functools.partial(last_load_kernel, len(loads[1]), sum(loads[0])),
        out_shape=[pltpu.VMEM((depth, wide), query_weight.dtype) for wide in loads[1]],
        in_specs=[HBM, ANY, ANY],
        out_specs=[VMEM] * len(loads[1]),
        scratch_shapes=[pltpu.SemaphoreType.DMA((len(loads[1]), pieces))],
        cost_estimate=load_cost,
        compiler_params=roomy,
        name="last_load",
    )(weight_hbm, factor, blocks[1])
    weights = [pltpu.with_memory_space_constraint(w, pltpu.VMEM) for w in weights]

    x, small = pl.pallas_call(
        functools.partial(rows_kernel, order, depth * groups),
        out_shape=(
            jax.ShapeDtypeStruct((rows, depth), bf16),
            jax.ShapeDtypeStruct((rows, 2 * LANES), bf16),
        ),
        in_specs=[VMEM] * (3 + n_x),
        out_specs=(VMEM,) * 2,
        compiler_params=roomy,
        name="scaled_rows",
    )(attention_norm_gain, jnp.swapaxes(slot_down_factors, 1, 2), factor, *blocks)

    one_hop = small = small + send(small, "gx", n_x, 1)
    hop = 2
    while hop < n_x:
        small = small + send(small, "gx", n_x, hop)
        hop *= 2

    def shapes(n, shape):
        return [jax.ShapeDtypeStruct(shape, f32 if k == 0 else bf16) for k in range(n)]

    base_columns = 2 * quarter
    base = pl.pallas_call(
        functools.partial(base_kernel, 2, step),
        out_shape=jax.ShapeDtypeStruct((rows, base_columns), f32),
        in_specs=[VMEM] * 3,
        out_specs=VMEM,
        cost_estimate=cost(2 * rows * depth * base_columns, 2 * depth * base_columns),
        compiler_params=roomy,
        name="first_columns",
    )(x, *weights[:2])

    def product(some, bases, times, name):
        first = sum(part.shape[1] for part in bases[:1])
        wide = first + quarter
        made = pl.pallas_call(
            functools.partial(product_kernel, len(some), n_y, n_z, step, first),
            out_shape=shapes(n_z, (kept, wide)),
            in_specs=[VMEM] * (1 + len(bases) + len(some)),
            out_specs=[VMEM] * n_z,
            scratch_shapes=[pltpu.VMEM((rows, wide), f32)],
            cost_estimate=cost(2 * rows * depth * wide * times, 2 * depth * wide),
            compiler_params=roomy,
            name=name,
        )(x, *bases, *some)
        return spread_out(made, "gz", n_z)

    firsts = product(weights[2:-1], [base, one_hop], 4, "middle_columns")
    lasts = product(weights[-1:], [], 8, "last_columns")
    smalls = spread_out([small] * n_z, "gz", n_z)

    def chip_sums(parts, sides, name):
        wide = parts[0].shape[1] + (2 * LANES if sides else 0)
        made = pl.pallas_call(
            functools.partial(pair_kernel, n_y, n_z),
            out_shape=shapes(n_y, (rows_here, wide)),
            in_specs=[VMEM] * (n_z + len(sides)),
            out_specs=[VMEM] * n_y,
            cost_estimate=cost(2 * rows * depth * quarter, 2 * depth * quarter),
            compiler_params=roomy,
            name=name,
        )(*parts, *sides)
        return spread_out(made, "gy", n_y)

    first_parts = chip_sums(firsts, [], "first_sums")
    last_parts = chip_sums(lasts, smalls, "last_sums")

    return pl.pallas_call(
        functools.partial(final_kernel, n_y, n_z, step),
        out_shape=jax.ShapeDtypeStruct((rows_here, columns), bf16),
        in_specs=[VMEM] * (2 + 2 * n_y),
        out_specs=VMEM,
        compiler_params=roomy,
        name="query_rows",
    )(spread, adapter_up_factors, *first_parts, *last_parts)


def solution(mesh):
    return jax.shard_map(
        body,
        mesh=mesh,
        in_specs=(
            P(("rep", "gx"), ("gy", "gz")),
            P(("gy", "gz")),
            P(("gy", "gz"), "gx"),
            P("gx", ("gy", "gz"), None),
            P(None, None, "gx"),
            P("rep"),
            P(),
            P(),
            P("rep"),
        ),
        out_specs=P(("rep", "gy", "gz"), "gx"),
        check_vma=False,
    )
```

```python
import functools

import jax
import jax.numpy as jnp
from jax import lax
from jax.experimental import pallas as pl
from jax.experimental.pallas import tpu as pltpu
from jax.sharding import PartitionSpec as P

EPSILON = 1e-05
ADAPTER_ALPHA = 32.0
LANES = 128
MIB = 1 << 20

VMEM = pl.BlockSpec(memory_space=pltpu.VMEM)
HBM = pl.BlockSpec(memory_space=pltpu.HBM)
ANY = pl.BlockSpec(memory_space=pl.ANY)


def params(mib):
    return pltpu.CompilerParams(vmem_limit_bytes=mib * MIB)


def cost(flops, moved):
    return pl.CostEstimate(flops=flops, bytes_accessed=moved, transcendentals=0)


def weight_copies(w_hbm, first, w_vmem, sems):
    pieces = sems.shape[0]
    depth, width = w_vmem.shape
    step = depth // pieces
    return [
        pltpu.make_async_copy(
            w_hbm.at[pl.ds(p * step, step), pl.ds(first, width)],
            w_vmem.at[pl.ds(p * step, step)],
            sems.at[p],
        )
        for p in range(pieces)
    ]


def fetch_kernel(n, w_hbm, rank_hbm, slot_hbm, start_hbm, factor_ref, spread_ref, *refs):
    weights, sems, scalar_sems = refs[:n], refs[n], refs[n + 1]
    rank_ref, slot_ref, start_ref = refs[n + 2 :]
    scalars = [
        pltpu.make_async_copy(source, target, scalar_sems.at[j])
        for j, (source, target) in enumerate(
            ((rank_hbm, rank_ref), (slot_hbm, slot_ref), (start_hbm, start_ref))
        )
    ]
    for copy in scalars:
        copy.start()
    copies = []
    first = 0
    for j, w_vmem in enumerate(weights):
        copies += weight_copies(w_hbm, first, w_vmem, sems.at[j])
        first += w_vmem.shape[1]
    for copy in copies:
        copy.start()
    for copy in scalars:
        copy.wait()
    slots, rows, rank_columns = factor_ref.shape
    home = lax.axis_index("gx")
    row = lax.broadcasted_iota(jnp.int32, (rows, rank_columns), 0)
    col = lax.broadcasted_iota(jnp.int32, (rows, rank_columns), 1)
    for s in range(slots):
        adapter = slot_ref[home * slots + s]
        rank = rank_ref[adapter]
        live = (row >= start_ref[adapter]) & (row < start_ref[adapter + 1]) & (col < rank)
        scale = ADAPTER_ALPHA / jnp.full((rows, rank_columns), rank, jnp.int32).astype(jnp.float32)
        factor_ref[s] = jnp.where(live, scale, 0.0)
    adapters = spread_ref.shape[1] // rank_columns
    for a in range(adapters):
        live = (row >= start_ref[a]) & (row < start_ref[a + 1])
        spread_ref[:, a * rank_columns : (a + 1) * rank_columns] = jnp.where(live, 1.0, 0.0)
    for copy in copies:
        copy.wait()


def split_wide(value):
    high = value.astype(jnp.bfloat16).astype(jnp.float32)
    low = jnp.where(high < jnp.inf, value - high, 0.0)
    lane = lax.broadcasted_iota(jnp.int32, value.shape, 1)
    return jnp.where(lane < LANES // 2, high, low)


def join_wide(value):
    return value[:, :1] + value[:, LANES - 1 :]


def rows_kernel(order, width, gain_ref, down_ref, factor_ref, *refs):
    n = len(order)
    blocks = refs[:n]
    x_ref, small_ref = refs[n:]
    home = lax.axis_index("gx")
    block_rows = blocks[0].shape[0]
    gain = gain_ref[...].astype(jnp.float32).reshape(1, gain_ref.shape[0])
    small_ref[...] = jnp.zeros(small_ref.shape, small_ref.dtype)
    for k, block in zip(order, blocks):
        begin = pl.multiple_of(jnp.bitwise_xor(home, k) * block_rows, block_rows)
        values = block[...].astype(jnp.float32)
        x_ref[pl.ds(begin, block_rows), :] = (values * gain).astype(jnp.bfloat16)
        if k == 0:
            squares = jnp.sum(values * values, axis=1, keepdims=True) / width
            squares = split_wide(jnp.broadcast_to(squares, (block_rows, LANES)))
            small_ref[pl.ds(begin, block_rows), LANES:] = squares.astype(jnp.bfloat16)
    slots, rows, rank_columns = factor_ref.shape
    total = jnp.zeros((rows, rank_columns), jnp.float32)
    for s in range(slots):
        projected = lax.dot_general(
            x_ref[...], down_ref[s], (((1,), (1,)), ((), ())), preferred_element_type=jnp.float32
        )
        factor = factor_ref[s]
        total = total + jnp.where(factor > 0, projected * factor, 0.0)
    small_ref[:, :rank_columns] = total.astype(small_ref.dtype)


def write_rows(acc, outs, n_y, n_z):
    z = lax.axis_index("gz")
    rows_here = outs[0].shape[0] // n_y
    for k in range(n_z):
        for y in range(n_y):
            owner = y * n_z + jnp.bitwise_xor(z, k)
            begin = pl.multiple_of(owner * rows_here, rows_here)
            outs[k][y * rows_here : (y + 1) * rows_here, :] = acc[
                pl.ds(begin, rows_here), :
            ].astype(outs[k].dtype)


def multiply(x_ref, weights, step, out, first):
    for weight in weights:
        width = weight.shape[1]
        for c in range(0, width, step):
            out[:, first + c : first + c + step] = jnp.dot(
                x_ref[...], weight[:, c : c + step], preferred_element_type=jnp.float32
            )
        first += width


def base_kernel(n_w, first, step, w_hbm, x_ref, *refs):
    weights, out_ref, rest = refs[:n_w], refs[n_w], refs[n_w + 1 :]
    copies = weight_copies(w_hbm, first, *rest) if rest else []
    for copy in copies:
        copy.start()
    multiply(x_ref, weights, step, out_ref, 0)
    for copy in copies:
        copy.wait()


def product_kernel(n_w, n_y, n_z, step, first, x_ref, *refs):
    if first:
        base_ref, refs = refs[0], refs[2:]
    weights, outs, acc = refs[:n_w], refs[n_w:-1], refs[-1]
    if first:
        acc[:, :first] = base_ref[...]
    multiply(x_ref, weights, step, acc, first)
    write_rows(acc, outs, n_y, n_z)


def chip_rows(parts, here):
    total = parts[0][here, :].astype(jnp.float32)
    for part in parts[1:]:
        total = total + part[here, :].astype(jnp.float32)
    return total


def pair_kernel(n_y, n_z, *refs):
    parts, smalls, outs = refs[:n_z], refs[n_z:-n_y], refs[-n_y:]
    rows_here = outs[0].shape[0]
    columns = parts[0].shape[1]
    y, z = lax.axis_index("gy"), lax.axis_index("gz")
    for k in range(n_y):
        other = jnp.bitwise_xor(y, k)
        here = pl.ds(pl.multiple_of(other * rows_here, rows_here), rows_here)
        outs[k][:, :columns] = chip_rows(parts, here).astype(outs[k].dtype)
        if smalls:
            owner = other * n_z + z
            here = pl.ds(pl.multiple_of(owner * rows_here, rows_here), rows_here)
            small = chip_rows(smalls, here)
            square = jnp.broadcast_to(join_wide(small[:, LANES:]), (rows_here, LANES))
            outs[k][:, columns : columns + LANES] = small[:, :LANES].astype(outs[k].dtype)
            outs[k][:, columns + LANES :] = split_wide(square).astype(outs[k].dtype)


def final_kernel(n, n_z, step, spread_ref, up_ref, *refs):
    firsts, lasts, out_ref = refs[:n], refs[n : 2 * n], refs[2 * n]
    rows_here, columns = out_ref.shape
    done = firsts[0].shape[1]
    late = columns - done
    adapters, rank_columns, _ = up_ref.shape

    def added(parts, begin, end):
        total = parts[0][:, begin:end]
        for part in parts[1:]:
            total = total + part[:, begin:end].astype(jnp.float32)
        return total

    side = added(lasts, late, late + 2 * LANES)
    mean_sq = join_wide(side[:, LANES:])
    scale = lax.rsqrt(mean_sq + EPSILON)
    owner = lax.axis_index("gy") * n_z + lax.axis_index("gz")
    live = spread_ref[pl.ds(pl.multiple_of(owner * rows_here, rows_here), rows_here), :]
    spread = jnp.concatenate([side[:, :rank_columns]] * adapters, axis=1)
    spread = jnp.where(live > 0, spread, 0.0).astype(jnp.bfloat16)
    for c in range(0, columns, step):
        if c < done:
            base = added(firsts, c, c + step)
        else:
            base = added(lasts, c - done, c - done + step)
        up = up_ref[:, :, c : c + step].reshape(adapters * rank_columns, step)
        total = base + jnp.dot(spread, up, preferred_element_type=jnp.float32)
        value = jnp.where(mean_sq < jnp.inf, total * scale, 0.0)
        out_ref[:, c : c + step] = value.astype(out_ref.dtype)


def body(
    hidden,
    attention_norm_gain,
    query_weight,
    slot_down_factors,
    adapter_up_factors,
    adapter_of_row,
    padded_adapter_rank,
    adapter_in_slot,
    segment_starts,
):
    n_x, n_y, n_z = lax.axis_size("gx"), lax.axis_size("gy"), lax.axis_size("gz")
    groups = n_y * n_z
    block_rows, depth = hidden.shape
    columns = query_weight.shape[1]
    rows = n_x * block_rows
    rows_here = rows // groups

    def send(value, axis, n, k):
        return lax.ppermute(value, axis, [(j, j ^ k) for j in range(n)])

    def spread_out(made, axis, n):
        return [made[0]] + [send(made[k], axis, n, k) for k in range(1, n)]

    order = [0, *range(n_x - 1, 0, -1)]
    blocks = [hidden] + [send(hidden, "gx", n_x, k) for k in order[1:]]

    step = min(512, columns // 4)
    pieces = 8
    f32, bf16 = jnp.float32, jnp.bfloat16
    slots, rank_columns = slot_down_factors.shape[0], slot_down_factors.shape[2]
    adapters = adapter_up_factors.shape[0]
    quarter = columns // 4
    late = quarter // 2 if quarter % (2 * LANES) == 0 else 0
    loads = [quarter] * 3 + [quarter - late]
    weight_hbm = pltpu.with_memory_space_constraint(query_weight, pltpu.HBM)
    kept = n_y * rows_here
    roomy = params(4 + (rows * depth >> 16))

    scalars = (padded_adapter_rank, adapter_in_slot, segment_starts)
    factor, spread, *weights = pl.pallas_call(
        functools.partial(fetch_kernel, len(loads)),
        out_shape=[
            jax.ShapeDtypeStruct((slots, rows, rank_columns), f32),
            jax.ShapeDtypeStruct((rows, adapters * rank_columns), f32),
        ]
        + [pltpu.VMEM((depth, wide), query_weight.dtype) for wide in loads],
        in_specs=[HBM] * 4,
        out_specs=[VMEM] * (2 + len(loads)),
        scratch_shapes=[
            pltpu.SemaphoreType.DMA((len(loads), pieces)),
            pltpu.SemaphoreType.DMA((len(scalars),)),
            *[pltpu.SMEM(value.shape, value.dtype) for value in scalars],
        ],
        cost_estimate=cost(0, 2 * query_weight.size),
        compiler_params=roomy,
        name="fetch_weight",
    )(weight_hbm, *[pltpu.with_memory_space_constraint(v, pltpu.HBM) for v in scalars])
    weights = [pltpu.with_memory_space_constraint(w, pltpu.VMEM) for w in weights]

    x, small = pl.pallas_call(
        functools.partial(rows_kernel, order, depth * groups),
        out_shape=(
            jax.ShapeDtypeStruct((rows, depth), bf16),
            jax.ShapeDtypeStruct((rows, 2 * LANES), bf16),
        ),
        in_specs=[VMEM] * (3 + n_x),
        out_specs=(VMEM,) * 2,
        compiler_params=roomy,
        name="scaled_rows",
    )(attention_norm_gain, jnp.swapaxes(slot_down_factors, 1, 2), factor, *blocks)

    one_hop = small = small + send(small, "gx", n_x, 1)
    hop = 2
    while hop < n_x:
        small = small + send(small, "gx", n_x, hop)
        hop *= 2

    def shapes(n, shape):
        return [jax.ShapeDtypeStruct(shape, f32 if k == 0 else bf16) for k in range(n)]

    base, *rest = pl.pallas_call(
        functools.partial(base_kernel, 2, columns - late, step),
        out_shape=[jax.ShapeDtypeStruct((rows, 2 * quarter), f32)]
        + ([pltpu.VMEM((depth, late), query_weight.dtype)] if late else []),
        in_specs=[HBM] + [VMEM] * 3,
        out_specs=[VMEM] * (2 if late else 1),
        scratch_shapes=[pltpu.SemaphoreType.DMA((pieces,))] if late else [],
        cost_estimate=cost(4 * rows * depth * quarter, 4 * depth * quarter),
        compiler_params=roomy,
        name="first_columns",
    )(weight_hbm, x, *weights[:2])
    weights += [pltpu.with_memory_space_constraint(w, pltpu.VMEM) for w in rest]

    def product(some, bases, times, name):
        first = sum(part.shape[1] for part in bases[:1])
        wide = first + quarter
        made = pl.pallas_call(
            functools.partial(product_kernel, len(some), n_y, n_z, step, first),
            out_shape=shapes(n_z, (kept, wide)),
            in_specs=[VMEM] * (1 + len(bases) + len(some)),
            out_specs=[VMEM] * n_z,
            scratch_shapes=[pltpu.VMEM((rows, wide), f32)],
            cost_estimate=cost(2 * rows * depth * wide * times, 2 * depth * wide),
            compiler_params=roomy,
            name=name,
        )(x, *bases, *some)
        return spread_out(made, "gz", n_z)

    firsts = product(weights[2:3], [base, one_hop], 4, "middle_columns")
    lasts = product(weights[3:], [], 8, "last_columns")
    smalls = spread_out([small] * n_z, "gz", n_z)

    def chip_sums(parts, sides, name):
        wide = parts[0].shape[1] + (2 * LANES if sides else 0)
        made = pl.pallas_call(
            functools.partial(pair_kernel, n_y, n_z),
            out_shape=shapes(n_y, (rows_here, wide)),
            in_specs=[VMEM] * (n_z + len(sides)),
            out_specs=[VMEM] * n_y,
            cost_estimate=cost(2 * rows * depth * quarter, 2 * depth * quarter),
            compiler_params=roomy,
            name=name,
        )(*parts, *sides)
        return spread_out(made, "gy", n_y)

    first_parts = chip_sums(firsts, [], "first_sums")
    last_parts = chip_sums(lasts, smalls, "last_sums")

    return pl.pallas_call(
        functools.partial(final_kernel, n_y, n_z, step),
        out_shape=jax.ShapeDtypeStruct((rows_here, columns), bf16),
        in_specs=[VMEM] * (2 + 2 * n_y),
        out_specs=VMEM,
        compiler_params=roomy,
        name="query_rows",
    )(spread, adapter_up_factors, *first_parts, *last_parts)


def solution(mesh):
    return jax.shard_map(
        body,
        mesh=mesh,
        in_specs=(
            P(("rep", "gx"), ("gy", "gz")),
            P(("gy", "gz")),
            P(("gy", "gz"), "gx"),
            P("gx", ("gy", "gz"), None),
            P(None, None, "gx"),
            P("rep"),
            P(),
            P(),
            P("rep"),
        ),
        out_specs=P(("rep", "gy", "gz"), "gx"),
        check_vma=False,
    )
```

```python
import functools

import jax
import jax.numpy as jnp
from jax import lax
from jax.experimental import pallas as pl
from jax.experimental.pallas import tpu as pltpu
from jax.sharding import PartitionSpec as P

EPSILON = 1e-05
ADAPTER_ALPHA = 32.0
LANES = 128
MIB = 1 << 20

VMEM = pl.BlockSpec(memory_space=pltpu.VMEM)
HBM = pl.BlockSpec(memory_space=pltpu.HBM)
ANY = pl.BlockSpec(memory_space=pl.ANY)


def params(mib):
    return pltpu.CompilerParams(vmem_limit_bytes=mib * MIB)


def cost(flops, moved):
    return pl.CostEstimate(flops=flops, bytes_accessed=moved, transcendentals=0)


def weight_copies(w_hbm, first, w_vmem, sems):
    pieces = sems.shape[0]
    depth, width = w_vmem.shape
    step = depth // pieces
    return [
        pltpu.make_async_copy(
            w_hbm.at[pl.ds(p * step, step), pl.ds(first, width)],
            w_vmem.at[pl.ds(p * step, step)],
            sems.at[p],
        )
        for p in range(pieces)
    ]


def fetch_kernel(n, w_hbm, rank_hbm, slot_hbm, start_hbm, factor_ref, spread_ref, *refs):
    weights, sems, scalar_sems = refs[:n], refs[n], refs[n + 1]
    rank_ref, slot_ref, start_ref = refs[n + 2 :]
    scalars = [
        pltpu.make_async_copy(source, target, scalar_sems.at[j])
        for j, (source, target) in enumerate(
            ((rank_hbm, rank_ref), (slot_hbm, slot_ref), (start_hbm, start_ref))
        )
    ]
    for copy in scalars:
        copy.start()
    copies = []
    first = 0
    for j, w_vmem in enumerate(weights):
        copies += weight_copies(w_hbm, first, w_vmem, sems.at[j])
        first += w_vmem.shape[1]
    for copy in copies:
        copy.start()
    for copy in scalars:
        copy.wait()
    slots, rows, rank_columns = factor_ref.shape
    home = lax.axis_index("gx")
    row = lax.broadcasted_iota(jnp.int32, (rows, rank_columns), 0)
    col = lax.broadcasted_iota(jnp.int32, (rows, rank_columns), 1)
    for s in range(slots):
        adapter = slot_ref[home * slots + s]
        rank = rank_ref[adapter]
        live = (row >= start_ref[adapter]) & (row < start_ref[adapter + 1]) & (col < rank)
        scale = ADAPTER_ALPHA / jnp.full((rows, rank_columns), rank, jnp.int32).astype(jnp.float32)
        factor_ref[s] = jnp.where(live, scale, 0.0)
    adapters = spread_ref.shape[1] // rank_columns
    for a in range(adapters):
        live = (row >= start_ref[a]) & (row < start_ref[a + 1])
        spread_ref[:, a * rank_columns : (a + 1) * rank_columns] = jnp.where(live, 1.0, 0.0)
    for copy in copies:
        copy.wait()


def split_wide(value):
    high = value.astype(jnp.bfloat16).astype(jnp.float32)
    low = jnp.where(high < jnp.inf, value - high, 0.0)
    lane = lax.broadcasted_iota(jnp.int32, value.shape, 1)
    return jnp.where(lane < LANES // 2, high, low)


def join_wide(value):
    return value[:, :1] + value[:, LANES - 1 :]


def rows_kernel(order, width, gain_ref, down_ref, factor_ref, *refs):
    n = len(order)
    blocks = refs[:n]
    x_ref, small_ref = refs[n:]
    home = lax.axis_index("gx")
    block_rows = blocks[0].shape[0]
    gain = gain_ref[...].astype(jnp.float32).reshape(1, gain_ref.shape[0])
    small_ref[...] = jnp.zeros(small_ref.shape, small_ref.dtype)
    for k, block in zip(order, blocks):
        begin = pl.multiple_of(jnp.bitwise_xor(home, k) * block_rows, block_rows)
        values = block[...].astype(jnp.float32)
        x_ref[pl.ds(begin, block_rows), :] = (values * gain).astype(jnp.bfloat16)
        if k == 0:
            squares = jnp.sum(values * values, axis=1, keepdims=True) / width
            squares = split_wide(jnp.broadcast_to(squares, (block_rows, LANES)))
            small_ref[pl.ds(begin, block_rows), LANES:] = squares.astype(jnp.bfloat16)
    slots, rows, rank_columns = factor_ref.shape
    total = jnp.zeros((rows, rank_columns), jnp.float32)
    for s in range(slots):
        projected = lax.dot_general(
            x_ref[...], down_ref[s], (((1,), (1,)), ((), ())), preferred_element_type=jnp.float32
        )
        factor = factor_ref[s]
        total = total + jnp.where(factor > 0, projected * factor, 0.0)
    small_ref[:, :rank_columns] = total.astype(small_ref.dtype)


def write_rows(acc, outs, n_y, n_z):
    z = lax.axis_index("gz")
    rows_here = outs[0].shape[0] // n_y
    for k in range(n_z):
        for y in range(n_y):
            owner = y * n_z + jnp.bitwise_xor(z, k)
            begin = pl.multiple_of(owner * rows_here, rows_here)
            outs[k][y * rows_here : (y + 1) * rows_here, :] = acc[
                pl.ds(begin, rows_here), :
            ].astype(outs[k].dtype)


def multiply(x_ref, weights, step, out, first):
    for weight in weights:

        def columns(j, weight=weight, first=first):
            here = pl.ds(pl.multiple_of(j * step, step), step)
            there = pl.ds(pl.multiple_of(first + j * step, step), step)
            out[:, there] = jnp.dot(x_ref[...], weight[:, here], preferred_element_type=jnp.float32)

        pl.loop(0, weight.shape[1] // step)(columns)
        first += weight.shape[1]


def base_kernel(n_w, first, step, w_hbm, x_ref, *refs):
    weights, out_ref, rest = refs[:n_w], refs[n_w], refs[n_w + 1 :]
    copies = weight_copies(w_hbm, first, *rest) if rest else []
    for copy in copies:
        copy.start()
    multiply(x_ref, weights, step, out_ref, 0)
    for copy in copies:
        copy.wait()


def product_kernel(n_w, n_y, n_z, step, first, x_ref, *refs):
    if first:
        base_ref, refs = refs[0], refs[2:]
    weights, outs, acc = refs[:n_w], refs[n_w:-1], refs[-1]
    if first:
        acc[:, :first] = base_ref[...]
    multiply(x_ref, weights, step, acc, first)
    write_rows(acc, outs, n_y, n_z)


def chip_rows(parts, here):
    total = parts[0][here, :].astype(jnp.float32)
    for part in parts[1:]:
        total = total + part[here, :].astype(jnp.float32)
    return total


def pair_kernel(n_y, n_z, *refs):
    parts, smalls, outs = refs[:n_z], refs[n_z:-n_y], refs[-n_y:]
    rows_here = outs[0].shape[0]
    columns = parts[0].shape[1]
    y, z = lax.axis_index("gy"), lax.axis_index("gz")
    for k in range(n_y):
        other = jnp.bitwise_xor(y, k)
        here = pl.ds(pl.multiple_of(other * rows_here, rows_here), rows_here)
        outs[k][:, :columns] = chip_rows(parts, here).astype(outs[k].dtype)
        if smalls:
            owner = other * n_z + z
            here = pl.ds(pl.multiple_of(owner * rows_here, rows_here), rows_here)
            small = chip_rows(smalls, here)
            square = jnp.broadcast_to(join_wide(small[:, LANES:]), (rows_here, LANES))
            outs[k][:, columns : columns + LANES] = small[:, :LANES].astype(outs[k].dtype)
            outs[k][:, columns + LANES :] = split_wide(square).astype(outs[k].dtype)


def final_kernel(n, n_z, step, spread_ref, up_ref, *refs):
    firsts, lasts, out_ref = refs[:n], refs[n : 2 * n], refs[2 * n]
    rows_here, columns = out_ref.shape
    done = firsts[0].shape[1]
    late = columns - done
    adapters, rank_columns, _ = up_ref.shape

    def added(parts, begin, end):
        total = parts[0][:, begin:end]
        for part in parts[1:]:
            total = total + part[:, begin:end].astype(jnp.float32)
        return total

    side = added(lasts, late, late + 2 * LANES)
    mean_sq = join_wide(side[:, LANES:])
    scale = lax.rsqrt(mean_sq + EPSILON)
    owner = lax.axis_index("gy") * n_z + lax.axis_index("gz")
    live = spread_ref[pl.ds(pl.multiple_of(owner * rows_here, rows_here), rows_here), :]
    spread = jnp.concatenate([side[:, :rank_columns]] * adapters, axis=1)
    spread = jnp.where(live > 0, spread, 0.0).astype(jnp.bfloat16)
    for c in range(0, columns, step):
        if c < done:
            base = added(firsts, c, c + step)
        else:
            base = added(lasts, c - done, c - done + step)
        up = up_ref[:, :, c : c + step].reshape(adapters * rank_columns, step)
        total = base + jnp.dot(spread, up, preferred_element_type=jnp.float32)
        value = jnp.where(mean_sq < jnp.inf, total * scale, 0.0)
        out_ref[:, c : c + step] = value.astype(out_ref.dtype)


def body(
    hidden,
    attention_norm_gain,
    query_weight,
    slot_down_factors,
    adapter_up_factors,
    adapter_of_row,
    padded_adapter_rank,
    adapter_in_slot,
    segment_starts,
):
    n_x, n_y, n_z = lax.axis_size("gx"), lax.axis_size("gy"), lax.axis_size("gz")
    groups = n_y * n_z
    block_rows, depth = hidden.shape
    columns = query_weight.shape[1]
    rows = n_x * block_rows
    rows_here = rows // groups

    def send(value, axis, n, k):
        return lax.ppermute(value, axis, [(j, j ^ k) for j in range(n)])

    def spread_out(made, axis, n):
        return [made[0]] + [send(made[k], axis, n, k) for k in range(1, n)]

    order = [0, *range(n_x - 1, 0, -1)]
    blocks = [hidden] + [send(hidden, "gx", n_x, k) for k in order[1:]]

    step = min(256, columns // 4)
    pieces = 8
    f32, bf16 = jnp.float32, jnp.bfloat16
    slots, rank_columns = slot_down_factors.shape[0], slot_down_factors.shape[2]
    adapters = adapter_up_factors.shape[0]
    quarter = columns // 4
    late = quarter // 2 if quarter % (2 * LANES) == 0 else 0
    loads = [quarter] * 3 + [quarter - late]
    weight_hbm = pltpu.with_memory_space_constraint(query_weight, pltpu.HBM)
    kept = n_y * rows_here
    roomy = params(4 + (rows * depth >> 16))

    scalars = (padded_adapter_rank, adapter_in_slot, segment_starts)
    factor, spread, *weights = pl.pallas_call(
        functools.partial(fetch_kernel, len(loads)),
        out_shape=[
            jax.ShapeDtypeStruct((slots, rows, rank_columns), f32),
            jax.ShapeDtypeStruct((rows, adapters * rank_columns), f32),
        ]
        + [pltpu.VMEM((depth, wide), query_weight.dtype) for wide in loads],
        in_specs=[HBM] * 4,
        out_specs=[VMEM] * (2 + len(loads)),
        scratch_shapes=[
            pltpu.SemaphoreType.DMA((len(loads), pieces)),
            pltpu.SemaphoreType.DMA((len(scalars),)),
            *[pltpu.SMEM(value.shape, value.dtype) for value in scalars],
        ],
        cost_estimate=cost(0, 2 * query_weight.size),
        compiler_params=roomy,
        name="fetch_weight",
    )(weight_hbm, *[pltpu.with_memory_space_constraint(v, pltpu.HBM) for v in scalars])
    weights = [pltpu.with_memory_space_constraint(w, pltpu.VMEM) for w in weights]

    x, small = pl.pallas_call(
        functools.partial(rows_kernel, order, depth * groups),
        out_shape=(
            jax.ShapeDtypeStruct((rows, depth), bf16),
            jax.ShapeDtypeStruct((rows, 2 * LANES), bf16),
        ),
        in_specs=[VMEM] * (3 + n_x),
        out_specs=(VMEM,) * 2,
        compiler_params=roomy,
        name="scaled_rows",
    )(attention_norm_gain, jnp.swapaxes(slot_down_factors, 1, 2), factor, *blocks)

    one_hop = small = small + send(small, "gx", n_x, 1)
    hop = 2
    while hop < n_x:
        small = small + send(small, "gx", n_x, hop)
        hop *= 2

    def shapes(n, shape):
        return [jax.ShapeDtypeStruct(shape, f32 if k == 0 else bf16) for k in range(n)]

    base, *rest = pl.pallas_call(
        functools.partial(base_kernel, 2, columns - late, step),
        out_shape=[jax.ShapeDtypeStruct((rows, 2 * quarter), f32)]
        + ([pltpu.VMEM((depth, late), query_weight.dtype)] if late else []),
        in_specs=[HBM] + [VMEM] * 3,
        out_specs=[VMEM] * (2 if late else 1),
        scratch_shapes=[pltpu.SemaphoreType.DMA((pieces,))] if late else [],
        cost_estimate=cost(4 * rows * depth * quarter, 4 * depth * quarter),
        compiler_params=roomy,
        name="first_columns",
    )(weight_hbm, x, *weights[:2])
    weights += [pltpu.with_memory_space_constraint(w, pltpu.VMEM) for w in rest]

    def product(some, bases, times, name):
        first = sum(part.shape[1] for part in bases[:1])
        wide = first + quarter
        made = pl.pallas_call(
            functools.partial(product_kernel, len(some), n_y, n_z, step, first),
            out_shape=shapes(n_z, (kept, wide)),
            in_specs=[VMEM] * (1 + len(bases) + len(some)),
            out_specs=[VMEM] * n_z,
            scratch_shapes=[pltpu.VMEM((rows, wide), f32)],
            cost_estimate=cost(2 * rows * depth * wide * times, 2 * depth * wide),
            compiler_params=roomy,
            name=name,
        )(x, *bases, *some)
        return spread_out(made, "gz", n_z)

    firsts = product(weights[2:3], [base, one_hop], 4, "middle_columns")
    lasts = product(weights[3:], [], 8, "last_columns")
    smalls = spread_out([small] * n_z, "gz", n_z)

    def chip_sums(parts, sides, name):
        wide = parts[0].shape[1] + (2 * LANES if sides else 0)
        made = pl.pallas_call(
            functools.partial(pair_kernel, n_y, n_z),
            out_shape=shapes(n_y, (rows_here, wide)),
            in_specs=[VMEM] * (n_z + len(sides)),
            out_specs=[VMEM] * n_y,
            cost_estimate=cost(2 * rows * depth * quarter, 2 * depth * quarter),
            compiler_params=roomy,
            name=name,
        )(*parts, *sides)
        return spread_out(made, "gy", n_y)

    first_parts = chip_sums(firsts, [], "first_sums")
    last_parts = chip_sums(lasts, smalls, "last_sums")

    return pl.pallas_call(
        functools.partial(final_kernel, n_y, n_z, min(512, columns // 4)),
        out_shape=jax.ShapeDtypeStruct((rows_here, columns), bf16),
        in_specs=[VMEM] * (2 + 2 * n_y),
        out_specs=VMEM,
        compiler_params=roomy,
        name="query_rows",
    )(spread, adapter_up_factors, *first_parts, *last_parts)


def solution(mesh):
    return jax.shard_map(
        body,
        mesh=mesh,
        in_specs=(
            P(("rep", "gx"), ("gy", "gz")),
            P(("gy", "gz")),
            P(("gy", "gz"), "gx"),
            P("gx", ("gy", "gz"), None),
            P(None, None, "gx"),
            P("rep"),
            P(),
            P(),
            P("rep"),
        ),
        out_specs=P(("rep", "gy", "gz"), "gx"),
        check_vma=False,
    )
```

```python
import functools

import jax
import jax.numpy as jnp
from jax import lax
from jax.experimental import pallas as pl
from jax.experimental.pallas import tpu as pltpu
from jax.sharding import PartitionSpec as P

EPSILON = 1e-05
ADAPTER_ALPHA = 32.0
LANES = 128
MIB = 1 << 20

VMEM = pl.BlockSpec(memory_space=pltpu.VMEM)
HBM = pl.BlockSpec(memory_space=pltpu.HBM)
ANY = pl.BlockSpec(memory_space=pl.ANY)


def params(mib):
    return pltpu.CompilerParams(vmem_limit_bytes=mib * MIB)


def cost(flops, moved):
    return pl.CostEstimate(flops=flops, bytes_accessed=moved, transcendentals=0)


def weight_copies(w_hbm, first, w_vmem, sems):
    pieces = sems.shape[0]
    depth, width = w_vmem.shape
    step = depth // pieces
    return [
        pltpu.make_async_copy(
            w_hbm.at[pl.ds(p * step, step), pl.ds(first, width)],
            w_vmem.at[pl.ds(p * step, step)],
            sems.at[p],
        )
        for p in range(pieces)
    ]


def load(w_hbm, first, weights, sems, meanwhile):
    copies = []
    for j, w_vmem in enumerate(weights):
        copies += weight_copies(w_hbm, first, w_vmem, sems.at[j])
        first += w_vmem.shape[1]
    for copy in copies:
        copy.start()
    meanwhile()
    for copy in copies:
        copy.wait()


def first_load_kernel(n, w_hbm, rank_hbm, slot_hbm, start_hbm, factor_ref, spread_ref, *refs):
    weights, sems, scalar_sems = refs[:n], refs[n], refs[n + 1]
    rank_ref, slot_ref, start_ref = refs[n + 2 :]

    def masks():
        pairs = ((rank_hbm, rank_ref), (slot_hbm, slot_ref), (start_hbm, start_ref))
        scalars = [
            pltpu.make_async_copy(source, target, scalar_sems.at[j])
            for j, (source, target) in enumerate(pairs)
        ]
        for copy in scalars:
            copy.start()
        for copy in scalars:
            copy.wait()
        slots, rows, rank_columns = factor_ref.shape
        home = lax.axis_index("gx")
        row = lax.broadcasted_iota(jnp.int32, (rows, rank_columns), 0)
        col = lax.broadcasted_iota(jnp.int32, (rows, rank_columns), 1)
        for s in range(slots):
            adapter = slot_ref[home * slots + s]
            rank = rank_ref[adapter]
            live = (row >= start_ref[adapter]) & (row < start_ref[adapter + 1]) & (col < rank)
            ranks = jnp.full((rows, rank_columns), rank, jnp.int32).astype(jnp.float32)
            factor_ref[s] = jnp.where(live, ADAPTER_ALPHA / ranks, 0.0)
        adapters = spread_ref.shape[1] // rank_columns
        for a in range(adapters):
            live = (row >= start_ref[a]) & (row < start_ref[a + 1])
            spread_ref[:, a * rank_columns : (a + 1) * rank_columns] = jnp.where(live, 1.0, 0.0)

    load(w_hbm, 0, weights, sems, masks)


def last_load_kernel(n, first, w_hbm, _, __, *refs):
    load(w_hbm, first, refs[:n], refs[n], lambda: None)


def split_wide(value):
    high = value.astype(jnp.bfloat16).astype(jnp.float32)
    low = jnp.where(high < jnp.inf, value - high, 0.0)
    lane = lax.broadcasted_iota(jnp.int32, value.shape, 1)
    return jnp.where(lane < LANES // 2, high, low)


def join_wide(value):
    return value[:, :1] + value[:, LANES - 1 :]


def rows_kernel(order, width, gain_ref, down_ref, factor_ref, *refs):
    n = len(order)
    blocks = refs[:n]
    x_ref, small_ref = refs[n:]
    home = lax.axis_index("gx")
    block_rows = blocks[0].shape[0]
    gain = gain_ref[...].astype(jnp.float32).reshape(1, gain_ref.shape[0])
    small_ref[...] = jnp.zeros(small_ref.shape, small_ref.dtype)
    for k, block in zip(order, blocks):
        begin = pl.multiple_of(jnp.bitwise_xor(home, k) * block_rows, block_rows)
        values = block[...].astype(jnp.float32)
        x_ref[pl.ds(begin, block_rows), :] = (values * gain).astype(jnp.bfloat16)
        if k == 0:
            squares = jnp.sum(values * values, axis=1, keepdims=True) / width
            squares = split_wide(jnp.broadcast_to(squares, (block_rows, LANES)))
            small_ref[pl.ds(begin, block_rows), LANES:] = squares.astype(jnp.bfloat16)
    slots, rows, rank_columns = factor_ref.shape
    total = jnp.zeros((rows, rank_columns), jnp.float32)
    for s in range(slots):
        projected = lax.dot_general(
            x_ref[...], down_ref[s], (((1,), (1,)), ((), ())), preferred_element_type=jnp.float32
        )
        factor = factor_ref[s]
        total = total + jnp.where(factor > 0, projected * factor, 0.0)
    small_ref[:, :rank_columns] = total.astype(small_ref.dtype)


def write_rows(acc, outs, n_y, n_z):
    z = lax.axis_index("gz")
    rows_here = outs[0].shape[0] // n_y
    for k in range(n_z):
        for y in range(n_y):
            owner = y * n_z + jnp.bitwise_xor(z, k)
            begin = pl.multiple_of(owner * rows_here, rows_here)
            outs[k][y * rows_here : (y + 1) * rows_here, :] = acc[
                pl.ds(begin, rows_here), :
            ].astype(outs[k].dtype)


def multiply(x_ref, weights, step, out, first):
    for weight in weights:
        width = weight.shape[1]
        for c in range(0, width, step):
            out[:, first + c : first + c + step] = jnp.dot(
                x_ref[...], weight[:, c : c + step], preferred_element_type=jnp.float32
            )
        first += width


def base_kernel(n_w, first, step, w_hbm, x_ref, *refs):
    weights, out_ref, rest = refs[:n_w], refs[n_w], refs[n_w + 1 :]
    copies = weight_copies(w_hbm, first, *rest) if rest else []
    for copy in copies:
        copy.start()

    @pl.when(lax.axis_index("gx") >= 0)
    def behind_the_copies():
        multiply(x_ref, weights, step, out_ref, 0)

    for copy in copies:
        copy.wait()


def product_kernel(n_w, n_y, n_z, step, first, x_ref, *refs):
    if first:
        base_ref, refs = refs[0], refs[2:]
    weights, outs, acc = refs[:n_w], refs[n_w:-1], refs[-1]
    if first:
        acc[:, :first] = base_ref[...]
    multiply(x_ref, weights, step, acc, first)
    write_rows(acc, outs, n_y, n_z)


def chip_rows(parts, here):
    total = parts[0][here, :].astype(jnp.float32)
    for part in parts[1:]:
        total = total + part[here, :].astype(jnp.float32)
    return total


def pair_kernel(n_y, n_z, *refs):
    parts, smalls, outs = refs[:n_z], refs[n_z:-n_y], refs[-n_y:]
    rows_here = outs[0].shape[0]
    columns = parts[0].shape[1]
    y, z = lax.axis_index("gy"), lax.axis_index("gz")
    for k in range(n_y):
        other = jnp.bitwise_xor(y, k)
        here = pl.ds(pl.multiple_of(other * rows_here, rows_here), rows_here)
        outs[k][:, :columns] = chip_rows(parts, here).astype(outs[k].dtype)
        if smalls:
            owner = other * n_z + z
            here = pl.ds(pl.multiple_of(owner * rows_here, rows_here), rows_here)
            small = chip_rows(smalls, here)
            square = jnp.broadcast_to(join_wide(small[:, LANES:]), (rows_here, LANES))
            outs[k][:, columns : columns + LANES] = small[:, :LANES].astype(outs[k].dtype)
            outs[k][:, columns + LANES :] = split_wide(square).astype(outs[k].dtype)


def final_kernel(n, n_z, step, spread_ref, up_ref, *refs):
    firsts, lasts, out_ref = refs[:n], refs[n : 2 * n], refs[2 * n]
    rows_here, columns = out_ref.shape
    done = firsts[0].shape[1]
    late = columns - done
    adapters, rank_columns, _ = up_ref.shape

    def added(parts, begin, end):
        total = parts[0][:, begin:end]
        for part in parts[1:]:
            total = total + part[:, begin:end].astype(jnp.float32)
        return total

    side = added(lasts, late, late + 2 * LANES)
    mean_sq = join_wide(side[:, LANES:])
    scale = lax.rsqrt(mean_sq + EPSILON)
    owner = lax.axis_index("gy") * n_z + lax.axis_index("gz")
    live = spread_ref[pl.ds(pl.multiple_of(owner * rows_here, rows_here), rows_here), :]
    spread = jnp.concatenate([side[:, :rank_columns]] * adapters, axis=1)
    spread = jnp.where(live > 0, spread, 0.0).astype(jnp.bfloat16)
    for c in range(0, columns, step):
        if c < done:
            base = added(firsts, c, c + step)
        else:
            base = added(lasts, c - done, c - done + step)
        up = up_ref[:, :, c : c + step].reshape(adapters * rank_columns, step)
        total = base + jnp.dot(spread, up, preferred_element_type=jnp.float32)
        value = jnp.where(mean_sq < jnp.inf, total * scale, 0.0)
        out_ref[:, c : c + step] = value.astype(out_ref.dtype)


def body(
    hidden,
    attention_norm_gain,
    query_weight,
    slot_down_factors,
    adapter_up_factors,
    adapter_of_row,
    padded_adapter_rank,
    adapter_in_slot,
    segment_starts,
):
    n_x, n_y, n_z = lax.axis_size("gx"), lax.axis_size("gy"), lax.axis_size("gz")
    groups = n_y * n_z
    block_rows, depth = hidden.shape
    columns = query_weight.shape[1]
    rows = n_x * block_rows
    rows_here = rows // groups

    def send(value, axis, n, k):
        return lax.ppermute(value, axis, [(j, j ^ k) for j in range(n)])

    def spread_out(made, axis, n):
        return [made[0]] + [send(made[k], axis, n, k) for k in range(1, n)]

    sent = {0: hidden}
    order = [0, *range(2, n_x, 2), 1, *range(3, n_x, 2)]
    for k in order[1:]:
        sent[k] = send(sent[k - 1], "gx", n_x, 1) if k % 2 else send(hidden, "gx", n_x, k)
    blocks = [sent[k] for k in order]

    step = min(512, columns // 4)
    pieces = 8
    f32, bf16 = jnp.float32, jnp.bfloat16
    slots, rank_columns = slot_down_factors.shape[0], slot_down_factors.shape[2]
    adapters = adapter_up_factors.shape[0]
    quarter = columns // 4
    half = quarter // 2 if quarter % (2 * LANES) == 0 else 0
    if half:
        loads = [quarter, quarter, half], [half, half]
    else:
        loads = [quarter, quarter], [quarter, quarter]
    kept = n_y * rows_here
    roomy = params(4 + (rows * depth >> 16))

    scalars = (padded_adapter_rank, adapter_in_slot, segment_starts)
    weight_hbm = pltpu.with_memory_space_constraint(query_weight, pltpu.HBM)
    load_cost = cost(300 * query_weight.size, query_weight.size)
    factor, spread, *weights = pl.pallas_call(
        functools.partial(first_load_kernel, len(loads[0])),
        out_shape=[
            jax.ShapeDtypeStruct((slots, rows, rank_columns), f32),
            jax.ShapeDtypeStruct((rows, adapters * rank_columns), f32),
        ]
        + [pltpu.VMEM((depth, wide), query_weight.dtype) for wide in loads[0]],
        in_specs=[HBM] * 4,
        out_specs=[VMEM] * (2 + len(loads[0])),
        scratch_shapes=[
            pltpu.SemaphoreType.DMA((len(loads[0]), pieces)),
            pltpu.SemaphoreType.DMA((len(scalars),)),
            *[pltpu.SMEM(value.shape, value.dtype) for value in scalars],
        ],
        cost_estimate=load_cost,
        compiler_params=roomy,
        name="first_load",
    )(weight_hbm, *[pltpu.with_memory_space_constraint(v, pltpu.HBM) for v in scalars])
    weights += pl.pallas_call(
        functools.partial(last_load_kernel, len(loads[1]), sum(loads[0])),
        out_shape=[pltpu.VMEM((depth, wide), query_weight.dtype) for wide in loads[1]],
        in_specs=[HBM, ANY, ANY],
        out_specs=[VMEM] * len(loads[1]),
        scratch_shapes=[pltpu.SemaphoreType.DMA((len(loads[1]), pieces))],
        cost_estimate=load_cost,
        compiler_params=roomy,
        name="last_load",
    )(weight_hbm, factor, blocks[1])
    weights = [pltpu.with_memory_space_constraint(w, pltpu.VMEM) for w in weights]

    x, small = pl.pallas_call(
        functools.partial(rows_kernel, order, depth * groups),
        out_shape=(
            jax.ShapeDtypeStruct((rows, depth), bf16),
            jax.ShapeDtypeStruct((rows, 2 * LANES), bf16),
        ),
        in_specs=[VMEM] * (3 + n_x),
        out_specs=(VMEM,) * 2,
        compiler_params=roomy,
        name="scaled_rows",
    )(attention_norm_gain, jnp.swapaxes(slot_down_factors, 1, 2), factor, *blocks)

    one_hop = small = small + send(small, "gx", n_x, 1)
    hop = 2
    while hop < n_x:
        small = small + send(small, "gx", n_x, hop)
        hop *= 2

    def shapes(n, shape):
        return [jax.ShapeDtypeStruct(shape, f32 if k == 0 else bf16) for k in range(n)]

    base, *rest = pl.pallas_call(
        functools.partial(base_kernel, 2, columns - half, step),
        out_shape=[jax.ShapeDtypeStruct((rows, 2 * quarter), f32)]
        + ([pltpu.VMEM((depth, half), query_weight.dtype)] if half else []),
        in_specs=[HBM] + [VMEM] * 3,
        out_specs=[VMEM] * (2 if half else 1),
        scratch_shapes=[pltpu.SemaphoreType.DMA((pieces,))] if half else [],
        cost_estimate=cost(4 * rows * depth * quarter, 4 * depth * quarter),
        compiler_params=roomy,
        name="first_columns",
    )(weight_hbm, x, *weights[:2])
    weights += [pltpu.with_memory_space_constraint(w, pltpu.VMEM) for w in rest]

    def product(some, bases, times, name):
        first = sum(part.shape[1] for part in bases[:1])
        wide = first + quarter
        made = pl.pallas_call(
            functools.partial(product_kernel, len(some), n_y, n_z, step, first),
            out_shape=shapes(n_z, (kept, wide)),
            in_specs=[VMEM] * (1 + len(bases) + len(some)),
            out_specs=[VMEM] * n_z,
            scratch_shapes=[pltpu.VMEM((rows, wide), f32)],
            cost_estimate=cost(2 * rows * depth * wide * times, 2 * depth * wide),
            compiler_params=roomy,
            name=name,
        )(x, *bases, *some)
        return spread_out(made, "gz", n_z)

    firsts = product(weights[2 : 4 if half else 3], [base, one_hop], 4, "middle_columns")
    lasts = product(weights[4 if half else 3 :], [], 8, "last_columns")
    smalls = spread_out([small] * n_z, "gz", n_z)

    def chip_sums(parts, sides, name):
        wide = parts[0].shape[1] + (2 * LANES if sides else 0)
        made = pl.pallas_call(
            functools.partial(pair_kernel, n_y, n_z),
            out_shape=shapes(n_y, (rows_here, wide)),
            in_specs=[VMEM] * (n_z + len(sides)),
            out_specs=[VMEM] * n_y,
            cost_estimate=cost(2 * rows * depth * quarter, 2 * depth * quarter),
            compiler_params=roomy,
            name=name,
        )(*parts, *sides)
        return spread_out(made, "gy", n_y)

    first_parts = chip_sums(firsts, [], "first_sums")
    last_parts = chip_sums(lasts, smalls, "last_sums")

    return pl.pallas_call(
        functools.partial(final_kernel, n_y, n_z, step),
        out_shape=jax.ShapeDtypeStruct((rows_here, columns), bf16),
        in_specs=[VMEM] * (2 + 2 * n_y),
        out_specs=VMEM,
        compiler_params=roomy,
        name="query_rows",
    )(spread, adapter_up_factors, *first_parts, *last_parts)


def solution(mesh):
    return jax.shard_map(
        body,
        mesh=mesh,
        in_specs=(
            P(("rep", "gx"), ("gy", "gz")),
            P(("gy", "gz")),
            P(("gy", "gz"), "gx"),
            P("gx", ("gy", "gz"), None),
            P(None, None, "gx"),
            P("rep"),
            P(),
            P(),
            P("rep"),
        ),
        out_specs=P(("rep", "gy", "gz"), "gx"),
        check_vma=False,
    )
```

```python
import functools

import jax
import jax.numpy as jnp
from jax import lax
from jax.experimental import pallas as pl
from jax.experimental.pallas import tpu as pltpu
from jax.sharding import PartitionSpec as P

EPSILON = 1e-05
ADAPTER_ALPHA = 32.0
LANES = 128
MIB = 1 << 20

VMEM = pl.BlockSpec(memory_space=pltpu.VMEM)
HBM = pl.BlockSpec(memory_space=pltpu.HBM)
ANY = pl.BlockSpec(memory_space=pl.ANY)


def params(mib):
    return pltpu.CompilerParams(vmem_limit_bytes=mib * MIB)


def cost(flops, moved):
    return pl.CostEstimate(flops=flops, bytes_accessed=moved, transcendentals=0)


def weight_copies(w_hbm, first, w_vmem, sems):
    pieces = sems.shape[0]
    depth, width = w_vmem.shape
    step = depth // pieces
    return [
        pltpu.make_async_copy(
            w_hbm.at[pl.ds(p * step, step), pl.ds(first, width)],
            w_vmem.at[pl.ds(p * step, step)],
            sems.at[p],
        )
        for p in range(pieces)
    ]


def load(w_hbm, first, weights, sems, meanwhile):
    copies = []
    for j, w_vmem in enumerate(weights):
        copies += weight_copies(w_hbm, first, w_vmem, sems.at[j])
        first += w_vmem.shape[1]
    for copy in copies:
        copy.start()
    meanwhile()
    for copy in copies:
        copy.wait()


def first_load_kernel(n, w_hbm, rank_hbm, slot_hbm, start_hbm, factor_ref, spread_ref, *refs):
    weights, sems, scalar_sems = refs[:n], refs[n], refs[n + 1]
    rank_ref, slot_ref, start_ref = refs[n + 2 :]

    def masks():
        pairs = ((rank_hbm, rank_ref), (slot_hbm, slot_ref), (start_hbm, start_ref))
        scalars = [
            pltpu.make_async_copy(source, target, scalar_sems.at[j])
            for j, (source, target) in enumerate(pairs)
        ]
        for copy in scalars:
            copy.start()
        for copy in scalars:
            copy.wait()
        slots, rows, rank_columns = factor_ref.shape
        home = lax.axis_index("gx")
        row = lax.broadcasted_iota(jnp.int32, (rows, rank_columns), 0)
        col = lax.broadcasted_iota(jnp.int32, (rows, rank_columns), 1)
        for s in range(slots):
            adapter = slot_ref[home * slots + s]
            rank = rank_ref[adapter]
            live = (row >= start_ref[adapter]) & (row < start_ref[adapter + 1]) & (col < rank)
            ranks = jnp.full((rows, rank_columns), rank, jnp.int32).astype(jnp.float32)
            factor_ref[s] = jnp.where(live, ADAPTER_ALPHA / ranks, 0.0)
        adapters = spread_ref.shape[1] // rank_columns
        for a in range(adapters):
            live = (row >= start_ref[a]) & (row < start_ref[a + 1])
            spread_ref[:, a * rank_columns : (a + 1) * rank_columns] = jnp.where(live, 1.0, 0.0)

    load(w_hbm, 0, weights, sems, masks)


def last_load_kernel(n, first, w_hbm, _, __, *refs):
    load(w_hbm, first, refs[:n], refs[n], lambda: None)


def split_wide(value):
    high = value.astype(jnp.bfloat16).astype(jnp.float32)
    low = jnp.where(high < jnp.inf, value - high, 0.0)
    lane = lax.broadcasted_iota(jnp.int32, value.shape, 1)
    return jnp.where(lane < LANES // 2, high, low)


def join_wide(value):
    return value[:, :1] + value[:, LANES - 1 :]


def rows_kernel(order, width, gain_ref, down_ref, factor_ref, *refs):
    n = len(order)
    blocks = refs[:n]
    x_ref, small_ref = refs[n:]
    home = lax.axis_index("gx")
    block_rows = blocks[0].shape[0]
    gain = gain_ref[...].astype(jnp.float32).reshape(1, gain_ref.shape[0])
    small_ref[...] = jnp.zeros(small_ref.shape, small_ref.dtype)
    for k, block in zip(order, blocks):
        begin = pl.multiple_of(jnp.bitwise_xor(home, k) * block_rows, block_rows)
        values = block[...].astype(jnp.float32)
        x_ref[pl.ds(begin, block_rows), :] = (values * gain).astype(jnp.bfloat16)
        if k == 0:
            squares = jnp.sum(values * values, axis=1, keepdims=True) / width
            squares = split_wide(jnp.broadcast_to(squares, (block_rows, LANES)))
            small_ref[pl.ds(begin, block_rows), LANES:] = squares.astype(jnp.bfloat16)
    slots, rows, rank_columns = factor_ref.shape
    total = jnp.zeros((rows, rank_columns), jnp.float32)
    for s in range(slots):
        projected = lax.dot_general(
            x_ref[...], down_ref[s], (((1,), (1,)), ((), ())), preferred_element_type=jnp.float32
        )
        factor = factor_ref[s]
        total = total + jnp.where(factor > 0, projected * factor, 0.0)
    small_ref[:, :rank_columns] = total.astype(small_ref.dtype)


def write_rows(acc, outs, n_y, n_z):
    z = lax.axis_index("gz")
    rows_here = outs[0].shape[0] // n_y
    for k in range(n_z):
        for y in range(n_y):
            owner = y * n_z + jnp.bitwise_xor(z, k)
            begin = pl.multiple_of(owner * rows_here, rows_here)
            outs[k][y * rows_here : (y + 1) * rows_here, :] = acc[
                pl.ds(begin, rows_here), :
            ].astype(outs[k].dtype)


def multiply(x_ref, weights, step, out, first):
    for weight in weights:
        width = weight.shape[1]
        wide = min(step, width)
        for c in range(0, width, wide):
            out[:, first + c : first + c + wide] = jnp.dot(
                x_ref[...], weight[:, c : c + wide], preferred_element_type=jnp.float32
            )
        first += width


def base_kernel(n_w, first, step, w_hbm, x_ref, *refs):
    weights, out_ref, rest = refs[:n_w], refs[n_w], refs[n_w + 1 :]
    copies = weight_copies(w_hbm, first, *rest) if rest else []
    for copy in copies:
        copy.start()

    @pl.when(lax.axis_index("gx") >= 0)
    def behind_the_copies():
        multiply(x_ref, weights, step, out_ref, 0)

    for copy in copies:
        copy.wait()


def product_kernel(n_w, n_y, n_z, step, first, x_ref, *refs):
    if first:
        base_ref, refs = refs[0], refs[2:]
    weights, outs, acc = refs[:n_w], refs[n_w:-1], refs[-1]
    if first:
        acc[:, :first] = base_ref[...]
    multiply(x_ref, weights, step, acc, first)
    write_rows(acc, outs, n_y, n_z)


def chip_rows(parts, here):
    total = parts[0][here, :].astype(jnp.float32)
    for part in parts[1:]:
        total = total + part[here, :].astype(jnp.float32)
    return total


def pair_kernel(n_y, n_z, *refs):
    parts, smalls, outs = refs[:n_z], refs[n_z:-n_y], refs[-n_y:]
    rows_here = outs[0].shape[0]
    columns = parts[0].shape[1]
    y, z = lax.axis_index("gy"), lax.axis_index("gz")
    for k in range(n_y):
        other = jnp.bitwise_xor(y, k)
        here = pl.ds(pl.multiple_of(other * rows_here, rows_here), rows_here)
        outs[k][:, :columns] = chip_rows(parts, here).astype(outs[k].dtype)
        if smalls:
            owner = other * n_z + z
            here = pl.ds(pl.multiple_of(owner * rows_here, rows_here), rows_here)
            small = chip_rows(smalls, here)
            square = jnp.broadcast_to(join_wide(small[:, LANES:]), (rows_here, LANES))
            outs[k][:, columns : columns + LANES] = small[:, :LANES].astype(outs[k].dtype)
            outs[k][:, columns + LANES :] = split_wide(square).astype(outs[k].dtype)


def final_kernel(n, n_z, step, spread_ref, up_ref, *refs):
    firsts, lasts, out_ref = refs[:n], refs[n : 2 * n], refs[2 * n]
    rows_here, columns = out_ref.shape
    done = firsts[0].shape[1]
    late = columns - done
    adapters, rank_columns, _ = up_ref.shape

    def added(parts, begin, end):
        total = parts[0][:, begin:end]
        for part in parts[1:]:
            total = total + part[:, begin:end].astype(jnp.float32)
        return total

    side = added(lasts, late, late + 2 * LANES)
    mean_sq = join_wide(side[:, LANES:])
    scale = lax.rsqrt(mean_sq + EPSILON)
    owner = lax.axis_index("gy") * n_z + lax.axis_index("gz")
    live = spread_ref[pl.ds(pl.multiple_of(owner * rows_here, rows_here), rows_here), :]
    spread = jnp.concatenate([side[:, :rank_columns]] * adapters, axis=1)
    spread = jnp.where(live > 0, spread, 0.0).astype(jnp.bfloat16)
    for c in range(0, columns, step):
        if c < done:
            base = added(firsts, c, c + step)
        else:
            base = added(lasts, c - done, c - done + step)
        up = up_ref[:, :, c : c + step].reshape(adapters * rank_columns, step)
        total = base + jnp.dot(spread, up, preferred_element_type=jnp.float32)
        value = jnp.where(mean_sq < jnp.inf, total * scale, 0.0)
        out_ref[:, c : c + step] = value.astype(out_ref.dtype)


def body(
    hidden,
    attention_norm_gain,
    query_weight,
    slot_down_factors,
    adapter_up_factors,
    adapter_of_row,
    padded_adapter_rank,
    adapter_in_slot,
    segment_starts,
):
    n_x, n_y, n_z = lax.axis_size("gx"), lax.axis_size("gy"), lax.axis_size("gz")
    groups = n_y * n_z
    block_rows, depth = hidden.shape
    columns = query_weight.shape[1]
    rows = n_x * block_rows
    rows_here = rows // groups

    def send(value, axis, n, k):
        return lax.ppermute(value, axis, [(j, j ^ k) for j in range(n)])

    def spread_out(made, axis, n):
        return [made[0]] + [send(made[k], axis, n, k) for k in range(1, n)]

    sent = {0: hidden}
    order = [0, *range(2, n_x, 2), 1, *range(3, n_x, 2)]
    for k in order[1:]:
        sent[k] = send(sent[k - 1], "gx", n_x, 1) if k % 2 else send(hidden, "gx", n_x, k)
    blocks = [sent[k] for k in order]

    step = min(1024, columns // 4)
    pieces = 8
    f32, bf16 = jnp.float32, jnp.bfloat16
    slots, rank_columns = slot_down_factors.shape[0], slot_down_factors.shape[2]
    adapters = adapter_up_factors.shape[0]
    quarter = columns // 4
    part = quarter // 4
    if part % LANES == 0:
        loads, late = ([quarter, quarter], [quarter, part]), quarter - part
    else:
        loads, late = ([quarter, quarter], [quarter, quarter]), 0
    kept = n_y * rows_here
    roomy = params(4 + (rows * depth >> 16))

    scalars = (padded_adapter_rank, adapter_in_slot, segment_starts)
    weight_hbm = pltpu.with_memory_space_constraint(query_weight, pltpu.HBM)
    load_cost = cost(300 * query_weight.size, query_weight.size)
    factor, spread, *weights = pl.pallas_call(
        functools.partial(first_load_kernel, len(loads[0])),
        out_shape=[
            jax.ShapeDtypeStruct((slots, rows, rank_columns), f32),
            jax.ShapeDtypeStruct((rows, adapters * rank_columns), f32),
        ]
        + [pltpu.VMEM((depth, wide), query_weight.dtype) for wide in loads[0]],
        in_specs=[HBM] * 4,
        out_specs=[VMEM] * (2 + len(loads[0])),
        scratch_shapes=[
            pltpu.SemaphoreType.DMA((len(loads[0]), pieces)),
            pltpu.SemaphoreType.DMA((len(scalars),)),
            *[pltpu.SMEM(value.shape, value.dtype) for value in scalars],
        ],
        cost_estimate=load_cost,
        compiler_params=roomy,
        name="first_load",
    )(weight_hbm, *[pltpu.with_memory_space_constraint(v, pltpu.HBM) for v in scalars])
    weights += pl.pallas_call(
        functools.partial(last_load_kernel, len(loads[1]), sum(loads[0])),
        out_shape=[pltpu.VMEM((depth, wide), query_weight.dtype) for wide in loads[1]],
        in_specs=[HBM, ANY, ANY],
        out_specs=[VMEM] * len(loads[1]),
        scratch_shapes=[pltpu.SemaphoreType.DMA((len(loads[1]), pieces))],
        cost_estimate=load_cost,
        compiler_params=roomy,
        name="last_load",
    )(weight_hbm, factor, blocks[1])
    weights = [pltpu.with_memory_space_constraint(w, pltpu.VMEM) for w in weights]

    x, small = pl.pallas_call(
        functools.partial(rows_kernel, order, depth * groups),
        out_shape=(
            jax.ShapeDtypeStruct((rows, depth), bf16),
            jax.ShapeDtypeStruct((rows, 2 * LANES), bf16),
        ),
        in_specs=[VMEM] * (3 + n_x),
        out_specs=(VMEM,) * 2,
        compiler_params=roomy,
        name="scaled_rows",
    )(attention_norm_gain, jnp.swapaxes(slot_down_factors, 1, 2), factor, *blocks)

    one_hop = small = small + send(small, "gx", n_x, 1)
    hop = 2
    while hop < n_x:
        small = small + send(small, "gx", n_x, hop)
        hop *= 2

    def shapes(n, shape):
        return [jax.ShapeDtypeStruct(shape, f32 if k == 0 else bf16) for k in range(n)]

    base, *rest = pl.pallas_call(
        functools.partial(base_kernel, 2, columns - late, step),
        out_shape=[jax.ShapeDtypeStruct((rows, 2 * quarter), f32)]
        + ([pltpu.VMEM((depth, late), query_weight.dtype)] if late else []),
        in_specs=[HBM] + [VMEM] * 3,
        out_specs=[VMEM] * (2 if late else 1),
        scratch_shapes=[pltpu.SemaphoreType.DMA((pieces,))] if late else [],
        cost_estimate=cost(4 * rows * depth * quarter, 4 * depth * quarter),
        compiler_params=roomy,
        name="first_columns",
    )(weight_hbm, x, *weights[:2])
    weights += [pltpu.with_memory_space_constraint(w, pltpu.VMEM) for w in rest]

    def product(some, bases, times, name):
        first = sum(part.shape[1] for part in bases[:1])
        wide = first + quarter
        made = pl.pallas_call(
            functools.partial(product_kernel, len(some), n_y, n_z, step, first),
            out_shape=shapes(n_z, (kept, wide)),
            in_specs=[VMEM] * (1 + len(bases) + len(some)),
            out_specs=[VMEM] * n_z,
            scratch_shapes=[pltpu.VMEM((rows, wide), f32)],
            cost_estimate=cost(2 * rows * depth * wide * times, 2 * depth * wide),
            compiler_params=roomy,
            name=name,
        )(x, *bases, *some)
        return spread_out(made, "gz", n_z)

    firsts = product(weights[2:3], [base, one_hop], 4, "middle_columns")
    lasts = product(weights[3:], [], 8, "last_columns")
    smalls = spread_out([small] * n_z, "gz", n_z)

    def chip_sums(parts, sides, name):
        wide = parts[0].shape[1] + (2 * LANES if sides else 0)
        made = pl.pallas_call(
            functools.partial(pair_kernel, n_y, n_z),
            out_shape=shapes(n_y, (rows_here, wide)),
            in_specs=[VMEM] * (n_z + len(sides)),
            out_specs=[VMEM] * n_y,
            cost_estimate=cost(2 * rows * depth * quarter, 2 * depth * quarter),
            compiler_params=roomy,
            name=name,
        )(*parts, *sides)
        return spread_out(made, "gy", n_y)

    first_parts = chip_sums(firsts, [], "first_sums")
    last_parts = chip_sums(lasts, smalls, "last_sums")

    return pl.pallas_call(
        functools.partial(final_kernel, n_y, n_z, min(512, columns // 4)),
        out_shape=jax.ShapeDtypeStruct((rows_here, columns), bf16),
        in_specs=[VMEM] * (2 + 2 * n_y),
        out_specs=VMEM,
        compiler_params=roomy,
        name="query_rows",
    )(spread, adapter_up_factors, *first_parts, *last_parts)


def solution(mesh):
    return jax.shard_map(
        body,
        mesh=mesh,
        in_specs=(
            P(("rep", "gx"), ("gy", "gz")),
            P(("gy", "gz")),
            P(("gy", "gz"), "gx"),
            P("gx", ("gy", "gz"), None),
            P(None, None, "gx"),
            P("rep"),
            P(),
            P(),
            P("rep"),
        ),
        out_specs=P(("rep", "gy", "gz"), "gx"),
        check_vma=False,
    )
```

```python
import functools

import jax
import jax.numpy as jnp
from jax import lax
from jax.experimental import pallas as pl
from jax.experimental.pallas import tpu as pltpu
from jax.sharding import PartitionSpec as P

EPSILON = 1e-05
ADAPTER_ALPHA = 32.0
LANES = 128
MIB = 1 << 20

VMEM = pl.BlockSpec(memory_space=pltpu.VMEM)
HBM = pl.BlockSpec(memory_space=pltpu.HBM)
ANY = pl.BlockSpec(memory_space=pl.ANY)


def params(mib):
    return pltpu.CompilerParams(vmem_limit_bytes=mib * MIB)


def cost(flops, moved):
    return pl.CostEstimate(flops=flops, bytes_accessed=moved, transcendentals=0)


def weight_copies(w_hbm, first, w_vmem, sems):
    pieces = sems.shape[0]
    depth, width = w_vmem.shape
    step = depth // pieces
    return [
        pltpu.make_async_copy(
            w_hbm.at[pl.ds(p * step, step), pl.ds(first, width)],
            w_vmem.at[pl.ds(p * step, step)],
            sems.at[p],
        )
        for p in range(pieces)
    ]


def load(w_hbm, first, weights, sems, meanwhile):
    copies = []
    for j, w_vmem in enumerate(weights):
        copies += weight_copies(w_hbm, first, w_vmem, sems.at[j])
        first += w_vmem.shape[1]
    for copy in copies:
        copy.start()
    meanwhile()
    for copy in copies:
        copy.wait()


def first_load_kernel(n, w_hbm, rank_hbm, slot_hbm, start_hbm, factor_ref, spread_ref, *refs):
    weights, sems, scalar_sems = refs[:n], refs[n], refs[n + 1]
    rank_ref, slot_ref, start_ref = refs[n + 2 :]

    def masks():
        pairs = ((rank_hbm, rank_ref), (slot_hbm, slot_ref), (start_hbm, start_ref))
        scalars = [
            pltpu.make_async_copy(source, target, scalar_sems.at[j])
            for j, (source, target) in enumerate(pairs)
        ]
        for copy in scalars:
            copy.start()
        for copy in scalars:
            copy.wait()
        slots, rows, rank_columns = factor_ref.shape
        home = lax.axis_index("gx")
        row = lax.broadcasted_iota(jnp.int32, (rows, rank_columns), 0)
        col = lax.broadcasted_iota(jnp.int32, (rows, rank_columns), 1)
        for s in range(slots):
            adapter = slot_ref[home * slots + s]
            rank = rank_ref[adapter]
            live = (row >= start_ref[adapter]) & (row < start_ref[adapter + 1]) & (col < rank)
            ranks = jnp.full((rows, rank_columns), rank, jnp.int32).astype(jnp.float32)
            factor_ref[s] = jnp.where(live, ADAPTER_ALPHA / ranks, 0.0)
        adapters = spread_ref.shape[1] // rank_columns
        for a in range(adapters):
            live = (row >= start_ref[a]) & (row < start_ref[a + 1])
            spread_ref[:, a * rank_columns : (a + 1) * rank_columns] = jnp.where(live, 1.0, 0.0)

    load(w_hbm, 0, weights, sems, masks)


def last_load_kernel(n, first, w_hbm, _, __, *refs):
    load(w_hbm, first, refs[:n], refs[n], lambda: None)


def split_wide(value):
    high = value.astype(jnp.bfloat16).astype(jnp.float32)
    low = jnp.where(high < jnp.inf, value - high, 0.0)
    lane = lax.broadcasted_iota(jnp.int32, value.shape, 1)
    return jnp.where(lane < LANES // 2, high, low)


def join_wide(value):
    return value[:, :1] + value[:, LANES - 1 :]


def rows_kernel(order, width, gain_ref, down_ref, factor_ref, *refs):
    n = len(order)
    blocks = refs[:n]
    x_ref, small_ref = refs[n:]
    home = lax.axis_index("gx")
    block_rows = blocks[0].shape[0]
    gain = gain_ref[...].astype(jnp.float32).reshape(1, gain_ref.shape[0])
    small_ref[...] = jnp.zeros(small_ref.shape, small_ref.dtype)
    for k, block in zip(order, blocks):
        begin = pl.multiple_of(jnp.bitwise_xor(home, k) * block_rows, block_rows)
        values = block[...].astype(jnp.float32)
        x_ref[pl.ds(begin, block_rows), :] = (values * gain).astype(jnp.bfloat16)
        if k == 0:
            squares = jnp.sum(values * values, axis=1, keepdims=True) / width
            squares = split_wide(jnp.broadcast_to(squares, (block_rows, LANES)))
            small_ref[pl.ds(begin, block_rows), LANES:] = squares.astype(jnp.bfloat16)
    slots, rows, rank_columns = factor_ref.shape
    total = jnp.zeros((rows, rank_columns), jnp.float32)
    for s in range(slots):
        projected = lax.dot_general(
            x_ref[...], down_ref[s], (((1,), (1,)), ((), ())), preferred_element_type=jnp.float32
        )
        factor = factor_ref[s]
        total = total + jnp.where(factor > 0, projected * factor, 0.0)
    small_ref[:, :rank_columns] = total.astype(small_ref.dtype)


def write_rows(acc, outs, n_y, n_z):
    z = lax.axis_index("gz")
    rows_here = outs[0].shape[0] // n_y
    for k in range(n_z):
        for y in range(n_y):
            owner = y * n_z + jnp.bitwise_xor(z, k)
            begin = pl.multiple_of(owner * rows_here, rows_here)
            outs[k][y * rows_here : (y + 1) * rows_here, :] = acc[
                pl.ds(begin, rows_here), :
            ].astype(outs[k].dtype)


def multiply(x_ref, weights, step, out, first):
    for weight in weights:
        width = weight.shape[1]
        wide = min(step, width)
        for c in range(0, width, wide):
            out[:, first + c : first + c + wide] = jnp.dot(
                x_ref[...], weight[:, c : c + wide], preferred_element_type=jnp.float32
            )
        first += width


def base_kernel(n_w, first, step, w_hbm, x_ref, *refs):
    weights, out_ref, rest = refs[:n_w], refs[n_w], refs[n_w + 1 :]
    copies = weight_copies(w_hbm, first, *rest) if rest else []
    for copy in copies:
        copy.start()

    @pl.when(lax.axis_index("gx") >= 0)
    def behind_the_copies():
        multiply(x_ref, weights, step, out_ref, 0)

    for copy in copies:
        copy.wait()


def last_kernel(n_w, step, x_ref, *refs):
    multiply(x_ref, refs[:n_w], step, refs[n_w], 0)


def product_kernel(n_w, n_y, n_z, step, first, x_ref, *refs):
    if first:
        base_ref, refs = refs[0], refs[2:]
    weights, outs, acc = refs[:n_w], refs[n_w:-1], refs[-1]
    if first:
        acc[:, :first] = base_ref[...]
    multiply(x_ref, weights, step, acc, first)
    write_rows(acc, outs, n_y, n_z)


def first_sums_kernel(n_y, n_z, last_ref, small_ref, *refs):
    parts, outs, last_outs = refs[:n_z], refs[n_z : n_z + n_y], refs[n_z + n_y :]
    pair_kernel(n_y, False, *parts, *outs)
    columns = last_ref.shape[1]
    write_rows(last_ref, [out.at[:, :columns] for out in last_outs], n_y, n_z)
    write_rows(small_ref, [out.at[:, columns:] for out in last_outs], n_y, n_z)


def pair_kernel(n_y, side, *refs):
    parts, outs = refs[:-n_y], refs[-n_y:]
    rows_here, columns = outs[0].shape
    late = columns - (LANES if side else 0)
    y = lax.axis_index("gy")
    for k in range(n_y):
        begin = pl.multiple_of(jnp.bitwise_xor(y, k) * rows_here, rows_here)
        here = pl.ds(begin, rows_here)
        total = parts[0][here, :].astype(jnp.float32)
        for part in parts[1:]:
            total = total + part[here, :].astype(jnp.float32)
        outs[k][:, :late] = total[:, :late].astype(outs[k].dtype)
        if side:
            square = jnp.broadcast_to(join_wide(total[:, late:]), (rows_here, LANES))
            outs[k][:, late:] = split_wide(square).astype(outs[k].dtype)


def final_kernel(n, n_z, step, spread_ref, up_ref, *refs):
    firsts, lasts, out_ref = refs[:n], refs[n : 2 * n], refs[2 * n]
    rows_here, columns = out_ref.shape
    done = firsts[0].shape[1]
    late = columns - done
    adapters, rank_columns, _ = up_ref.shape

    def added(parts, begin, end):
        total = parts[0][:, begin:end]
        for part in parts[1:]:
            total = total + part[:, begin:end].astype(jnp.float32)
        return total

    side = added(lasts, late, late + 2 * LANES)
    mean_sq = join_wide(side[:, LANES:])
    scale = lax.rsqrt(mean_sq + EPSILON)
    owner = lax.axis_index("gy") * n_z + lax.axis_index("gz")
    live = spread_ref[pl.ds(pl.multiple_of(owner * rows_here, rows_here), rows_here), :]
    spread = jnp.concatenate([side[:, :rank_columns]] * adapters, axis=1)
    spread = jnp.where(live > 0, spread, 0.0).astype(jnp.bfloat16)
    for c in range(0, columns, step):
        if c < done:
            base = added(firsts, c, c + step)
        else:
            base = added(lasts, c - done, c - done + step)
        up = up_ref[:, :, c : c + step].reshape(adapters * rank_columns, step)
        total = base + jnp.dot(spread, up, preferred_element_type=jnp.float32)
        value = jnp.where(mean_sq < jnp.inf, total * scale, 0.0)
        out_ref[:, c : c + step] = value.astype(out_ref.dtype)


def body(
    hidden,
    attention_norm_gain,
    query_weight,
    slot_down_factors,
    adapter_up_factors,
    adapter_of_row,
    padded_adapter_rank,
    adapter_in_slot,
    segment_starts,
):
    n_x, n_y, n_z = lax.axis_size("gx"), lax.axis_size("gy"), lax.axis_size("gz")
    groups = n_y * n_z
    block_rows, depth = hidden.shape
    columns = query_weight.shape[1]
    rows = n_x * block_rows
    rows_here = rows // groups

    def send(value, axis, n, k):
        return lax.ppermute(value, axis, [(j, j ^ k) for j in range(n)])

    def spread_out(made, axis, n):
        return [made[0]] + [send(made[k], axis, n, k) for k in range(1, n)]

    sent = {0: hidden}
    order = [0, *range(2, n_x, 2), 1, *range(3, n_x, 2)]
    for k in order[1:]:
        sent[k] = send(sent[k - 1], "gx", n_x, 1) if k % 2 else send(hidden, "gx", n_x, k)
    blocks = [sent[k] for k in order]

    step = min(1024, columns // 4)
    pieces = 8
    f32, bf16 = jnp.float32, jnp.bfloat16
    slots, rank_columns = slot_down_factors.shape[0], slot_down_factors.shape[2]
    adapters = adapter_up_factors.shape[0]
    quarter = columns // 4
    part = quarter // 4
    if part % LANES == 0:
        loads, late = ([quarter, quarter], [quarter, part]), quarter - part
    else:
        loads, late = ([quarter, quarter], [quarter, quarter]), 0
    kept = n_y * rows_here
    roomy = params(4 + (rows * depth >> 16))

    scalars = (padded_adapter_rank, adapter_in_slot, segment_starts)
    weight_hbm = pltpu.with_memory_space_constraint(query_weight, pltpu.HBM)
    load_cost = cost(300 * query_weight.size, query_weight.size)
    factor, spread, *weights = pl.pallas_call(
        functools.partial(first_load_kernel, len(loads[0])),
        out_shape=[
            jax.ShapeDtypeStruct((slots, rows, rank_columns), f32),
            jax.ShapeDtypeStruct((rows, adapters * rank_columns), f32),
        ]
        + [pltpu.VMEM((depth, wide), query_weight.dtype) for wide in loads[0]],
        in_specs=[HBM] * 4,
        out_specs=[VMEM] * (2 + len(loads[0])),
        scratch_shapes=[
            pltpu.SemaphoreType.DMA((len(loads[0]), pieces)),
            pltpu.SemaphoreType.DMA((len(scalars),)),
            *[pltpu.SMEM(value.shape, value.dtype) for value in scalars],
        ],
        cost_estimate=load_cost,
        compiler_params=roomy,
        name="first_load",
    )(weight_hbm, *[pltpu.with_memory_space_constraint(v, pltpu.HBM) for v in scalars])
    weights += pl.pallas_call(
        functools.partial(last_load_kernel, len(loads[1]), sum(loads[0])),
        out_shape=[pltpu.VMEM((depth, wide), query_weight.dtype) for wide in loads[1]],
        in_specs=[HBM, ANY, ANY],
        out_specs=[VMEM] * len(loads[1]),
        scratch_shapes=[pltpu.SemaphoreType.DMA((len(loads[1]), pieces))],
        cost_estimate=load_cost,
        compiler_params=roomy,
        name="last_load",
    )(weight_hbm, factor, blocks[1])
    weights = [pltpu.with_memory_space_constraint(w, pltpu.VMEM) for w in weights]

    x, small = pl.pallas_call(
        functools.partial(rows_kernel, order, depth * groups),
        out_shape=(
            jax.ShapeDtypeStruct((rows, depth), bf16),
            jax.ShapeDtypeStruct((rows, 2 * LANES), bf16),
        ),
        in_specs=[VMEM] * (3 + n_x),
        out_specs=(VMEM,) * 2,
        compiler_params=roomy,
        name="scaled_rows",
    )(attention_norm_gain, jnp.swapaxes(slot_down_factors, 1, 2), factor, *blocks)

    one_hop = small = small + send(small, "gx", n_x, 1)
    hop = 2
    while hop < n_x:
        small = small + send(small, "gx", n_x, hop)
        hop *= 2

    def shapes(n, shape):
        return [jax.ShapeDtypeStruct(shape, f32 if k == 0 else bf16) for k in range(n)]

    base, *rest = pl.pallas_call(
        functools.partial(base_kernel, 2, columns - late, step),
        out_shape=[jax.ShapeDtypeStruct((rows, 2 * quarter), f32)]
        + ([pltpu.VMEM((depth, late), query_weight.dtype)] if late else []),
        in_specs=[HBM] + [VMEM] * 3,
        out_specs=[VMEM] * (2 if late else 1),
        scratch_shapes=[pltpu.SemaphoreType.DMA((pieces,))] if late else [],
        cost_estimate=cost(4 * rows * depth * quarter, 4 * depth * quarter),
        compiler_params=roomy,
        name="first_columns",
    )(weight_hbm, x, *weights[:2])
    weights += [pltpu.with_memory_space_constraint(w, pltpu.VMEM) for w in rest]

    def product(some, bases, times, name):
        first = sum(part.shape[1] for part in bases[:1])
        wide = first + sum(w.shape[1] for w in some)
        made = pl.pallas_call(
            functools.partial(product_kernel, len(some), n_y, n_z, step, first),
            out_shape=shapes(n_z, (kept, wide)),
            in_specs=[VMEM] * (1 + len(bases) + len(some)),
            out_specs=[VMEM] * n_z,
            scratch_shapes=[pltpu.VMEM((rows, wide), f32)],
            cost_estimate=cost(2 * rows * depth * wide * times, 2 * depth * wide),
            compiler_params=roomy,
            name=name,
        )(x, *bases, *some)
        return spread_out(made, "gz", n_z)

    split = 3
    last_columns = sum(w.shape[1] for w in weights[split:])
    firsts = product(weights[2:split], [base, one_hop], 4, "middle_columns")
    last = pl.pallas_call(
        functools.partial(last_kernel, len(weights) - split, step),
        out_shape=jax.ShapeDtypeStruct((rows, last_columns), f32),
        in_specs=[VMEM] * (len(weights) - split + 1),
        out_specs=VMEM,
        cost_estimate=cost(16 * rows * depth * quarter, 2 * depth * quarter),
        compiler_params=roomy,
        name="last_columns",
    )(x, *weights[split:])
    wide = firsts[0].shape[1]
    made = pl.pallas_call(
        functools.partial(first_sums_kernel, n_y, n_z),
        out_shape=shapes(n_y, (rows_here, wide)) + shapes(n_z, (kept, last_columns + 2 * LANES)),
        in_specs=[VMEM] * (2 + n_z),
        out_specs=[VMEM] * (n_y + n_z),
        cost_estimate=cost(0, 0),
        compiler_params=roomy,
        name="first_sums",
    )(last, small, *firsts)
    first_parts = spread_out(made[:n_y], "gy", n_y)
    lasts = spread_out(made[n_y:], "gz", n_z)

    made = pl.pallas_call(
        functools.partial(pair_kernel, n_y, True),
        out_shape=shapes(n_y, (rows_here, last_columns + 2 * LANES)),
        in_specs=[VMEM] * n_z,
        out_specs=[VMEM] * n_y,
        cost_estimate=cost(0, 0),
        compiler_params=roomy,
        name="last_sums",
    )(*lasts)
    last_parts = spread_out(made, "gy", n_y)

    return pl.pallas_call(
        functools.partial(final_kernel, n_y, n_z, min(512, columns // 4)),
        out_shape=jax.ShapeDtypeStruct((rows_here, columns), bf16),
        in_specs=[VMEM] * (2 + 2 * n_y),
        out_specs=VMEM,
        compiler_params=roomy,
        name="query_rows",
    )(spread, adapter_up_factors, *first_parts, *last_parts)


def solution(mesh):
    return jax.shard_map(
        body,
        mesh=mesh,
        in_specs=(
            P(("rep", "gx"), ("gy", "gz")),
            P(("gy", "gz")),
            P(("gy", "gz"), "gx"),
            P("gx", ("gy", "gz"), None),
            P(None, None, "gx"),
            P("rep"),
            P(),
            P(),
            P("rep"),
        ),
        out_specs=P(("rep", "gy", "gz"), "gx"),
        check_vma=False,
    )
```

```python
import functools

import jax
import jax.numpy as jnp
from jax import lax
from jax.experimental import pallas as pl
from jax.experimental.pallas import tpu as pltpu
from jax.sharding import PartitionSpec as P

EPSILON = 1e-05
ADAPTER_ALPHA = 32.0
LANES = 128
MIB = 1 << 20

VMEM = pl.BlockSpec(memory_space=pltpu.VMEM)
HBM = pl.BlockSpec(memory_space=pltpu.HBM)
ANY = pl.BlockSpec(memory_space=pl.ANY)


def params(mib):
    return pltpu.CompilerParams(vmem_limit_bytes=mib * MIB)


def cost(flops, moved):
    return pl.CostEstimate(flops=flops, bytes_accessed=moved, transcendentals=0)


def weight_copies(w_hbm, first, w_vmem, sems):
    pieces = sems.shape[0]
    depth, width = w_vmem.shape
    step = depth // pieces
    return [
        pltpu.make_async_copy(
            w_hbm.at[pl.ds(p * step, step), pl.ds(first, width)],
            w_vmem.at[pl.ds(p * step, step)],
            sems.at[p],
        )
        for p in range(pieces)
    ]


def load(w_hbm, first, weights, sems, meanwhile):
    copies = []
    for j, w_vmem in enumerate(weights):
        copies += weight_copies(w_hbm, first, w_vmem, sems.at[j])
        first += w_vmem.shape[1]
    for copy in copies:
        copy.start()
    meanwhile()
    for copy in copies:
        copy.wait()


def first_load_kernel(n, w_hbm, rank_hbm, slot_hbm, start_hbm, factor_ref, spread_ref, *refs):
    weights, sems, scalar_sems = refs[:n], refs[n], refs[n + 1]
    rank_ref, slot_ref, start_ref = refs[n + 2 :]

    def masks():
        pairs = ((rank_hbm, rank_ref), (slot_hbm, slot_ref), (start_hbm, start_ref))
        scalars = [
            pltpu.make_async_copy(source, target, scalar_sems.at[j])
            for j, (source, target) in enumerate(pairs)
        ]
        for copy in scalars:
            copy.start()
        for copy in scalars:
            copy.wait()
        slots, rows, rank_columns = factor_ref.shape
        home = lax.axis_index("gx")
        row = lax.broadcasted_iota(jnp.int32, (rows, rank_columns), 0)
        col = lax.broadcasted_iota(jnp.int32, (rows, rank_columns), 1)
        for s in range(slots):
            adapter = slot_ref[home * slots + s]
            rank = rank_ref[adapter]
            live = (row >= start_ref[adapter]) & (row < start_ref[adapter + 1]) & (col < rank)
            ranks = jnp.full((rows, rank_columns), rank, jnp.int32).astype(jnp.float32)
            factor_ref[s] = jnp.where(live, ADAPTER_ALPHA / ranks, 0.0)
        adapters = spread_ref.shape[1] // rank_columns
        for a in range(adapters):
            live = (row >= start_ref[a]) & (row < start_ref[a + 1])
            spread_ref[:, a * rank_columns : (a + 1) * rank_columns] = jnp.where(live, 1.0, 0.0)

    load(w_hbm, 0, weights, sems, masks)


def last_load_kernel(n, first, w_hbm, _, __, *refs):
    load(w_hbm, first, refs[:n], refs[n], lambda: None)


def split_wide(value):
    high = value.astype(jnp.bfloat16).astype(jnp.float32)
    low = jnp.where(high < jnp.inf, value - high, 0.0)
    lane = lax.broadcasted_iota(jnp.int32, value.shape, 1)
    return jnp.where(lane < LANES // 2, high, low)


def join_wide(value):
    return value[:, :1] + value[:, LANES - 1 :]


def rows_kernel(order, width, gain_ref, down_ref, factor_ref, *refs):
    n = len(order)
    blocks = refs[:n]
    x_ref, small_ref = refs[n:]
    home = lax.axis_index("gx")
    block_rows = blocks[0].shape[0]
    gain = gain_ref[...].astype(jnp.float32).reshape(1, gain_ref.shape[0])
    small_ref[...] = jnp.zeros(small_ref.shape, small_ref.dtype)
    for k, block in zip(order, blocks):
        begin = pl.multiple_of(jnp.bitwise_xor(home, k) * block_rows, block_rows)
        values = block[...].astype(jnp.float32)
        x_ref[pl.ds(begin, block_rows), :] = (values * gain).astype(jnp.bfloat16)
        if k == 0:
            squares = jnp.sum(values * values, axis=1, keepdims=True) / width
            squares = split_wide(jnp.broadcast_to(squares, (block_rows, LANES)))
            small_ref[pl.ds(begin, block_rows), LANES:] = squares.astype(jnp.bfloat16)
    slots, rows, rank_columns = factor_ref.shape
    total = jnp.zeros((rows, rank_columns), jnp.float32)
    for s in range(slots):
        projected = lax.dot_general(
            x_ref[...], down_ref[s], (((1,), (1,)), ((), ())), preferred_element_type=jnp.float32
        )
        factor = factor_ref[s]
        total = total + jnp.where(factor > 0, projected * factor, 0.0)
    small_ref[:, :rank_columns] = total.astype(small_ref.dtype)


def write_rows(acc, outs, n_y, n_z):
    z = lax.axis_index("gz")
    rows_here = outs[0].shape[0] // n_y
    for k in range(n_z):
        for y in range(n_y):
            owner = y * n_z + jnp.bitwise_xor(z, k)
            begin = pl.multiple_of(owner * rows_here, rows_here)
            outs[k][y * rows_here : (y + 1) * rows_here, :] = acc[
                pl.ds(begin, rows_here), :
            ].astype(outs[k].dtype)


def multiply(x_ref, weights, step, out, first):
    for weight in weights:
        width = weight.shape[1]
        wide = min(step, width)
        for c in range(0, width, wide):
            out[:, first + c : first + c + wide] = jnp.dot(
                x_ref[...], weight[:, c : c + wide], preferred_element_type=jnp.float32
            )
        first += width


def base_kernel(n_w, first, step, w_hbm, x_ref, *refs):
    weights, out_ref, rest = refs[:n_w], refs[n_w], refs[n_w + 1 :]
    copies = weight_copies(w_hbm, first, *rest) if rest else []
    for copy in copies:
        copy.start()

    @pl.when(lax.axis_index("gx") >= 0)
    def behind_the_copies():
        multiply(x_ref, weights, step, out_ref, 0)

    for copy in copies:
        copy.wait()


def last_kernel(n_w, step, x_ref, *refs):
    multiply(x_ref, refs[:n_w], step, refs[n_w], 0)


def product_kernel(n_w, n_y, n_z, step, first, x_ref, *refs):
    if first:
        base_ref, refs = refs[0], refs[2:]
    weights, outs, acc = refs[:n_w], refs[n_w:-1], refs[-1]
    if first:
        acc[:, :first] = base_ref[...]
    multiply(x_ref, weights, step, acc, first)
    write_rows(acc, outs, n_y, n_z)


def pack_kernel(n_y, n_z, last_ref, small_ref, *outs):
    columns = last_ref.shape[1]
    write_rows(last_ref, [out.at[:, :columns] for out in outs], n_y, n_z)
    write_rows(small_ref, [out.at[:, columns:] for out in outs], n_y, n_z)


def first_sums_kernel(n_y, _, *refs):
    pair_kernel(n_y, False, *refs)


def add_kernel(*refs):
    total = refs[0][...]
    for part in refs[1:-1]:
        total = total + part[...].astype(jnp.float32)
    refs[-1][...] = total


def pair_kernel(n_y, side, *refs):
    parts, outs = refs[:-n_y], refs[-n_y:]
    rows_here, columns = outs[0].shape
    late = columns - (LANES if side else 0)
    y = lax.axis_index("gy")
    for k in range(n_y):
        begin = pl.multiple_of(jnp.bitwise_xor(y, k) * rows_here, rows_here)
        here = pl.ds(begin, rows_here)
        total = parts[0][here, :].astype(jnp.float32)
        for part in parts[1:]:
            total = total + part[here, :].astype(jnp.float32)
        outs[k][:, :late] = total[:, :late].astype(outs[k].dtype)
        if side:
            square = jnp.broadcast_to(join_wide(total[:, late:]), (rows_here, LANES))
            outs[k][:, late:] = split_wide(square).astype(outs[k].dtype)


def final_kernel(n_z, step, spread_ref, up_ref, first_ref, *refs):
    lasts, out_ref = refs[:-1], refs[-1]
    rows_here, columns = out_ref.shape
    done = first_ref.shape[1]
    late = columns - done
    adapters, rank_columns, _ = up_ref.shape

    def added(parts, begin, end):
        total = parts[0][:, begin:end]
        for part in parts[1:]:
            total = total + part[:, begin:end].astype(jnp.float32)
        return total

    side = added(lasts, late, late + 2 * LANES)
    mean_sq = join_wide(side[:, LANES:])
    scale = lax.rsqrt(mean_sq + EPSILON)
    owner = lax.axis_index("gy") * n_z + lax.axis_index("gz")
    live = spread_ref[pl.ds(pl.multiple_of(owner * rows_here, rows_here), rows_here), :]
    spread = jnp.concatenate([side[:, :rank_columns]] * adapters, axis=1)
    spread = jnp.where(live > 0, spread, 0.0).astype(jnp.bfloat16)
    for c in range(0, columns, step):
        if c < done:
            base = first_ref[:, c : c + step]
        else:
            base = added(lasts, c - done, c - done + step)
        up = up_ref[:, :, c : c + step].reshape(adapters * rank_columns, step)
        total = base + jnp.dot(spread, up, preferred_element_type=jnp.float32)
        value = jnp.where(mean_sq < jnp.inf, total * scale, 0.0)
        out_ref[:, c : c + step] = value.astype(out_ref.dtype)


def body(
    hidden,
    attention_norm_gain,
    query_weight,
    slot_down_factors,
    adapter_up_factors,
    adapter_of_row,
    padded_adapter_rank,
    adapter_in_slot,
    segment_starts,
):
    n_x, n_y, n_z = lax.axis_size("gx"), lax.axis_size("gy"), lax.axis_size("gz")
    groups = n_y * n_z
    block_rows, depth = hidden.shape
    columns = query_weight.shape[1]
    rows = n_x * block_rows
    rows_here = rows // groups

    def send(value, axis, n, k):
        return lax.ppermute(value, axis, [(j, j ^ k) for j in range(n)])

    def spread_out(made, axis, n):
        return [made[0]] + [send(made[k], axis, n, k) for k in range(1, n)]

    sent = {0: hidden}
    order = [0, *range(2, n_x, 2), 1, *range(3, n_x, 2)]
    for k in order[1:]:
        sent[k] = send(sent[k - 1], "gx", n_x, 1) if k % 2 else send(hidden, "gx", n_x, k)
    blocks = [sent[k] for k in order]

    step = min(1024, columns // 4)
    pieces = 8
    f32, bf16 = jnp.float32, jnp.bfloat16
    slots, rank_columns = slot_down_factors.shape[0], slot_down_factors.shape[2]
    adapters = adapter_up_factors.shape[0]
    quarter = columns // 4
    part = quarter // 4
    if part % LANES == 0:
        loads, late = ([quarter, quarter], [quarter, part]), quarter - part
    else:
        loads, late = ([quarter, quarter], [quarter, quarter]), 0
    kept = n_y * rows_here
    roomy = params(4 + (rows * depth >> 16))

    scalars = (padded_adapter_rank, adapter_in_slot, segment_starts)
    weight_hbm = pltpu.with_memory_space_constraint(query_weight, pltpu.HBM)
    load_cost = cost(300 * query_weight.size, query_weight.size)
    factor, spread, *weights = pl.pallas_call(
        functools.partial(first_load_kernel, len(loads[0])),
        out_shape=[
            jax.ShapeDtypeStruct((slots, rows, rank_columns), f32),
            jax.ShapeDtypeStruct((rows, adapters * rank_columns), f32),
        ]
        + [pltpu.VMEM((depth, wide), query_weight.dtype) for wide in loads[0]],
        in_specs=[HBM] * 4,
        out_specs=[VMEM] * (2 + len(loads[0])),
        scratch_shapes=[
            pltpu.SemaphoreType.DMA((len(loads[0]), pieces)),
            pltpu.SemaphoreType.DMA((len(scalars),)),
            *[pltpu.SMEM(value.shape, value.dtype) for value in scalars],
        ],
        cost_estimate=load_cost,
        compiler_params=roomy,
        name="first_load",
    )(weight_hbm, *[pltpu.with_memory_space_constraint(v, pltpu.HBM) for v in scalars])
    weights += pl.pallas_call(
        functools.partial(last_load_kernel, len(loads[1]), sum(loads[0])),
        out_shape=[pltpu.VMEM((depth, wide), query_weight.dtype) for wide in loads[1]],
        in_specs=[HBM, ANY, ANY],
        out_specs=[VMEM] * len(loads[1]),
        scratch_shapes=[pltpu.SemaphoreType.DMA((len(loads[1]), pieces))],
        cost_estimate=load_cost,
        compiler_params=roomy,
        name="last_load",
    )(weight_hbm, factor, blocks[1])
    weights = [pltpu.with_memory_space_constraint(w, pltpu.VMEM) for w in weights]

    x, small = pl.pallas_call(
        functools.partial(rows_kernel, order, depth * groups),
        out_shape=(
            jax.ShapeDtypeStruct((rows, depth), bf16),
            jax.ShapeDtypeStruct((rows, 2 * LANES), bf16),
        ),
        in_specs=[VMEM] * (3 + n_x),
        out_specs=(VMEM,) * 2,
        compiler_params=roomy,
        name="scaled_rows",
    )(attention_norm_gain, jnp.swapaxes(slot_down_factors, 1, 2), factor, *blocks)

    one_hop = small = small + send(small, "gx", n_x, 1)
    hop = 2
    while hop < n_x:
        small = small + send(small, "gx", n_x, hop)
        hop *= 2

    def shapes(n, shape):
        return [jax.ShapeDtypeStruct(shape, f32 if k == 0 else bf16) for k in range(n)]

    base, *rest = pl.pallas_call(
        functools.partial(base_kernel, 2, columns - late, step),
        out_shape=[jax.ShapeDtypeStruct((rows, 2 * quarter), f32)]
        + ([pltpu.VMEM((depth, late), query_weight.dtype)] if late else []),
        in_specs=[HBM] + [VMEM] * 3,
        out_specs=[VMEM] * (2 if late else 1),
        scratch_shapes=[pltpu.SemaphoreType.DMA((pieces,))] if late else [],
        cost_estimate=cost(4 * rows * depth * quarter, 4 * depth * quarter),
        compiler_params=roomy,
        name="first_columns",
    )(weight_hbm, x, *weights[:2])
    weights += [pltpu.with_memory_space_constraint(w, pltpu.VMEM) for w in rest]

    def product(some, bases, times, name):
        first = sum(part.shape[1] for part in bases[:1])
        wide = first + sum(w.shape[1] for w in some)
        made = pl.pallas_call(
            functools.partial(product_kernel, len(some), n_y, n_z, step, first),
            out_shape=shapes(n_z, (kept, wide)),
            in_specs=[VMEM] * (1 + len(bases) + len(some)),
            out_specs=[VMEM] * n_z,
            scratch_shapes=[pltpu.VMEM((rows, wide), f32)],
            cost_estimate=cost(2 * rows * depth * wide * times, 2 * depth * wide),
            compiler_params=roomy,
            name=name,
        )(x, *bases, *some)
        return spread_out(made, "gz", n_z)

    split = 3
    last_columns = sum(w.shape[1] for w in weights[split:])
    firsts = product(weights[2:split], [base, one_hop], 4, "middle_columns")
    last = pl.pallas_call(
        functools.partial(last_kernel, len(weights) - split, step),
        out_shape=jax.ShapeDtypeStruct((rows, last_columns), f32),
        in_specs=[VMEM] * (len(weights) - split + 1),
        out_specs=VMEM,
        cost_estimate=cost(16 * rows * depth * quarter, 2 * depth * quarter),
        compiler_params=roomy,
        name="last_columns",
    )(x, *weights[split:])
    wide = firsts[0].shape[1]
    made = pl.pallas_call(
        functools.partial(first_sums_kernel, n_y),
        out_shape=shapes(n_y, (rows_here, wide)),
        in_specs=[ANY] + [VMEM] * n_z,
        out_specs=[VMEM] * n_y,
        cost_estimate=cost(0, 0),
        compiler_params=roomy,
        name="first_sums",
    )(last, *firsts)
    first_parts = spread_out(made, "gy", n_y)

    made = pl.pallas_call(
        functools.partial(pack_kernel, n_y, n_z),
        out_shape=shapes(n_z, (kept, last_columns + 2 * LANES)),
        in_specs=[VMEM] * 2,
        out_specs=[VMEM] * n_z,
        cost_estimate=cost(0, 0),
        compiler_params=roomy,
        name="pack_last",
    )(last, small)
    lasts = spread_out(made, "gz", n_z)

    made = pl.pallas_call(
        functools.partial(pair_kernel, n_y, True),
        out_shape=shapes(n_y, (rows_here, last_columns + 2 * LANES)),
        in_specs=[VMEM] * n_z,
        out_specs=[VMEM] * n_y,
        cost_estimate=cost(0, 0),
        compiler_params=roomy,
        name="last_sums",
    )(*lasts)
    last_parts = spread_out(made, "gy", n_y)

    first_total = pl.pallas_call(
        add_kernel,
        out_shape=jax.ShapeDtypeStruct((rows_here, wide), f32),
        in_specs=[VMEM] * n_y,
        out_specs=VMEM,
        cost_estimate=cost(16 * rows * depth * quarter, 0),
        compiler_params=roomy,
        name="first_total",
    )(*first_parts)

    return pl.pallas_call(
        functools.partial(final_kernel, n_z, min(512, columns // 4)),
        out_shape=jax.ShapeDtypeStruct((rows_here, columns), bf16),
        in_specs=[VMEM] * (3 + n_y),
        out_specs=VMEM,
        compiler_params=roomy,
        name="query_rows",
    )(spread, adapter_up_factors, first_total, *last_parts)


def solution(mesh):
    return jax.shard_map(
        body,
        mesh=mesh,
        in_specs=(
            P(("rep", "gx"), ("gy", "gz")),
            P(("gy", "gz")),
            P(("gy", "gz"), "gx"),
            P("gx", ("gy", "gz"), None),
            P(None, None, "gx"),
            P("rep"),
            P(),
            P(),
            P("rep"),
        ),
        out_specs=P(("rep", "gy", "gz"), "gx"),
        check_vma=False,
    )
```

```python
import functools

import jax
import jax.numpy as jnp
from jax import lax
from jax.experimental import pallas as pl
from jax.experimental.pallas import tpu as pltpu
from jax.sharding import PartitionSpec as P

EPSILON = 1e-05
ADAPTER_ALPHA = 32.0
LANES = 128
MIB = 1 << 20

VMEM = pl.BlockSpec(memory_space=pltpu.VMEM)
HBM = pl.BlockSpec(memory_space=pltpu.HBM)
ANY = pl.BlockSpec(memory_space=pl.ANY)


def params(mib):
    return pltpu.CompilerParams(vmem_limit_bytes=mib * MIB)


def cost(flops, moved):
    return pl.CostEstimate(flops=flops, bytes_accessed=moved, transcendentals=0)


def weight_copies(w_hbm, first, w_vmem, sems):
    pieces = sems.shape[0]
    depth, width = w_vmem.shape
    step = depth // pieces
    return [
        pltpu.make_async_copy(
            w_hbm.at[pl.ds(p * step, step), pl.ds(first, width)],
            w_vmem.at[pl.ds(p * step, step)],
            sems.at[p],
        )
        for p in range(pieces)
    ]


def load(w_hbm, firsts, weights, sems, meanwhile):
    copies = []
    for j, w_vmem in enumerate(weights):
        copies += weight_copies(w_hbm, firsts[j], w_vmem, sems.at[j])
    for copy in copies:
        copy.start()
    meanwhile()
    for copy in copies:
        copy.wait()


def first_load_kernel(n, firsts, w_hbm, rank_hbm, slot_hbm, start_hbm, factor_ref, spread_ref, *refs):
    weights, sems, scalar_sems = refs[:n], refs[n], refs[n + 1]
    rank_ref, slot_ref, start_ref = refs[n + 2 :]

    def masks():
        pairs = ((rank_hbm, rank_ref), (slot_hbm, slot_ref), (start_hbm, start_ref))
        scalars = [
            pltpu.make_async_copy(source, target, scalar_sems.at[j])
            for j, (source, target) in enumerate(pairs)
        ]
        for copy in scalars:
            copy.start()
        for copy in scalars:
            copy.wait()
        slots, rows, rank_columns = factor_ref.shape
        home = lax.axis_index("gx")
        row = lax.broadcasted_iota(jnp.int32, (rows, rank_columns), 0)
        col = lax.broadcasted_iota(jnp.int32, (rows, rank_columns), 1)
        for s in range(slots):
            adapter = slot_ref[home * slots + s]
            rank = rank_ref[adapter]
            live = (row >= start_ref[adapter]) & (row < start_ref[adapter + 1]) & (col < rank)
            ranks = jnp.full((rows, rank_columns), rank, jnp.int32).astype(jnp.float32)
            factor_ref[s] = jnp.where(live, ADAPTER_ALPHA / ranks, 0.0)
        adapters = spread_ref.shape[1] // rank_columns
        for a in range(adapters):
            live = (row >= start_ref[a]) & (row < start_ref[a + 1])
            spread_ref[:, a * rank_columns : (a + 1) * rank_columns] = jnp.where(live, 1.0, 0.0)

    load(w_hbm, firsts, weights, sems, masks)


def last_load_kernel(n, firsts, w_hbm, _, __, *refs):
    load(w_hbm, firsts, refs[:n], refs[n], lambda: None)


def split_wide(value):
    high = value.astype(jnp.bfloat16).astype(jnp.float32)
    low = jnp.where(high < jnp.inf, value - high, 0.0)
    lane = lax.broadcasted_iota(jnp.int32, value.shape, 1)
    return jnp.where(lane < LANES // 2, high, low)


def join_wide(value):
    return value[:, :1] + value[:, LANES - 1 :]


def rows_kernel(order, width, gain_ref, down_ref, factor_ref, *refs):
    n = len(order)
    blocks = refs[:n]
    x_ref, small_ref = refs[n:]
    home = lax.axis_index("gx")
    block_rows = blocks[0].shape[0]
    gain = gain_ref[...].astype(jnp.float32).reshape(1, gain_ref.shape[0])
    small_ref[...] = jnp.zeros(small_ref.shape, small_ref.dtype)
    for k, block in zip(order, blocks):
        begin = pl.multiple_of(jnp.bitwise_xor(home, k) * block_rows, block_rows)
        values = block[...].astype(jnp.float32)
        x_ref[pl.ds(begin, block_rows), :] = (values * gain).astype(jnp.bfloat16)
        if k == 0:
            squares = jnp.sum(values * values, axis=1, keepdims=True) / width
            squares = split_wide(jnp.broadcast_to(squares, (block_rows, LANES)))
            small_ref[pl.ds(begin, block_rows), LANES:] = squares.astype(jnp.bfloat16)
    slots, rows, rank_columns = factor_ref.shape
    total = jnp.zeros((rows, rank_columns), jnp.float32)
    for s in range(slots):
        projected = lax.dot_general(
            x_ref[...], down_ref[s], (((1,), (1,)), ((), ())), preferred_element_type=jnp.float32
        )
        factor = factor_ref[s]
        total = total + jnp.where(factor > 0, projected * factor, 0.0)
    small_ref[:, :rank_columns] = total.astype(small_ref.dtype)


def write_rows(acc, outs, n_y, n_z):
    z = lax.axis_index("gz")
    rows_here = outs[0].shape[0] // n_y
    for k in range(n_z):
        for y in range(n_y):
            owner = y * n_z + jnp.bitwise_xor(z, k)
            begin = pl.multiple_of(owner * rows_here, rows_here)
            outs[k][y * rows_here : (y + 1) * rows_here, :] = acc[
                pl.ds(begin, rows_here), :
            ].astype(outs[k].dtype)


def multiply(x_ref, weights, step, out, first):
    for weight in weights:
        width = weight.shape[1]
        wide = min(step, width)
        for c in range(0, width, wide):
            out[:, first + c : first + c + wide] = jnp.dot(
                x_ref[...], weight[:, c : c + wide], preferred_element_type=jnp.float32
            )
        first += width


def base_kernel(n_w, first, step, w_hbm, x_ref, *refs):
    weights, out_ref, rest = refs[:n_w], refs[n_w], refs[n_w + 1 :]
    copies = weight_copies(w_hbm, first, *rest) if rest else []
    for copy in copies:
        copy.start()

    @pl.when(lax.axis_index("gx") >= 0)
    def behind_the_copies():
        multiply(x_ref, weights, step, out_ref, 0)

    for copy in copies:
        copy.wait()


def last_kernel(n_w, step, x_ref, *refs):
    multiply(x_ref, refs[:n_w], step, refs[n_w], 0)


def product_kernel(n_w, n_y, n_z, step, first, x_ref, *refs):
    if first:
        base_ref, refs = refs[0], refs[2:]
    weights, outs, acc = refs[:n_w], refs[n_w:-1], refs[-1]
    if first:
        acc[:, :first] = base_ref[...]
    multiply(x_ref, weights, step, acc, first)
    write_rows(acc, outs, n_y, n_z)


def first_sums_kernel(n_y, n_z, last_ref, small_ref, *refs):
    parts, outs, last_outs = refs[:n_z], refs[n_z : n_z + n_y], refs[n_z + n_y :]
    pair_kernel(n_y, False, *parts, *outs)
    columns = last_ref.shape[1]
    write_rows(last_ref, [out.at[:, :columns] for out in last_outs], n_y, n_z)
    write_rows(small_ref, [out.at[:, columns:] for out in last_outs], n_y, n_z)


def pair_kernel(n_y, side, *refs):
    parts, outs = refs[:-n_y], refs[-n_y:]
    rows_here, columns = outs[0].shape
    late = columns - (LANES if side else 0)
    y = lax.axis_index("gy")
    for k in range(n_y):
        begin = pl.multiple_of(jnp.bitwise_xor(y, k) * rows_here, rows_here)
        here = pl.ds(begin, rows_here)
        total = parts[0][here, :].astype(jnp.float32)
        for part in parts[1:]:
            total = total + part[here, :].astype(jnp.float32)
        outs[k][:, :late] = total[:, :late].astype(outs[k].dtype)
        if side:
            square = jnp.broadcast_to(join_wide(total[:, late:]), (rows_here, LANES))
            outs[k][:, late:] = split_wide(square).astype(outs[k].dtype)


def final_kernel(n, n_z, step, spread_ref, up_ref, *refs):
    firsts, lasts, out_ref = refs[:n], refs[n : 2 * n], refs[2 * n]
    rows_here, columns = out_ref.shape
    done = firsts[0].shape[1]
    late = columns - done
    adapters, rank_columns, _ = up_ref.shape

    def added(parts, begin, end):
        total = parts[0][:, begin:end]
        for part in parts[1:]:
            total = total + part[:, begin:end].astype(jnp.float32)
        return total

    side = added(lasts, late, late + 2 * LANES)
    mean_sq = join_wide(side[:, LANES:])
    scale = lax.rsqrt(mean_sq + EPSILON)
    owner = lax.axis_index("gy") * n_z + lax.axis_index("gz")
    live = spread_ref[pl.ds(pl.multiple_of(owner * rows_here, rows_here), rows_here), :]
    spread = jnp.concatenate([side[:, :rank_columns]] * adapters, axis=1)
    spread = jnp.where(live > 0, spread, 0.0).astype(jnp.bfloat16)
    for c in range(0, columns, step):
        if c < done:
            base = added(firsts, c, c + step)
        else:
            base = added(lasts, c - done, c - done + step)
        up = up_ref[:, :, c : c + step].reshape(adapters * rank_columns, step)
        total = base + jnp.dot(spread, up, preferred_element_type=jnp.float32)
        value = jnp.where(mean_sq < jnp.inf, total * scale, 0.0)
        out_ref[:, c : c + step] = value.astype(out_ref.dtype)


def body(
    hidden,
    attention_norm_gain,
    query_weight,
    slot_down_factors,
    adapter_up_factors,
    adapter_of_row,
    padded_adapter_rank,
    adapter_in_slot,
    segment_starts,
):
    n_x, n_y, n_z = lax.axis_size("gx"), lax.axis_size("gy"), lax.axis_size("gz")
    groups = n_y * n_z
    block_rows, depth = hidden.shape
    columns = query_weight.shape[1]
    rows = n_x * block_rows
    rows_here = rows // groups

    def send(value, axis, n, k):
        return lax.ppermute(value, axis, [(j, j ^ k) for j in range(n)])

    def spread_out(made, axis, n):
        return [made[0]] + [send(made[k], axis, n, k) for k in range(1, n)]

    sent = {0: hidden}
    order = [0, *range(2, n_x, 2), 1, *range(3, n_x, 2)]
    for k in order[1:]:
        sent[k] = send(sent[k - 1], "gx", n_x, 1) if k % 2 else send(hidden, "gx", n_x, k)
    blocks = [sent[k] for k in order]

    step = min(1024, columns // 4)
    pieces = 8
    f32, bf16 = jnp.float32, jnp.bfloat16
    slots, rank_columns = slot_down_factors.shape[0], slot_down_factors.shape[2]
    adapters = adapter_up_factors.shape[0]
    quarter = columns // 4
    part = quarter // 4
    if part % LANES == 0:
        loads, late = ([quarter, quarter, part], [quarter]), quarter - part
        firsts = [0, quarter, 3 * quarter], [2 * quarter]
    else:
        loads, late = ([quarter, quarter], [quarter, quarter]), 0
        firsts = [0, quarter], [2 * quarter, 3 * quarter]
    kept = n_y * rows_here
    roomy = params(4 + (rows * depth >> 16))

    scalars = (padded_adapter_rank, adapter_in_slot, segment_starts)
    weight_hbm = pltpu.with_memory_space_constraint(query_weight, pltpu.HBM)
    load_cost = cost(300 * query_weight.size, query_weight.size)
    factor, spread, *weights = pl.pallas_call(
        functools.partial(first_load_kernel, len(loads[0]), firsts[0]),
        out_shape=[
            jax.ShapeDtypeStruct((slots, rows, rank_columns), f32),
            jax.ShapeDtypeStruct((rows, adapters * rank_columns), f32),
        ]
        + [pltpu.VMEM((depth, wide), query_weight.dtype) for wide in loads[0]],
        in_specs=[HBM] * 4,
        out_specs=[VMEM] * (2 + len(loads[0])),
        scratch_shapes=[
            pltpu.SemaphoreType.DMA((len(loads[0]), pieces)),
            pltpu.SemaphoreType.DMA((len(scalars),)),
            *[pltpu.SMEM(value.shape, value.dtype) for value in scalars],
        ],
        cost_estimate=load_cost,
        compiler_params=roomy,
        name="first_load",
    )(weight_hbm, *[pltpu.with_memory_space_constraint(v, pltpu.HBM) for v in scalars])
    weights += pl.pallas_call(
        functools.partial(last_load_kernel, len(loads[1]), firsts[1]),
        out_shape=[pltpu.VMEM((depth, wide), query_weight.dtype) for wide in loads[1]],
        in_specs=[HBM, ANY, ANY],
        out_specs=[VMEM] * len(loads[1]),
        scratch_shapes=[pltpu.SemaphoreType.DMA((len(loads[1]), pieces))],
        cost_estimate=load_cost,
        compiler_params=roomy,
        name="last_load",
    )(weight_hbm, factor, blocks[1])
    weights = [pltpu.with_memory_space_constraint(w, pltpu.VMEM) for w in weights]
    if late:
        weights[2:] = weights[:1:-1]

    x, small = pl.pallas_call(
        functools.partial(rows_kernel, order, depth * groups),
        out_shape=(
            jax.ShapeDtypeStruct((rows, depth), bf16),
            jax.ShapeDtypeStruct((rows, 2 * LANES), bf16),
        ),
        in_specs=[VMEM] * (3 + n_x),
        out_specs=(VMEM,) * 2,
        compiler_params=roomy,
        name="scaled_rows",
    )(attention_norm_gain, jnp.swapaxes(slot_down_factors, 1, 2), factor, *blocks)

    one_hop = small = small + send(small, "gx", n_x, 1)
    hop = 2
    while hop < n_x:
        small = small + send(small, "gx", n_x, hop)
        hop *= 2

    def shapes(n, shape):
        return [jax.ShapeDtypeStruct(shape, f32 if k == 0 else bf16) for k in range(n)]

    base, *rest = pl.pallas_call(
        functools.partial(base_kernel, 2, columns - late, step),
        out_shape=[jax.ShapeDtypeStruct((rows, 2 * quarter), f32)]
        + ([pltpu.VMEM((depth, late), query_weight.dtype)] if late else []),
        in_specs=[HBM] + [VMEM] * 3,
        out_specs=[VMEM] * (2 if late else 1),
        scratch_shapes=[pltpu.SemaphoreType.DMA((pieces,))] if late else [],
        cost_estimate=cost(4 * rows * depth * quarter, 4 * depth * quarter),
        compiler_params=roomy,
        name="first_columns",
    )(weight_hbm, x, *weights[:2])
    weights += [pltpu.with_memory_space_constraint(w, pltpu.VMEM) for w in rest]

    def product(some, bases, times, name):
        first = sum(part.shape[1] for part in bases[:1])
        wide = first + sum(w.shape[1] for w in some)
        made = pl.pallas_call(
            functools.partial(product_kernel, len(some), n_y, n_z, step, first),
            out_shape=shapes(n_z, (kept, wide)),
            in_specs=[VMEM] * (1 + len(bases) + len(some)),
            out_specs=[VMEM] * n_z,
            scratch_shapes=[pltpu.VMEM((rows, wide), f32)],
            cost_estimate=cost(2 * rows * depth * wide * times, 2 * depth * wide),
            compiler_params=roomy,
            name=name,
        )(x, *bases, *some)
        return spread_out(made, "gz", n_z)

    split = 3
    last_columns = sum(w.shape[1] for w in weights[split:])
    base_parts = product(weights[2:split], [base, one_hop], 4, "middle_columns")
    last = pl.pallas_call(
        functools.partial(last_kernel, len(weights) - split, step),
        out_shape=jax.ShapeDtypeStruct((rows, last_columns), f32),
        in_specs=[VMEM] * (len(weights) - split + 1),
        out_specs=VMEM,
        cost_estimate=cost(16 * rows * depth * quarter, 2 * depth * quarter),
        compiler_params=roomy,
        name="last_columns",
    )(x, *weights[split:])
    wide = base_parts[0].shape[1]
    made = pl.pallas_call(
        functools.partial(first_sums_kernel, n_y, n_z),
        out_shape=shapes(n_y, (rows_here, wide)) + shapes(n_z, (kept, last_columns + 2 * LANES)),
        in_specs=[VMEM] * (2 + n_z),
        out_specs=[VMEM] * (n_y + n_z),
        cost_estimate=cost(0, 0),
        compiler_params=roomy,
        name="first_sums",
    )(last, small, *base_parts)
    first_parts = spread_out(made[:n_y], "gy", n_y)
    lasts = spread_out(made[n_y:], "gz", n_z)

    made = pl.pallas_call(
        functools.partial(pair_kernel, n_y, True),
        out_shape=shapes(n_y, (rows_here, last_columns + 2 * LANES)),
        in_specs=[VMEM] * n_z,
        out_specs=[VMEM] * n_y,
        cost_estimate=cost(0, 0),
        compiler_params=roomy,
        name="last_sums",
    )(*lasts)
    last_parts = spread_out(made, "gy", n_y)

    return pl.pallas_call(
        functools.partial(final_kernel, n_y, n_z, min(512, columns // 4)),
        out_shape=jax.ShapeDtypeStruct((rows_here, columns), bf16),
        in_specs=[VMEM] * (2 + 2 * n_y),
        out_specs=VMEM,
        compiler_params=roomy,
        name="query_rows",
    )(spread, adapter_up_factors, *first_parts, *last_parts)


def solution(mesh):
    return jax.shard_map(
        body,
        mesh=mesh,
        in_specs=(
            P(("rep", "gx"), ("gy", "gz")),
            P(("gy", "gz")),
            P(("gy", "gz"), "gx"),
            P("gx", ("gy", "gz"), None),
            P(None, None, "gx"),
            P("rep"),
            P(),
            P(),
            P("rep"),
        ),
        out_specs=P(("rep", "gy", "gz"), "gx"),
        check_vma=False,
    )
```

```python
import functools

import jax
import jax.numpy as jnp
from jax import lax
from jax.experimental import pallas as pl
from jax.experimental.pallas import tpu as pltpu
from jax.sharding import PartitionSpec as P

EPSILON = 1e-05
ADAPTER_ALPHA = 32.0
LANES = 128
MIB = 1 << 20

VMEM = pl.BlockSpec(memory_space=pltpu.VMEM)
HBM = pl.BlockSpec(memory_space=pltpu.HBM)
ANY = pl.BlockSpec(memory_space=pl.ANY)


def params(mib):
    return pltpu.CompilerParams(vmem_limit_bytes=mib * MIB)


def cost(flops, moved):
    return pl.CostEstimate(flops=flops, bytes_accessed=moved, transcendentals=0)


def weight_copies(w_hbm, first, w_vmem, sems):
    pieces = sems.shape[0]
    depth, width = w_vmem.shape
    step = depth // pieces
    return [
        pltpu.make_async_copy(
            w_hbm.at[pl.ds(p * step, step), pl.ds(first, width)],
            w_vmem.at[pl.ds(p * step, step)],
            sems.at[p],
        )
        for p in range(pieces)
    ]


def load(w_hbm, firsts, weights, sems, meanwhile):
    copies = []
    for j, w_vmem in enumerate(weights):
        copies += weight_copies(w_hbm, firsts[j], w_vmem, sems.at[j])
    for copy in copies:
        copy.start()
    meanwhile()
    for copy in copies:
        copy.wait()


def first_load_kernel(n, firsts, w_hbm, rank_hbm, slot_hbm, start_hbm, factor_ref, spread_ref, *refs):
    weights, sems, scalar_sems = refs[:n], refs[n], refs[n + 1]
    rank_ref, slot_ref, start_ref = refs[n + 2 :]

    def masks():
        pairs = ((rank_hbm, rank_ref), (slot_hbm, slot_ref), (start_hbm, start_ref))
        scalars = [
            pltpu.make_async_copy(source, target, scalar_sems.at[j])
            for j, (source, target) in enumerate(pairs)
        ]
        for copy in scalars:
            copy.start()
        for copy in scalars:
            copy.wait()
        slots, rows, rank_columns = factor_ref.shape
        home = lax.axis_index("gx")
        row = lax.broadcasted_iota(jnp.int32, (rows, rank_columns), 0)
        col = lax.broadcasted_iota(jnp.int32, (rows, rank_columns), 1)
        for s in range(slots):
            adapter = slot_ref[home * slots + s]
            rank = rank_ref[adapter]
            live = (row >= start_ref[adapter]) & (row < start_ref[adapter + 1]) & (col < rank)
            ranks = jnp.full((rows, rank_columns), rank, jnp.int32).astype(jnp.float32)
            factor_ref[s] = jnp.where(live, ADAPTER_ALPHA / ranks, 0.0)
        adapters = spread_ref.shape[1] // rank_columns
        for a in range(adapters):
            live = (row >= start_ref[a]) & (row < start_ref[a + 1])
            spread_ref[:, a * rank_columns : (a + 1) * rank_columns] = jnp.where(live, 1.0, 0.0)

    load(w_hbm, firsts, weights, sems, masks)


def last_load_kernel(n, firsts, w_hbm, _, __, *refs):
    load(w_hbm, firsts, refs[:n], refs[n], lambda: None)


def split_wide(value):
    high = value.astype(jnp.bfloat16).astype(jnp.float32)
    low = jnp.where(high < jnp.inf, value - high, 0.0)
    lane = lax.broadcasted_iota(jnp.int32, value.shape, 1)
    return jnp.where(lane < value.shape[1] // 2, high, low)


def join_wide(value):
    return value[:, :1] + value[:, value.shape[1] - 1 :]


def rows_kernel(order, width, gain_ref, down_ref, factor_ref, *refs):
    n = len(order)
    blocks = refs[:n]
    x_ref, small_ref = refs[n:]
    home = lax.axis_index("gx")
    block_rows = blocks[0].shape[0]
    gain = gain_ref[...].astype(jnp.float32).reshape(1, gain_ref.shape[0])
    for k, block in zip(order, blocks):
        begin = pl.multiple_of(jnp.bitwise_xor(home, k) * block_rows, block_rows)
        values = block[...].astype(jnp.float32)
        x_ref[pl.ds(begin, block_rows), :] = (values * gain).astype(jnp.bfloat16)
    slots, rows, rank_columns = factor_ref.shape
    total = jnp.zeros((rows, rank_columns), jnp.float32)
    for s in range(slots):
        projected = lax.dot_general(
            x_ref[...], down_ref[s], (((1,), (1,)), ((), ())), preferred_element_type=jnp.float32
        )
        factor = factor_ref[s]
        total = total + jnp.where(factor > 0, projected * factor, 0.0)
    spare = LANES - rank_columns
    small = jnp.concatenate([total, jnp.zeros((rows, spare), jnp.float32)], axis=1)
    small_ref[...] = small.astype(small_ref.dtype)
    values = blocks[0][...].astype(jnp.float32)
    squares = jnp.sum(values * values, axis=1, keepdims=True) / width
    squares = split_wide(jnp.broadcast_to(squares, (block_rows, spare)))
    begin = pl.multiple_of(home * block_rows, block_rows)
    small_ref[pl.ds(begin, block_rows), rank_columns:] = squares.astype(small_ref.dtype)


def write_rows(acc, outs, n_y, n_z):
    z = lax.axis_index("gz")
    rows_here = outs[0].shape[0] // n_y
    for k in range(n_z):
        for y in range(n_y):
            owner = y * n_z + jnp.bitwise_xor(z, k)
            begin = pl.multiple_of(owner * rows_here, rows_here)
            outs[k][y * rows_here : (y + 1) * rows_here, :] = acc[
                pl.ds(begin, rows_here), :
            ].astype(outs[k].dtype)


def multiply(x_ref, weights, step, out, first):
    for weight in weights:
        width = weight.shape[1]
        wide = min(step, width)
        for c in range(0, width, wide):
            out[:, first + c : first + c + wide] = jnp.dot(
                x_ref[...], weight[:, c : c + wide], preferred_element_type=jnp.float32
            )
        first += width


def base_kernel(n_w, first, step, w_hbm, x_ref, *refs):
    weights, out_ref, rest = refs[:n_w], refs[n_w], refs[n_w + 1 :]
    copies = weight_copies(w_hbm, first, *rest) if rest else []
    for copy in copies:
        copy.start()

    @pl.when(lax.axis_index("gx") >= 0)
    def behind_the_copies():
        multiply(x_ref, weights, step, out_ref, 0)

    for copy in copies:
        copy.wait()


def last_kernel(n_w, step, x_ref, *refs):
    multiply(x_ref, refs[:n_w], step, refs[n_w], 0)


def product_kernel(n_w, n_y, n_z, step, first, x_ref, *refs):
    if first:
        base_ref, refs = refs[0], refs[2:]
    weights, outs, acc = refs[:n_w], refs[n_w:-1], refs[-1]
    if first:
        acc[:, :first] = base_ref[...]
    multiply(x_ref, weights, step, acc, first)
    write_rows(acc, outs, n_y, n_z)


def first_sums_kernel(n_y, n_z, last_ref, small_ref, *refs):
    parts, outs, last_outs = refs[:n_z], refs[n_z : n_z + n_y], refs[n_z + n_y :]
    pair_kernel(n_y, 0, *parts, *outs)
    columns = last_ref.shape[1]
    write_rows(last_ref, [out.at[:, :columns] for out in last_outs], n_y, n_z)
    write_rows(small_ref, [out.at[:, columns:] for out in last_outs], n_y, n_z)


def pair_kernel(n_y, rank_columns, *refs):
    parts, outs = refs[:-n_y], refs[-n_y:]
    rows_here, columns = outs[0].shape
    late = columns - (LANES if rank_columns else 0)
    y = lax.axis_index("gy")
    for k in range(n_y):
        begin = pl.multiple_of(jnp.bitwise_xor(y, k) * rows_here, rows_here)
        here = pl.ds(begin, rows_here)
        total = parts[0][here, :].astype(jnp.float32)
        for part in parts[1:]:
            total = total + part[here, :].astype(jnp.float32)
        outs[k][:, :late] = total[:, :late].astype(outs[k].dtype)
        if rank_columns:
            square = join_wide(total[:, late + rank_columns :])
            square = jnp.broadcast_to(square, (rows_here, LANES - rank_columns))
            side = [total[:, late : late + rank_columns], split_wide(square)]
            outs[k][:, late:] = jnp.concatenate(side, axis=1).astype(outs[k].dtype)


def final_kernel(n, n_z, step, spread_ref, up_ref, *refs):
    firsts, lasts, out_ref = refs[:n], refs[n : 2 * n], refs[2 * n]
    rows_here, columns = out_ref.shape
    done = firsts[0].shape[1]
    late = columns - done
    adapters, rank_columns, _ = up_ref.shape

    def added(parts, begin, end):
        total = parts[0][:, begin:end]
        for part in parts[1:]:
            total = total + part[:, begin:end].astype(jnp.float32)
        return total

    side = added(lasts, late, late + LANES)
    mean_sq = join_wide(side[:, rank_columns:])
    scale = lax.rsqrt(mean_sq + EPSILON)
    owner = lax.axis_index("gy") * n_z + lax.axis_index("gz")
    live = spread_ref[pl.ds(pl.multiple_of(owner * rows_here, rows_here), rows_here), :]
    spread = jnp.concatenate([side[:, :rank_columns]] * adapters, axis=1)
    spread = jnp.where(live > 0, spread, 0.0).astype(jnp.bfloat16)
    for c in range(0, columns, step):
        if c < done:
            base = added(firsts, c, c + step)
        else:
            base = added(lasts, c - done, c - done + step)
        up = up_ref[:, :, c : c + step].reshape(adapters * rank_columns, step)
        total = base + jnp.dot(spread, up, preferred_element_type=jnp.float32)
        value = jnp.where(mean_sq < jnp.inf, total * scale, 0.0)
        out_ref[:, c : c + step] = value.astype(out_ref.dtype)


def body(
    hidden,
    attention_norm_gain,
    query_weight,
    slot_down_factors,
    adapter_up_factors,
    adapter_of_row,
    padded_adapter_rank,
    adapter_in_slot,
    segment_starts,
):
    n_x, n_y, n_z = lax.axis_size("gx"), lax.axis_size("gy"), lax.axis_size("gz")
    groups = n_y * n_z
    block_rows, depth = hidden.shape
    columns = query_weight.shape[1]
    rows = n_x * block_rows
    rows_here = rows // groups

    def send(value, axis, n, k):
        return lax.ppermute(value, axis, [(j, j ^ k) for j in range(n)])

    def spread_out(made, axis, n):
        return [made[0]] + [send(made[k], axis, n, k) for k in range(1, n)]

    sent = {0: hidden}
    order = [0, *range(2, n_x, 2), 1, *range(3, n_x, 2)]
    for k in order[1:]:
        sent[k] = send(sent[k - 1], "gx", n_x, 1) if k % 2 else send(hidden, "gx", n_x, k)
    blocks = [sent[k] for k in order]

    step = min(1024, columns // 4)
    pieces = 8
    f32, bf16 = jnp.float32, jnp.bfloat16
    slots, rank_columns = slot_down_factors.shape[0], slot_down_factors.shape[2]
    adapters = adapter_up_factors.shape[0]
    quarter = columns // 4
    part = quarter // 4
    if part % LANES == 0:
        loads, late = ([quarter, quarter, part], [quarter]), quarter - part
        firsts = [0, quarter, 3 * quarter], [2 * quarter]
    else:
        loads, late = ([quarter, quarter], [quarter, quarter]), 0
        firsts = [0, quarter], [2 * quarter, 3 * quarter]
    kept = n_y * rows_here
    roomy = params(4 + (rows * depth >> 16))

    scalars = (padded_adapter_rank, adapter_in_slot, segment_starts)
    weight_hbm = pltpu.with_memory_space_constraint(query_weight, pltpu.HBM)
    load_cost = cost(300 * query_weight.size, query_weight.size)
    factor, spread, *weights = pl.pallas_call(
        functools.partial(first_load_kernel, len(loads[0]), firsts[0]),
        out_shape=[
            jax.ShapeDtypeStruct((slots, rows, rank_columns), f32),
            jax.ShapeDtypeStruct((rows, adapters * rank_columns), f32),
        ]
        + [pltpu.VMEM((depth, wide), query_weight.dtype) for wide in loads[0]],
        in_specs=[HBM] * 4,
        out_specs=[VMEM] * (2 + len(loads[0])),
        scratch_shapes=[
            pltpu.SemaphoreType.DMA((len(loads[0]), pieces)),
            pltpu.SemaphoreType.DMA((len(scalars),)),
            *[pltpu.SMEM(value.shape, value.dtype) for value in scalars],
        ],
        cost_estimate=load_cost,
        compiler_params=roomy,
        name="first_load",
    )(weight_hbm, *[pltpu.with_memory_space_constraint(v, pltpu.HBM) for v in scalars])
    weights += pl.pallas_call(
        functools.partial(last_load_kernel, len(loads[1]), firsts[1]),
        out_shape=[pltpu.VMEM((depth, wide), query_weight.dtype) for wide in loads[1]],
        in_specs=[HBM, ANY, ANY],
        out_specs=[VMEM] * len(loads[1]),
        scratch_shapes=[pltpu.SemaphoreType.DMA((len(loads[1]), pieces))],
        cost_estimate=load_cost,
        compiler_params=roomy,
        name="last_load",
    )(weight_hbm, factor, blocks[1])
    weights = [pltpu.with_memory_space_constraint(w, pltpu.VMEM) for w in weights]
    if late:
        weights[2:] = weights[:1:-1]

    x, small = pl.pallas_call(
        functools.partial(rows_kernel, order, depth * groups),
        out_shape=(
            jax.ShapeDtypeStruct((rows, depth), bf16),
            jax.ShapeDtypeStruct((rows, LANES), bf16),
        ),
        in_specs=[VMEM] * (3 + n_x),
        out_specs=(VMEM,) * 2,
        compiler_params=roomy,
        name="scaled_rows",
    )(attention_norm_gain, jnp.swapaxes(slot_down_factors, 1, 2), factor, *blocks)

    one_hop = small = small + send(small, "gx", n_x, 1)
    hop = 2
    while hop < n_x:
        small = small + send(small, "gx", n_x, hop)
        hop *= 2

    def shapes(n, shape):
        return [jax.ShapeDtypeStruct(shape, f32 if k == 0 else bf16) for k in range(n)]

    base, *rest = pl.pallas_call(
        functools.partial(base_kernel, 2, columns - late, step),
        out_shape=[jax.ShapeDtypeStruct((rows, 2 * quarter), f32)]
        + ([pltpu.VMEM((depth, late), query_weight.dtype)] if late else []),
        in_specs=[HBM] + [VMEM] * 3,
        out_specs=[VMEM] * (2 if late else 1),
        scratch_shapes=[pltpu.SemaphoreType.DMA((pieces,))] if late else [],
        cost_estimate=cost(4 * rows * depth * quarter, 4 * depth * quarter),
        compiler_params=roomy,
        name="first_columns",
    )(weight_hbm, x, *weights[:2])
    weights += [pltpu.with_memory_space_constraint(w, pltpu.VMEM) for w in rest]

    def product(some, bases, times, name):
        first = sum(part.shape[1] for part in bases[:1])
        wide = first + sum(w.shape[1] for w in some)
        made = pl.pallas_call(
            functools.partial(product_kernel, len(some), n_y, n_z, step, first),
            out_shape=shapes(n_z, (kept, wide)),
            in_specs=[VMEM] * (1 + len(bases) + len(some)),
            out_specs=[VMEM] * n_z,
            scratch_shapes=[pltpu.VMEM((rows, wide), f32)],
            cost_estimate=cost(2 * rows * depth * wide * times, 2 * depth * wide),
            compiler_params=roomy,
            name=name,
        )(x, *bases, *some)
        return spread_out(made, "gz", n_z)

    split = 3
    last_columns = sum(w.shape[1] for w in weights[split:])
    base_parts = product(weights[2:split], [base, one_hop], 4, "middle_columns")
    last = pl.pallas_call(
        functools.partial(last_kernel, len(weights) - split, step),
        out_shape=jax.ShapeDtypeStruct((rows, last_columns), f32),
        in_specs=[VMEM] * (len(weights) - split + 1),
        out_specs=VMEM,
        cost_estimate=cost(16 * rows * depth * quarter, 2 * depth * quarter),
        compiler_params=roomy,
        name="last_columns",
    )(x, *weights[split:])
    wide = base_parts[0].shape[1]
    made = pl.pallas_call(
        functools.partial(first_sums_kernel, n_y, n_z),
        out_shape=shapes(n_y, (rows_here, wide)) + shapes(n_z, (kept, last_columns + LANES)),
        in_specs=[VMEM] * (2 + n_z),
        out_specs=[VMEM] * (n_y + n_z),
        cost_estimate=cost(0, 0),
        compiler_params=roomy,
        name="first_sums",
    )(last, small, *base_parts)
    first_parts = spread_out(made[:n_y], "gy", n_y)
    lasts = spread_out(made[n_y:], "gz", n_z)

    made = pl.pallas_call(
        functools.partial(pair_kernel, n_y, rank_columns),
        out_shape=shapes(n_y, (rows_here, last_columns + LANES)),
        in_specs=[VMEM] * n_z,
        out_specs=[VMEM] * n_y,
        cost_estimate=cost(0, 0),
        compiler_params=roomy,
        name="last_sums",
    )(*lasts)
    last_parts = spread_out(made, "gy", n_y)

    return pl.pallas_call(
        functools.partial(final_kernel, n_y, n_z, min(512, columns // 4)),
        out_shape=jax.ShapeDtypeStruct((rows_here, columns), bf16),
        in_specs=[VMEM] * (2 + 2 * n_y),
        out_specs=VMEM,
        compiler_params=roomy,
        name="query_rows",
    )(spread, adapter_up_factors, *first_parts, *last_parts)


def solution(mesh):
    return jax.shard_map(
        body,
        mesh=mesh,
        in_specs=(
            P(("rep", "gx"), ("gy", "gz")),
            P(("gy", "gz")),
            P(("gy", "gz"), "gx"),
            P("gx", ("gy", "gz"), None),
            P(None, None, "gx"),
            P("rep"),
            P(),
            P(),
            P("rep"),
        ),
        out_specs=P(("rep", "gy", "gz"), "gx"),
        check_vma=False,
    )
```

```python
import functools

import jax
import jax.numpy as jnp
from jax import lax
from jax.experimental import pallas as pl
from jax.experimental.pallas import tpu as pltpu
from jax.sharding import PartitionSpec as P

EPSILON = 1e-05
ADAPTER_ALPHA = 32.0
LANES = 128
MIB = 1 << 20

VMEM = pl.BlockSpec(memory_space=pltpu.VMEM)
HBM = pl.BlockSpec(memory_space=pltpu.HBM)
ANY = pl.BlockSpec(memory_space=pl.ANY)


def params(mib):
    return pltpu.CompilerParams(vmem_limit_bytes=mib * MIB)


def cost(flops, moved):
    return pl.CostEstimate(flops=flops, bytes_accessed=moved, transcendentals=0)


def weight_copies(w_hbm, first, w_vmem, sems):
    pieces = sems.shape[0]
    depth, width = w_vmem.shape
    step = depth // pieces
    return [
        pltpu.make_async_copy(
            w_hbm.at[pl.ds(p * step, step), pl.ds(first, width)],
            w_vmem.at[pl.ds(p * step, step)],
            sems.at[p],
        )
        for p in range(pieces)
    ]


def load(w_hbm, firsts, weights, sems, meanwhile):
    copies = []
    for j, w_vmem in enumerate(weights):
        copies += weight_copies(w_hbm, firsts[j], w_vmem, sems.at[j])
    for copy in copies:
        copy.start()
    meanwhile()
    for copy in copies:
        copy.wait()


def first_load_kernel(n, firsts, w_hbm, rank_hbm, slot_hbm, start_hbm, factor_ref, spread_ref, *refs):
    weights, sems, scalar_sems = refs[:n], refs[n], refs[n + 1]
    rank_ref, slot_ref, start_ref = refs[n + 2 :]

    def masks():
        pairs = ((rank_hbm, rank_ref), (slot_hbm, slot_ref), (start_hbm, start_ref))
        scalars = [
            pltpu.make_async_copy(source, target, scalar_sems.at[j])
            for j, (source, target) in enumerate(pairs)
        ]
        for copy in scalars:
            copy.start()
        for copy in scalars:
            copy.wait()
        slots, rows, rank_columns = factor_ref.shape
        home = lax.axis_index("gx")
        row = lax.broadcasted_iota(jnp.int32, (rows, rank_columns), 0)
        col = lax.broadcasted_iota(jnp.int32, (rows, rank_columns), 1)
        for s in range(slots):
            adapter = slot_ref[home * slots + s]
            rank = rank_ref[adapter]
            live = (row >= start_ref[adapter]) & (row < start_ref[adapter + 1]) & (col < rank)
            ranks = jnp.full((rows, rank_columns), rank, jnp.int32).astype(jnp.float32)
            factor_ref[s] = jnp.where(live, ADAPTER_ALPHA / ranks, 0.0)
        adapters = spread_ref.shape[1] // rank_columns
        for a in range(adapters):
            live = (row >= start_ref[a]) & (row < start_ref[a + 1])
            spread_ref[:, a * rank_columns : (a + 1) * rank_columns] = jnp.where(live, 1.0, 0.0)

    load(w_hbm, firsts, weights, sems, masks)


def last_load_kernel(n, firsts, w_hbm, _, __, *refs):
    load(w_hbm, firsts, refs[:n], refs[n], lambda: None)


def split_wide(value):
    high = value.astype(jnp.bfloat16).astype(jnp.float32)
    low = jnp.where(high < jnp.inf, value - high, 0.0)
    lane = lax.broadcasted_iota(jnp.int32, value.shape, 1)
    return jnp.where(lane < value.shape[1] // 2, high, low)


def join_wide(value):
    return value[:, :1] + value[:, value.shape[1] - 1 :]


def rows_kernel(order, width, gain_ref, down_ref, factor_ref, *refs):
    n = len(order)
    blocks = refs[:n]
    x_ref, small_ref = refs[n:]
    home = lax.axis_index("gx")
    block_rows = blocks[0].shape[0]
    gain = gain_ref[...].astype(jnp.float32).reshape(1, gain_ref.shape[0])
    for k, block in zip(order, blocks):
        begin = pl.multiple_of(jnp.bitwise_xor(home, k) * block_rows, block_rows)
        values = block[...].astype(jnp.float32)
        x_ref[pl.ds(begin, block_rows), :] = (values * gain).astype(jnp.bfloat16)
    slots, rows, rank_columns = factor_ref.shape
    total = jnp.zeros((rows, rank_columns), jnp.float32)
    for s in range(slots):
        projected = lax.dot_general(
            x_ref[...], down_ref[s], (((1,), (1,)), ((), ())), preferred_element_type=jnp.float32
        )
        factor = factor_ref[s]
        total = total + jnp.where(factor > 0, projected * factor, 0.0)
    spare = LANES - rank_columns
    small = jnp.concatenate([total, jnp.zeros((rows, spare), jnp.float32)], axis=1)
    small_ref[...] = small.astype(small_ref.dtype)
    values = blocks[0][...].astype(jnp.float32)
    squares = jnp.sum(values * values, axis=1, keepdims=True) / width
    squares = split_wide(jnp.broadcast_to(squares, (block_rows, spare)))
    begin = pl.multiple_of(home * block_rows, block_rows)
    small_ref[pl.ds(begin, block_rows), rank_columns:] = squares.astype(small_ref.dtype)


def write_rows(acc, outs, n_y, n_z):
    z = lax.axis_index("gz")
    rows_here = outs[0].shape[0] // n_y
    for k in range(n_z):
        for y in range(n_y):
            owner = y * n_z + jnp.bitwise_xor(z, k)
            begin = pl.multiple_of(owner * rows_here, rows_here)
            outs[k][y * rows_here : (y + 1) * rows_here, :] = acc[
                pl.ds(begin, rows_here), :
            ].astype(outs[k].dtype)


def multiply(x_ref, weights, step, out, first):
    for weight in weights:
        width = weight.shape[1]
        wide = min(step, width)
        for c in range(0, width, wide):
            out[:, first + c : first + c + wide] = jnp.dot(
                x_ref[...], weight[:, c : c + wide], preferred_element_type=jnp.float32
            )
        first += width


def base_kernel(n_w, first, step, w_hbm, x_ref, *refs):
    weights, out_ref, rest = refs[:n_w], refs[n_w], refs[n_w + 1 :]
    copies = weight_copies(w_hbm, first, *rest) if rest else []
    for copy in copies:
        copy.start()

    @pl.when(lax.axis_index("gx") >= 0)
    def behind_the_copies():
        multiply(x_ref, weights, step, out_ref, 0)

    for copy in copies:
        copy.wait()


def last_kernel(n_w, step, x_ref, *refs):
    multiply(x_ref, refs[:n_w], step, refs[n_w], 0)


def product_kernel(n_w, n_y, n_z, step, first, x_ref, *refs):
    if first:
        base_ref, refs = refs[0], refs[2:]
    weights, outs, acc = refs[:n_w], refs[n_w:-1], refs[-1]
    if first:
        acc[:, :first] = base_ref[...]
    multiply(x_ref, weights, step, acc, first)
    write_rows(acc, outs, n_y, n_z)


def first_sums_kernel(n_y, n_z, last_ref, small_ref, *refs):
    parts, outs, last_outs = refs[:n_z], refs[n_z : n_z + n_y], refs[n_z + n_y :]
    pair_kernel(n_y, 0, *parts, *outs)
    columns = last_ref.shape[1]
    write_rows(last_ref, [out.at[:, :columns] for out in last_outs], n_y, n_z)
    write_rows(small_ref, [out.at[:, columns:] for out in last_outs], n_y, n_z)


def pair_kernel(n_y, rank_columns, *refs):
    parts, outs = refs[:-n_y], refs[-n_y:]
    rows_here, columns = outs[0].shape
    late = columns - (LANES if rank_columns else 0)
    y = lax.axis_index("gy")
    for k in range(n_y):
        begin = pl.multiple_of(jnp.bitwise_xor(y, k) * rows_here, rows_here)
        here = pl.ds(begin, rows_here)
        total = parts[0][here, :].astype(jnp.float32)
        for part in parts[1:]:
            total = total + part[here, :].astype(jnp.float32)
        outs[k][:, :late] = total[:, :late].astype(outs[k].dtype)
        if rank_columns:
            square = join_wide(total[:, late + rank_columns :])
            square = jnp.broadcast_to(square, (rows_here, LANES - rank_columns))
            side = [total[:, late : late + rank_columns], split_wide(square)]
            outs[k][:, late:] = jnp.concatenate(side, axis=1).astype(outs[k].dtype)


def final_kernel(n, n_z, step, spread_ref, up_ref, *refs):
    firsts, lasts, out_ref = refs[:n], refs[n : 2 * n], refs[2 * n]
    rows_here, columns = out_ref.shape
    done = firsts[0].shape[1]
    late = columns - done
    adapters, rank_columns, _ = up_ref.shape

    def added(parts, begin, end):
        total = parts[0][:, begin:end]
        for part in parts[1:]:
            total = total + part[:, begin:end].astype(jnp.float32)
        return total

    side = added(lasts, late, late + LANES)
    mean_sq = join_wide(side[:, rank_columns:])
    scale = lax.rsqrt(mean_sq + EPSILON)
    owner = lax.axis_index("gy") * n_z + lax.axis_index("gz")
    live = spread_ref[pl.ds(pl.multiple_of(owner * rows_here, rows_here), rows_here), :]
    spread = jnp.concatenate([side[:, :rank_columns]] * adapters, axis=1)
    spread = jnp.where(live > 0, spread, 0.0).astype(jnp.bfloat16)
    for c in range(0, columns, step):
        if c < done:
            base = added(firsts, c, c + step)
        else:
            base = added(lasts, c - done, c - done + step)
        up = up_ref[:, :, c : c + step].reshape(adapters * rank_columns, step)
        total = base + jnp.dot(spread, up, preferred_element_type=jnp.float32)
        value = jnp.where(mean_sq < jnp.inf, total * scale, 0.0)
        out_ref[:, c : c + step] = value.astype(out_ref.dtype)


def body(
    hidden,
    attention_norm_gain,
    query_weight,
    slot_down_factors,
    adapter_up_factors,
    adapter_of_row,
    padded_adapter_rank,
    adapter_in_slot,
    segment_starts,
):
    n_x, n_y, n_z = lax.axis_size("gx"), lax.axis_size("gy"), lax.axis_size("gz")
    groups = n_y * n_z
    block_rows, depth = hidden.shape
    columns = query_weight.shape[1]
    rows = n_x * block_rows
    rows_here = rows // groups

    def send(value, axis, n, k):
        return lax.ppermute(value, axis, [(j, j ^ k) for j in range(n)])

    def spread_out(made, axis, n):
        return [made[0]] + [send(made[k], axis, n, k) for k in range(1, n)]

    sent = {0: hidden}
    order = [0, *range(2, n_x, 2), 1, *range(3, n_x, 2)]
    for k in order[1:]:
        sent[k] = send(sent[k - 1], "gx", n_x, 1) if k % 2 else send(hidden, "gx", n_x, k)
    blocks = [sent[k] for k in order]

    step = min(1024, columns // 4)
    pieces = 8
    f32, bf16 = jnp.float32, jnp.bfloat16
    slots, rank_columns = slot_down_factors.shape[0], slot_down_factors.shape[2]
    adapters = adapter_up_factors.shape[0]
    quarter = columns // 4
    part = quarter // 4
    if part % LANES == 0:
        loads, late = ([quarter, quarter, part], [quarter]), quarter - part
        firsts = [0, quarter, 3 * quarter], [2 * quarter]
    else:
        loads, late = ([quarter, quarter], [quarter, quarter]), 0
        firsts = [0, quarter], [2 * quarter, 3 * quarter]
    kept = n_y * rows_here
    roomy = params(4 + (rows * depth >> 16))

    scalars = (padded_adapter_rank, adapter_in_slot, segment_starts)
    weight_hbm = pltpu.with_memory_space_constraint(query_weight, pltpu.HBM)
    load_cost = cost(300 * query_weight.size, query_weight.size)
    factor, spread, *weights = pl.pallas_call(
        functools.partial(first_load_kernel, len(loads[0]), firsts[0]),
        out_shape=[
            jax.ShapeDtypeStruct((slots, rows, rank_columns), f32),
            jax.ShapeDtypeStruct((rows, adapters * rank_columns), f32),
        ]
        + [pltpu.VMEM((depth, wide), query_weight.dtype) for wide in loads[0]],
        in_specs=[HBM] * 4,
        out_specs=[VMEM] * (2 + len(loads[0])),
        scratch_shapes=[
            pltpu.SemaphoreType.DMA((len(loads[0]), pieces)),
            pltpu.SemaphoreType.DMA((len(scalars),)),
            *[pltpu.SMEM(value.shape, value.dtype) for value in scalars],
        ],
        cost_estimate=load_cost,
        compiler_params=roomy,
        name="first_load",
    )(weight_hbm, *[pltpu.with_memory_space_constraint(v, pltpu.HBM) for v in scalars])
    weights += pl.pallas_call(
        functools.partial(last_load_kernel, len(loads[1]), firsts[1]),
        out_shape=[pltpu.VMEM((depth, wide), query_weight.dtype) for wide in loads[1]],
        in_specs=[HBM, ANY, ANY],
        out_specs=[VMEM] * len(loads[1]),
        scratch_shapes=[pltpu.SemaphoreType.DMA((len(loads[1]), pieces))],
        cost_estimate=load_cost,
        compiler_params=roomy,
        name="last_load",
    )(weight_hbm, factor, blocks[1])
    weights = [pltpu.with_memory_space_constraint(w, pltpu.VMEM) for w in weights]
    if late:
        weights[2:] = weights[:1:-1]

    x, small = pl.pallas_call(
        functools.partial(rows_kernel, order, depth * groups),
        out_shape=(
            jax.ShapeDtypeStruct((rows, depth), bf16),
            jax.ShapeDtypeStruct((rows, LANES), bf16),
        ),
        in_specs=[VMEM] * (3 + n_x),
        out_specs=(VMEM,) * 2,
        compiler_params=roomy,
        name="scaled_rows",
    )(attention_norm_gain, jnp.swapaxes(slot_down_factors, 1, 2), factor, *blocks)

    hop = n_x // 2
    crossed = small = small + send(small, "gx", n_x, hop)
    while hop > 1:
        hop //= 2
        small = small + send(small, "gx", n_x, hop)

    def shapes(n, shape):
        return [jax.ShapeDtypeStruct(shape, f32 if k == 0 else bf16) for k in range(n)]

    base, *rest = pl.pallas_call(
        functools.partial(base_kernel, 2, columns - late, step),
        out_shape=[jax.ShapeDtypeStruct((rows, 2 * quarter), f32)]
        + ([pltpu.VMEM((depth, late), query_weight.dtype)] if late else []),
        in_specs=[HBM] + [VMEM] * 3,
        out_specs=[VMEM] * (2 if late else 1),
        scratch_shapes=[pltpu.SemaphoreType.DMA((pieces,))] if late else [],
        cost_estimate=cost(4 * rows * depth * quarter, 4 * depth * quarter),
        compiler_params=roomy,
        name="first_columns",
    )(weight_hbm, x, *weights[:2])
    weights += [pltpu.with_memory_space_constraint(w, pltpu.VMEM) for w in rest]

    def product(some, bases, times, name):
        first = sum(part.shape[1] for part in bases[:1])
        wide = first + sum(w.shape[1] for w in some)
        made = pl.pallas_call(
            functools.partial(product_kernel, len(some), n_y, n_z, step, first),
            out_shape=shapes(n_z, (kept, wide)),
            in_specs=[VMEM] * (1 + len(bases) + len(some)),
            out_specs=[VMEM] * n_z,
            scratch_shapes=[pltpu.VMEM((rows, wide), f32)],
            cost_estimate=cost(2 * rows * depth * wide * times, 2 * depth * wide),
            compiler_params=roomy,
            name=name,
        )(x, *bases, *some)
        return spread_out(made, "gz", n_z)

    split = 3
    last_columns = sum(w.shape[1] for w in weights[split:])
    base_parts = product(weights[2:split], [base, crossed], 4, "middle_columns")
    last = pl.pallas_call(
        functools.partial(last_kernel, len(weights) - split, step),
        out_shape=jax.ShapeDtypeStruct((rows, last_columns), f32),
        in_specs=[VMEM] * (len(weights) - split + 1),
        out_specs=VMEM,
        cost_estimate=cost(16 * rows * depth * quarter, 2 * depth * quarter),
        compiler_params=roomy,
        name="last_columns",
    )(x, *weights[split:])
    wide = base_parts[0].shape[1]
    made = pl.pallas_call(
        functools.partial(first_sums_kernel, n_y, n_z),
        out_shape=shapes(n_y, (rows_here, wide)) + shapes(n_z, (kept, last_columns + LANES)),
        in_specs=[VMEM] * (2 + n_z),
        out_specs=[VMEM] * (n_y + n_z),
        cost_estimate=cost(0, 0),
        compiler_params=roomy,
        name="first_sums",
    )(last, small, *base_parts)
    first_parts = spread_out(made[:n_y], "gy", n_y)
    lasts = spread_out(made[n_y:], "gz", n_z)

    made = pl.pallas_call(
        functools.partial(pair_kernel, n_y, rank_columns),
        out_shape=shapes(n_y, (rows_here, last_columns + LANES)),
        in_specs=[VMEM] * n_z,
        out_specs=[VMEM] * n_y,
        cost_estimate=cost(0, 0),
        compiler_params=roomy,
        name="last_sums",
    )(*lasts)
    last_parts = spread_out(made, "gy", n_y)

    return pl.pallas_call(
        functools.partial(final_kernel, n_y, n_z, min(512, columns // 4)),
        out_shape=jax.ShapeDtypeStruct((rows_here, columns), bf16),
        in_specs=[VMEM] * (2 + 2 * n_y),
        out_specs=VMEM,
        compiler_params=roomy,
        name="query_rows",
    )(spread, adapter_up_factors, *first_parts, *last_parts)


def solution(mesh):
    return jax.shard_map(
        body,
        mesh=mesh,
        in_specs=(
            P(("rep", "gx"), ("gy", "gz")),
            P(("gy", "gz")),
            P(("gy", "gz"), "gx"),
            P("gx", ("gy", "gz"), None),
            P(None, None, "gx"),
            P("rep"),
            P(),
            P(),
            P("rep"),
        ),
        out_specs=P(("rep", "gy", "gz"), "gx"),
        check_vma=False,
    )
```

```python
import functools

import jax
import jax.numpy as jnp
from jax import lax
from jax.experimental import pallas as pl
from jax.experimental.pallas import tpu as pltpu
from jax.sharding import PartitionSpec as P

EPSILON = 1e-05
ADAPTER_ALPHA = 32.0
LANES = 128
MIB = 1 << 20

VMEM = pl.BlockSpec(memory_space=pltpu.VMEM)
HBM = pl.BlockSpec(memory_space=pltpu.HBM)
ANY = pl.BlockSpec(memory_space=pl.ANY)


def params(mib):
    return pltpu.CompilerParams(vmem_limit_bytes=mib * MIB)


def cost(flops, moved):
    return pl.CostEstimate(flops=flops, bytes_accessed=moved, transcendentals=0)


def weight_copies(w_hbm, first, w_vmem, sems):
    pieces = sems.shape[0]
    depth, width = w_vmem.shape
    step = depth // pieces
    return [
        pltpu.make_async_copy(
            w_hbm.at[pl.ds(p * step, step), pl.ds(first, width)],
            w_vmem.at[pl.ds(p * step, step)],
            sems.at[p],
        )
        for p in range(pieces)
    ]


def load(w_hbm, firsts, weights, sems, meanwhile):
    copies = []
    for j, w_vmem in enumerate(weights):
        copies += weight_copies(w_hbm, firsts[j], w_vmem, sems.at[j])
    for copy in copies:
        copy.start()
    meanwhile()
    for copy in copies:
        copy.wait()


def first_load_kernel(n, firsts, w_hbm, rank_hbm, slot_hbm, start_hbm, factor_ref, spread_ref, *refs):
    weights, sems, scalar_sems = refs[:n], refs[n], refs[n + 1]
    rank_ref, slot_ref, start_ref = refs[n + 2 :]

    def masks():
        pairs = ((rank_hbm, rank_ref), (slot_hbm, slot_ref), (start_hbm, start_ref))
        scalars = [
            pltpu.make_async_copy(source, target, scalar_sems.at[j])
            for j, (source, target) in enumerate(pairs)
        ]
        for copy in scalars:
            copy.start()
        for copy in scalars:
            copy.wait()
        slots, rows, rank_columns = factor_ref.shape
        home = lax.axis_index("gx")
        row = lax.broadcasted_iota(jnp.int32, (rows, rank_columns), 0)
        col = lax.broadcasted_iota(jnp.int32, (rows, rank_columns), 1)
        for s in range(slots):
            adapter = slot_ref[home * slots + s]
            rank = rank_ref[adapter]
            live = (row >= start_ref[adapter]) & (row < start_ref[adapter + 1]) & (col < rank)
            ranks = jnp.full((rows, rank_columns), rank, jnp.int32).astype(jnp.float32)
            factor_ref[s] = jnp.where(live, ADAPTER_ALPHA / ranks, 0.0)
        adapters = spread_ref.shape[1] // rank_columns
        for a in range(adapters):
            live = (row >= start_ref[a]) & (row < start_ref[a + 1])
            spread_ref[:, a * rank_columns : (a + 1) * rank_columns] = jnp.where(live, 1.0, 0.0)

    load(w_hbm, firsts, weights, sems, masks)


def last_load_kernel(n, firsts, w_hbm, _, __, *refs):
    load(w_hbm, firsts, refs[:n], refs[n], lambda: None)


def split_wide(value):
    high = value.astype(jnp.bfloat16).astype(jnp.float32)
    low = jnp.where(high < jnp.inf, value - high, 0.0)
    lane = lax.broadcasted_iota(jnp.int32, value.shape, 1)
    return jnp.where(lane < value.shape[1] // 2, high, low)


def join_wide(value):
    return value[:, :1] + value[:, value.shape[1] - 1 :]


def rows_kernel(order, width, gain_ref, down_ref, factor_ref, *refs):
    n = len(order)
    blocks = refs[:n]
    x_ref, small_ref = refs[n:]
    home = lax.axis_index("gx")
    block_rows = blocks[0].shape[0]
    gain = gain_ref[...].astype(jnp.float32).reshape(1, gain_ref.shape[0])
    for k, block in zip(order, blocks):
        begin = pl.multiple_of(jnp.bitwise_xor(home, k) * block_rows, block_rows)
        values = block[...].astype(jnp.float32)
        x_ref[pl.ds(begin, block_rows), :] = (values * gain).astype(jnp.bfloat16)
    slots, rows, rank_columns = factor_ref.shape
    total = jnp.zeros((rows, rank_columns), jnp.float32)
    for s in range(slots):
        projected = lax.dot_general(
            x_ref[...], down_ref[s], (((1,), (1,)), ((), ())), preferred_element_type=jnp.float32
        )
        factor = factor_ref[s]
        total = total + jnp.where(factor > 0, projected * factor, 0.0)
    spare = LANES - rank_columns
    small = jnp.concatenate([total, jnp.zeros((rows, spare), jnp.float32)], axis=1)
    small_ref[...] = small.astype(small_ref.dtype)
    values = blocks[0][...].astype(jnp.float32)
    squares = jnp.sum(values * values, axis=1, keepdims=True) / width
    squares = split_wide(jnp.broadcast_to(squares, (block_rows, spare)))
    begin = pl.multiple_of(home * block_rows, block_rows)
    small_ref[pl.ds(begin, block_rows), rank_columns:] = squares.astype(small_ref.dtype)


def write_rows(acc, outs, n_y, n_z):
    z = lax.axis_index("gz")
    rows_here = outs[0].shape[0] // n_y
    for k in range(n_z):
        for y in range(n_y):
            owner = y * n_z + jnp.bitwise_xor(z, k)
            begin = pl.multiple_of(owner * rows_here, rows_here)
            outs[k][y * rows_here : (y + 1) * rows_here, :] = acc[
                pl.ds(begin, rows_here), :
            ].astype(outs[k].dtype)


def multiply(x_ref, weights, step, out, first):
    for weight in weights:
        width = weight.shape[1]
        wide = min(step, width)
        for c in range(0, width, wide):
            out[:, first + c : first + c + wide] = jnp.dot(
                x_ref[...], weight[:, c : c + wide], preferred_element_type=jnp.float32
            )
        first += width


def base_kernel(n_w, first, step, w_hbm, x_ref, *refs):
    weights, out_ref, rest = refs[:n_w], refs[n_w], refs[n_w + 1 :]
    copies = weight_copies(w_hbm, first, *rest) if rest else []
    for copy in copies:
        copy.start()

    @pl.when(lax.axis_index("gx") >= 0)
    def behind_the_copies():
        multiply(x_ref, weights, step, out_ref, 0)

    for copy in copies:
        copy.wait()


def last_kernel(n_w, step, x_ref, *refs):
    multiply(x_ref, refs[:n_w], step, refs[n_w], 0)


def product_kernel(n_w, n_y, n_z, step, first, x_ref, *refs):
    if first:
        base_ref, refs = refs[0], refs[2:]
    weights, outs, acc = refs[:n_w], refs[n_w:-1], refs[-1]
    if first:
        acc[:, :first] = base_ref[...]
    multiply(x_ref, weights, step, acc, first)
    write_rows(acc, outs, n_y, n_z)


def first_sums_kernel(n_y, n_z, last_ref, small_ref, *refs):
    parts, outs, last_outs = refs[:n_z], refs[n_z : n_z + n_y], refs[n_z + n_y :]
    pair_kernel(n_y, 0, *parts, *outs)
    columns = last_ref.shape[1]
    write_rows(last_ref, [out.at[:, :columns] for out in last_outs], n_y, n_z)
    write_rows(small_ref, [out.at[:, columns:] for out in last_outs], n_y, n_z)


def pair_kernel(n_y, rank_columns, *refs):
    parts, outs = refs[:-n_y], refs[-n_y:]
    rows_here, columns = outs[0].shape
    late = columns - (LANES if rank_columns else 0)
    y = lax.axis_index("gy")
    for k in range(n_y):
        begin = pl.multiple_of(jnp.bitwise_xor(y, k) * rows_here, rows_here)
        here = pl.ds(begin, rows_here)
        total = parts[0][here, :].astype(jnp.float32)
        for part in parts[1:]:
            total = total + part[here, :].astype(jnp.float32)
        outs[k][:, :late] = total[:, :late].astype(outs[k].dtype)
        if rank_columns:
            square = join_wide(total[:, late + rank_columns :])
            square = jnp.broadcast_to(square, (rows_here, LANES - rank_columns))
            side = [total[:, late : late + rank_columns], split_wide(square)]
            outs[k][:, late:] = jnp.concatenate(side, axis=1).astype(outs[k].dtype)


def final_kernel(n, n_z, step, spread_ref, up_ref, *refs):
    firsts, lasts, out_ref = refs[:n], refs[n : 2 * n], refs[2 * n]
    rows_here, columns = out_ref.shape
    done = firsts[0].shape[1]
    late = columns - done
    adapters, rank_columns, _ = up_ref.shape

    def added(parts, begin, end):
        total = parts[0][:, begin:end]
        for part in parts[1:]:
            total = total + part[:, begin:end].astype(jnp.float32)
        return total

    side = added(lasts, late, late + LANES)
    mean_sq = join_wide(side[:, rank_columns:])
    scale = lax.rsqrt(mean_sq + EPSILON)
    owner = lax.axis_index("gy") * n_z + lax.axis_index("gz")
    live = spread_ref[pl.ds(pl.multiple_of(owner * rows_here, rows_here), rows_here), :]
    spread = jnp.concatenate([side[:, :rank_columns]] * adapters, axis=1)
    spread = jnp.where(live > 0, spread, 0.0).astype(jnp.bfloat16)
    for c in range(0, columns, step):
        if c < done:
            base = added(firsts, c, c + step)
        else:
            base = added(lasts, c - done, c - done + step)
        up = up_ref[:, :, c : c + step].reshape(adapters * rank_columns, step)
        total = base + jnp.dot(spread, up, preferred_element_type=jnp.float32)
        value = jnp.where(mean_sq < jnp.inf, total * scale, 0.0)
        out_ref[:, c : c + step] = value.astype(out_ref.dtype)


def body(
    hidden,
    attention_norm_gain,
    query_weight,
    slot_down_factors,
    adapter_up_factors,
    adapter_of_row,
    padded_adapter_rank,
    adapter_in_slot,
    segment_starts,
):
    n_x, n_y, n_z = lax.axis_size("gx"), lax.axis_size("gy"), lax.axis_size("gz")
    groups = n_y * n_z
    block_rows, depth = hidden.shape
    columns = query_weight.shape[1]
    rows = n_x * block_rows
    rows_here = rows // groups

    def send(value, axis, n, k):
        return lax.ppermute(value, axis, [(j, j ^ k) for j in range(n)])

    def spread_out(made, axis, n):
        return [made[0]] + [send(made[k], axis, n, k) for k in range(1, n)]

    sent = {0: hidden}
    order = [0, *range(2, n_x, 2), 1, *range(3, n_x, 2)]
    for k in order[1:]:
        sent[k] = send(sent[k - 1], "gx", n_x, 1) if k % 2 else send(hidden, "gx", n_x, k)
    blocks = [sent[k] for k in order]

    step = min(1024, columns // 4)
    pieces = 8
    f32, bf16 = jnp.float32, jnp.bfloat16
    slots, rank_columns = slot_down_factors.shape[0], slot_down_factors.shape[2]
    adapters = adapter_up_factors.shape[0]
    quarter = columns // 4
    part = quarter // 4
    if part % LANES == 0:
        loads, late = ([quarter, quarter, part], [quarter]), quarter - part
        firsts = [0, quarter, 2 * quarter], [2 * quarter + part]
    else:
        loads, late = ([quarter, quarter], [quarter, quarter]), 0
        firsts = [0, quarter], [2 * quarter, 3 * quarter]
    kept = n_y * rows_here
    roomy = params(4 + (rows * depth >> 16))

    scalars = (padded_adapter_rank, adapter_in_slot, segment_starts)
    weight_hbm = pltpu.with_memory_space_constraint(query_weight, pltpu.HBM)
    load_cost = cost(300 * query_weight.size, query_weight.size)
    factor, spread, *weights = pl.pallas_call(
        functools.partial(first_load_kernel, len(loads[0]), firsts[0]),
        out_shape=[
            jax.ShapeDtypeStruct((slots, rows, rank_columns), f32),
            jax.ShapeDtypeStruct((rows, adapters * rank_columns), f32),
        ]
        + [pltpu.VMEM((depth, wide), query_weight.dtype) for wide in loads[0]],
        in_specs=[HBM] * 4,
        out_specs=[VMEM] * (2 + len(loads[0])),
        scratch_shapes=[
            pltpu.SemaphoreType.DMA((len(loads[0]), pieces)),
            pltpu.SemaphoreType.DMA((len(scalars),)),
            *[pltpu.SMEM(value.shape, value.dtype) for value in scalars],
        ],
        cost_estimate=load_cost,
        compiler_params=roomy,
        name="first_load",
    )(weight_hbm, *[pltpu.with_memory_space_constraint(v, pltpu.HBM) for v in scalars])
    weights += pl.pallas_call(
        functools.partial(last_load_kernel, len(loads[1]), firsts[1]),
        out_shape=[pltpu.VMEM((depth, wide), query_weight.dtype) for wide in loads[1]],
        in_specs=[HBM, ANY, ANY],
        out_specs=[VMEM] * len(loads[1]),
        scratch_shapes=[pltpu.SemaphoreType.DMA((len(loads[1]), pieces))],
        cost_estimate=load_cost,
        compiler_params=roomy,
        name="last_load",
    )(weight_hbm, factor, blocks[1])
    weights = [pltpu.with_memory_space_constraint(w, pltpu.VMEM) for w in weights]
    soon = 3 if late else 2
    base_columns = sum(w.shape[1] for w in weights[:soon])

    x, small = pl.pallas_call(
        functools.partial(rows_kernel, order, depth * groups),
        out_shape=(
            jax.ShapeDtypeStruct((rows, depth), bf16),
            jax.ShapeDtypeStruct((rows, LANES), bf16),
        ),
        in_specs=[VMEM] * (3 + n_x),
        out_specs=(VMEM,) * 2,
        compiler_params=roomy,
        name="scaled_rows",
    )(attention_norm_gain, jnp.swapaxes(slot_down_factors, 1, 2), factor, *blocks)

    hop = n_x // 2
    crossed = small = small + send(small, "gx", n_x, hop)
    while hop > 1:
        hop //= 2
        small = small + send(small, "gx", n_x, hop)

    def shapes(n, shape):
        return [jax.ShapeDtypeStruct(shape, f32 if k == 0 else bf16) for k in range(n)]

    base, *rest = pl.pallas_call(
        functools.partial(base_kernel, soon, columns - late, step),
        out_shape=[jax.ShapeDtypeStruct((rows, base_columns), f32)]
        + ([pltpu.VMEM((depth, late), query_weight.dtype)] if late else []),
        in_specs=[HBM] + [VMEM] * (1 + soon),
        out_specs=[VMEM] * (2 if late else 1),
        scratch_shapes=[pltpu.SemaphoreType.DMA((pieces,))] if late else [],
        cost_estimate=cost(4 * rows * depth * quarter, 4 * depth * quarter),
        compiler_params=roomy,
        name="first_columns",
    )(weight_hbm, x, *weights[:soon])
    weights += [pltpu.with_memory_space_constraint(w, pltpu.VMEM) for w in rest]

    def product(some, bases, times, name):
        first = sum(part.shape[1] for part in bases[:1])
        wide = first + sum(w.shape[1] for w in some)
        made = pl.pallas_call(
            functools.partial(product_kernel, len(some), n_y, n_z, step, first),
            out_shape=shapes(n_z, (kept, wide)),
            in_specs=[VMEM] * (1 + len(bases) + len(some)),
            out_specs=[VMEM] * n_z,
            scratch_shapes=[pltpu.VMEM((rows, wide), f32)],
            cost_estimate=cost(2 * rows * depth * wide * times, 2 * depth * wide),
            compiler_params=roomy,
            name=name,
        )(x, *bases, *some)
        return spread_out(made, "gz", n_z)

    split = soon + 1
    last_columns = sum(w.shape[1] for w in weights[split:])
    base_parts = product(weights[soon:split], [base, crossed], 4, "middle_columns")
    last = pl.pallas_call(
        functools.partial(last_kernel, len(weights) - split, step),
        out_shape=jax.ShapeDtypeStruct((rows, last_columns), f32),
        in_specs=[VMEM] * (len(weights) - split + 1),
        out_specs=VMEM,
        cost_estimate=cost(16 * rows * depth * quarter, 2 * depth * quarter),
        compiler_params=roomy,
        name="last_columns",
    )(x, *weights[split:])
    wide = base_parts[0].shape[1]
    made = pl.pallas_call(
        functools.partial(first_sums_kernel, n_y, n_z),
        out_shape=shapes(n_y, (rows_here, wide)) + shapes(n_z, (kept, last_columns + LANES)),
        in_specs=[VMEM] * (2 + n_z),
        out_specs=[VMEM] * (n_y + n_z),
        cost_estimate=cost(0, 0),
        compiler_params=roomy,
        name="first_sums",
    )(last, small, *base_parts)
    first_parts = spread_out(made[:n_y], "gy", n_y)
    lasts = spread_out(made[n_y:], "gz", n_z)

    made = pl.pallas_call(
        functools.partial(pair_kernel, n_y, rank_columns),
        out_shape=shapes(n_y, (rows_here, last_columns + LANES)),
        in_specs=[VMEM] * n_z,
        out_specs=[VMEM] * n_y,
        cost_estimate=cost(0, 0),
        compiler_params=roomy,
        name="last_sums",
    )(*lasts)
    last_parts = spread_out(made, "gy", n_y)

    return pl.pallas_call(
        functools.partial(final_kernel, n_y, n_z, min(256, columns // 4)),
        out_shape=jax.ShapeDtypeStruct((rows_here, columns), bf16),
        in_specs=[VMEM] * (2 + 2 * n_y),
        out_specs=VMEM,
        compiler_params=roomy,
        name="query_rows",
    )(spread, adapter_up_factors, *first_parts, *last_parts)


def solution(mesh):
    return jax.shard_map(
        body,
        mesh=mesh,
        in_specs=(
            P(("rep", "gx"), ("gy", "gz")),
            P(("gy", "gz")),
            P(("gy", "gz"), "gx"),
            P("gx", ("gy", "gz"), None),
            P(None, None, "gx"),
            P("rep"),
            P(),
            P(),
            P("rep"),
        ),
        out_specs=P(("rep", "gy", "gz"), "gx"),
        check_vma=False,
    )
```

```python
import functools

import jax
import jax.numpy as jnp
from jax import lax
from jax.experimental import pallas as pl
from jax.experimental.pallas import tpu as pltpu
from jax.sharding import PartitionSpec as P

EPSILON = 1e-05
ADAPTER_ALPHA = 32.0
LANES = 128
MIB = 1 << 20

VMEM = pl.BlockSpec(memory_space=pltpu.VMEM)
HBM = pl.BlockSpec(memory_space=pltpu.HBM)
ANY = pl.BlockSpec(memory_space=pl.ANY)


def params(mib):
    return pltpu.CompilerParams(vmem_limit_bytes=mib * MIB)


def cost(flops, moved):
    return pl.CostEstimate(flops=flops, bytes_accessed=moved, transcendentals=0)


def weight_copies(w_hbm, first, w_vmem, sems):
    pieces = sems.shape[0]
    depth, width = w_vmem.shape
    step = depth // pieces
    return [
        pltpu.make_async_copy(
            w_hbm.at[pl.ds(p * step, step), pl.ds(first, width)],
            w_vmem.at[pl.ds(p * step, step)],
            sems.at[p],
        )
        for p in range(pieces)
    ]


def load(w_hbm, firsts, weights, sems, meanwhile):
    copies = []
    for j, w_vmem in enumerate(weights):
        copies += weight_copies(w_hbm, firsts[j], w_vmem, sems.at[j])
    for copy in copies:
        copy.start()
    meanwhile()
    for copy in copies:
        copy.wait()


def first_load_kernel(n, firsts, w_hbm, rank_hbm, slot_hbm, start_hbm, factor_ref, spread_ref, *refs):
    weights, sems, scalar_sems = refs[:n], refs[n], refs[n + 1]
    rank_ref, slot_ref, start_ref = refs[n + 2 :]

    def masks():
        pairs = ((rank_hbm, rank_ref), (slot_hbm, slot_ref), (start_hbm, start_ref))
        scalars = [
            pltpu.make_async_copy(source, target, scalar_sems.at[j])
            for j, (source, target) in enumerate(pairs)
        ]
        for copy in scalars:
            copy.start()
        for copy in scalars:
            copy.wait()
        slots, rows, rank_columns = factor_ref.shape
        home = lax.axis_index("gx")
        row = lax.broadcasted_iota(jnp.int32, (rows, rank_columns), 0)
        col = lax.broadcasted_iota(jnp.int32, (rows, rank_columns), 1)
        for s in range(slots):
            adapter = slot_ref[home * slots + s]
            rank = rank_ref[adapter]
            live = (row >= start_ref[adapter]) & (row < start_ref[adapter + 1]) & (col < rank)
            ranks = jnp.full((rows, rank_columns), rank, jnp.int32).astype(jnp.float32)
            factor_ref[s] = jnp.where(live, ADAPTER_ALPHA / ranks, 0.0)
        adapters = spread_ref.shape[1] // rank_columns
        for a in range(adapters):
            live = (row >= start_ref[a]) & (row < start_ref[a + 1])
            spread_ref[:, a * rank_columns : (a + 1) * rank_columns] = jnp.where(live, 1.0, 0.0)

    load(w_hbm, firsts, weights, sems, masks)


def last_load_kernel(n, firsts, w_hbm, _, __, *refs):
    load(w_hbm, firsts, refs[:n], refs[n], lambda: None)


def split_wide(value):
    high = value.astype(jnp.bfloat16).astype(jnp.float32)
    low = jnp.where(high < jnp.inf, value - high, 0.0)
    lane = lax.broadcasted_iota(jnp.int32, value.shape, 1)
    return jnp.where(lane < value.shape[1] // 2, high, low)


def join_wide(value):
    return value[:, :1] + value[:, value.shape[1] - 1 :]


def rows_kernel(order, width, gain_ref, down_ref, factor_ref, *refs):
    n = len(order)
    blocks = refs[:n]
    x_ref, small_ref = refs[n:]
    home = lax.axis_index("gx")
    block_rows = blocks[0].shape[0]
    gain = gain_ref[...].astype(jnp.float32).reshape(1, gain_ref.shape[0])
    for k, block in zip(order, blocks):
        begin = pl.multiple_of(jnp.bitwise_xor(home, k) * block_rows, block_rows)
        values = block[...].astype(jnp.float32)
        x_ref[pl.ds(begin, block_rows), :] = (values * gain).astype(jnp.bfloat16)
    slots, rows, rank_columns = factor_ref.shape
    total = jnp.zeros((rows, rank_columns), jnp.float32)
    for s in range(slots):
        projected = lax.dot_general(
            x_ref[...], down_ref[s], (((1,), (1,)), ((), ())), preferred_element_type=jnp.float32
        )
        factor = factor_ref[s]
        total = total + jnp.where(factor > 0, projected * factor, 0.0)
    spare = LANES - rank_columns
    small = jnp.concatenate([total, jnp.zeros((rows, spare), jnp.float32)], axis=1)
    small_ref[...] = small.astype(small_ref.dtype)
    values = blocks[0][...].astype(jnp.float32)
    squares = jnp.sum(values * values, axis=1, keepdims=True) / width
    squares = split_wide(jnp.broadcast_to(squares, (block_rows, spare)))
    begin = pl.multiple_of(home * block_rows, block_rows)
    small_ref[pl.ds(begin, block_rows), rank_columns:] = squares.astype(small_ref.dtype)


def write_rows(acc, outs, n_y, n_z):
    z = lax.axis_index("gz")
    rows_here = outs[0].shape[0] // n_y
    for k in range(n_z):
        for y in range(n_y):
            owner = y * n_z + jnp.bitwise_xor(z, k)
            begin = pl.multiple_of(owner * rows_here, rows_here)
            outs[k][y * rows_here : (y + 1) * rows_here, :] = acc[
                pl.ds(begin, rows_here), :
            ].astype(outs[k].dtype)


def multiply(x_ref, weights, step, out, first):
    for weight in weights:
        width = weight.shape[1]
        wide = min(step, width)
        for c in range(0, width, wide):
            out[:, first + c : first + c + wide] = jnp.dot(
                x_ref[...], weight[:, c : c + wide], preferred_element_type=jnp.float32
            )
        first += width


def base_kernel(n_w, first, step, w_hbm, x_ref, *refs):
    weights, out_ref, rest = refs[:n_w], refs[n_w], refs[n_w + 1 :]
    copies = weight_copies(w_hbm, first, *rest) if rest else []
    for copy in copies:
        copy.start()

    @pl.when(lax.axis_index("gx") >= 0)
    def behind_the_copies():
        multiply(x_ref, weights, step, out_ref, 0)

    for copy in copies:
        copy.wait()


def last_kernel(n_w, step, x_ref, *refs):
    multiply(x_ref, refs[:n_w], step, refs[n_w], 0)


def product_kernel(n_w, n_y, n_z, step, first, x_ref, *refs):
    if first:
        base_ref, refs = refs[0], refs[2:]
    weights, outs, acc = refs[:n_w], refs[n_w:-1], refs[-1]
    if first:
        acc[:, :first] = base_ref[...]
    multiply(x_ref, weights, step, acc, first)
    write_rows(acc, outs, n_y, n_z)


def first_sums_kernel(n_y, n_z, last_ref, small_ref, *refs):
    parts, outs, last_outs = refs[:n_z], refs[n_z : n_z + n_y], refs[n_z + n_y :]
    pair_kernel(n_y, 0, *parts, *outs)
    columns = last_ref.shape[1]
    write_rows(last_ref, [out.at[:, :columns] for out in last_outs], n_y, n_z)
    write_rows(small_ref, [out.at[:, columns:] for out in last_outs], n_y, n_z)


def pair_kernel(n_y, rank_columns, *refs):
    parts, outs = refs[:-n_y], refs[-n_y:]
    rows_here, columns = outs[0].shape
    late = columns - (LANES if rank_columns else 0)
    y = lax.axis_index("gy")
    for k in range(n_y):
        begin = pl.multiple_of(jnp.bitwise_xor(y, k) * rows_here, rows_here)
        here = pl.ds(begin, rows_here)
        total = parts[0][here, :].astype(jnp.float32)
        for part in parts[1:]:
            total = total + part[here, :].astype(jnp.float32)
        outs[k][:, :late] = total[:, :late].astype(outs[k].dtype)
        if rank_columns:
            square = join_wide(total[:, late + rank_columns :])
            square = jnp.broadcast_to(square, (rows_here, LANES - rank_columns))
            side = [total[:, late : late + rank_columns], split_wide(square)]
            outs[k][:, late:] = jnp.concatenate(side, axis=1).astype(outs[k].dtype)


def final_kernel(n, n_z, step, spread_ref, up_ref, *refs):
    firsts, lasts, out_ref = refs[:n], refs[n : 2 * n], refs[2 * n]
    rows_here, columns = out_ref.shape
    done = firsts[0].shape[1]
    late = columns - done
    adapters, rank_columns, _ = up_ref.shape

    def added(parts, begin, end):
        total = parts[0][:, begin:end]
        for part in parts[1:]:
            total = total + part[:, begin:end].astype(jnp.float32)
        return total

    side = added(lasts, late, late + LANES)
    mean_sq = join_wide(side[:, rank_columns:])
    scale = lax.rsqrt(mean_sq + EPSILON)
    owner = lax.axis_index("gy") * n_z + lax.axis_index("gz")
    live = spread_ref[pl.ds(pl.multiple_of(owner * rows_here, rows_here), rows_here), :]
    spread = jnp.concatenate([side[:, :rank_columns]] * adapters, axis=1)
    spread = jnp.where(live > 0, spread, 0.0).astype(jnp.bfloat16)
    for c in range(0, columns, step):
        if c < done:
            base = added(firsts, c, c + step)
        else:
            base = added(lasts, c - done, c - done + step)
        up = up_ref[:, :, c : c + step].reshape(adapters * rank_columns, step)
        total = base + jnp.dot(spread, up, preferred_element_type=jnp.float32)
        value = jnp.where(mean_sq < jnp.inf, total * scale, 0.0)
        out_ref[:, c : c + step] = value.astype(out_ref.dtype)


def body(
    hidden,
    attention_norm_gain,
    query_weight,
    slot_down_factors,
    adapter_up_factors,
    adapter_of_row,
    padded_adapter_rank,
    adapter_in_slot,
    segment_starts,
):
    n_x, n_y, n_z = lax.axis_size("gx"), lax.axis_size("gy"), lax.axis_size("gz")
    groups = n_y * n_z
    block_rows, depth = hidden.shape
    columns = query_weight.shape[1]
    rows = n_x * block_rows
    rows_here = rows // groups

    def send(value, axis, n, k):
        return lax.ppermute(value, axis, [(j, j ^ k) for j in range(n)])

    def spread_out(made, axis, n):
        return [made[0]] + [send(made[k], axis, n, k) for k in range(1, n)]

    sent = {0: hidden}
    order = [0, *range(2, n_x, 2), 1, *range(3, n_x, 2)]
    for k in order[1:]:
        sent[k] = send(sent[k - 1], "gx", n_x, 1) if k % 2 else send(hidden, "gx", n_x, k)
    blocks = [sent[k] for k in order]

    step = min(1024, columns // 4)
    pieces = 8
    f32, bf16 = jnp.float32, jnp.bfloat16
    slots, rank_columns = slot_down_factors.shape[0], slot_down_factors.shape[2]
    adapters = adapter_up_factors.shape[0]
    quarter = columns // 4
    part = quarter // 4
    if part % LANES == 0:
        loads, late = ([quarter, quarter, part], [quarter]), quarter - part
        firsts = [0, quarter, 2 * quarter], [2 * quarter + part]
    else:
        loads, late = ([quarter, quarter], [quarter, quarter]), 0
        firsts = [0, quarter], [2 * quarter, 3 * quarter]
    kept = n_y * rows_here
    roomy = params(4 + (rows * depth >> 16))

    scalars = (padded_adapter_rank, adapter_in_slot, segment_starts)
    weight_hbm = pltpu.with_memory_space_constraint(query_weight, pltpu.HBM)
    load_cost = cost(300 * query_weight.size, query_weight.size)
    factor, spread, *weights = pl.pallas_call(
        functools.partial(first_load_kernel, len(loads[0]), firsts[0]),
        out_shape=[
            jax.ShapeDtypeStruct((slots, rows, rank_columns), f32),
            jax.ShapeDtypeStruct((rows, adapters * rank_columns), f32),
        ]
        + [pltpu.VMEM((depth, wide), query_weight.dtype) for wide in loads[0]],
        in_specs=[HBM] * 4,
        out_specs=[VMEM] * (2 + len(loads[0])),
        scratch_shapes=[
            pltpu.SemaphoreType.DMA((len(loads[0]), pieces)),
            pltpu.SemaphoreType.DMA((len(scalars),)),
            *[pltpu.SMEM(value.shape, value.dtype) for value in scalars],
        ],
        cost_estimate=load_cost,
        compiler_params=roomy,
        name="first_load",
    )(weight_hbm, *[pltpu.with_memory_space_constraint(v, pltpu.HBM) for v in scalars])
    weights += pl.pallas_call(
        functools.partial(last_load_kernel, len(loads[1]), firsts[1]),
        out_shape=[pltpu.VMEM((depth, wide), query_weight.dtype) for wide in loads[1]],
        in_specs=[HBM, ANY, ANY],
        out_specs=[VMEM] * len(loads[1]),
        scratch_shapes=[pltpu.SemaphoreType.DMA((len(loads[1]), pieces))],
        cost_estimate=load_cost,
        compiler_params=roomy,
        name="last_load",
    )(weight_hbm, factor, blocks[1])
    weights = [pltpu.with_memory_space_constraint(w, pltpu.VMEM) for w in weights]
    soon = 3 if late else 2
    base_columns = sum(w.shape[1] for w in weights[:soon])

    x, small = pl.pallas_call(
        functools.partial(rows_kernel, order, depth * groups),
        out_shape=(
            jax.ShapeDtypeStruct((rows, depth), bf16),
            jax.ShapeDtypeStruct((rows, LANES), bf16),
        ),
        in_specs=[VMEM] * (3 + n_x),
        out_specs=(VMEM,) * 2,
        compiler_params=roomy,
        name="scaled_rows",
    )(attention_norm_gain, jnp.swapaxes(slot_down_factors, 1, 2), factor, *blocks)

    hop = n_x // 2
    crossed = small = small + send(small, "gx", n_x, hop)
    while hop > 1:
        hop //= 2
        small = small + send(small, "gx", n_x, hop)

    def shapes(n, shape):
        return [jax.ShapeDtypeStruct(shape, f32 if k == 0 else bf16) for k in range(n)]

    base, *rest = pl.pallas_call(
        functools.partial(base_kernel, soon, columns - late, step),
        out_shape=[jax.ShapeDtypeStruct((rows, base_columns), f32)]
        + ([pltpu.VMEM((depth, late), query_weight.dtype)] if late else []),
        in_specs=[HBM] + [VMEM] * (1 + soon),
        out_specs=[VMEM] * (2 if late else 1),
        scratch_shapes=[pltpu.SemaphoreType.DMA((pieces,))] if late else [],
        cost_estimate=cost(4 * rows * depth * quarter, 4 * depth * quarter),
        compiler_params=roomy,
        name="first_columns",
    )(weight_hbm, x, *weights[:soon])
    weights += [pltpu.with_memory_space_constraint(w, pltpu.VMEM) for w in rest]

    def product(some, bases, times, name):
        first = sum(part.shape[1] for part in bases[:1])
        wide = first + sum(w.shape[1] for w in some)
        made = pl.pallas_call(
            functools.partial(product_kernel, len(some), n_y, n_z, step, first),
            out_shape=shapes(n_z, (kept, wide)),
            in_specs=[VMEM] * (1 + len(bases) + len(some)),
            out_specs=[VMEM] * n_z,
            scratch_shapes=[pltpu.VMEM((rows, wide), f32)],
            cost_estimate=cost(2 * rows * depth * wide * times, 2 * depth * wide),
            compiler_params=roomy,
            name=name,
        )(x, *bases, *some)
        return spread_out(made, "gz", n_z)

    split = soon + 1
    last_columns = sum(w.shape[1] for w in weights[split:])
    base_parts = product(weights[soon:split], [base, crossed], 4, "middle_columns")
    last = pl.pallas_call(
        functools.partial(last_kernel, len(weights) - split, step),
        out_shape=jax.ShapeDtypeStruct((rows, last_columns), f32),
        in_specs=[VMEM] * (len(weights) - split + 1),
        out_specs=VMEM,
        cost_estimate=cost(16 * rows * depth * quarter, 2 * depth * quarter),
        compiler_params=roomy,
        name="last_columns",
    )(x, *weights[split:])
    wide = base_parts[0].shape[1]
    made = pl.pallas_call(
        functools.partial(first_sums_kernel, n_y, n_z),
        out_shape=shapes(n_y, (rows_here, wide)) + shapes(n_z, (kept, last_columns + LANES)),
        in_specs=[VMEM] * (2 + n_z),
        out_specs=[VMEM] * (n_y + n_z),
        cost_estimate=cost(0, 0),
        compiler_params=roomy,
        name="first_sums",
    )(last, small, *base_parts)
    first_parts = spread_out(made[:n_y], "gy", n_y)
    lasts = spread_out(made[n_y:], "gz", n_z)

    made = pl.pallas_call(
        functools.partial(pair_kernel, n_y, rank_columns),
        out_shape=shapes(n_y, (rows_here, last_columns + LANES)),
        in_specs=[VMEM] * n_z,
        out_specs=[VMEM] * n_y,
        cost_estimate=cost(4 * rows * depth * quarter, 0),
        compiler_params=roomy,
        name="last_sums",
    )(*lasts)
    last_parts = spread_out(made, "gy", n_y)

    return pl.pallas_call(
        functools.partial(final_kernel, n_y, n_z, min(256, columns // 4)),
        out_shape=jax.ShapeDtypeStruct((rows_here, columns), bf16),
        in_specs=[VMEM] * (2 + 2 * n_y),
        out_specs=VMEM,
        compiler_params=roomy,
        name="query_rows",
    )(spread, adapter_up_factors, *first_parts, *last_parts)


def solution(mesh):
    return jax.shard_map(
        body,
        mesh=mesh,
        in_specs=(
            P(("rep", "gx"), ("gy", "gz")),
            P(("gy", "gz")),
            P(("gy", "gz"), "gx"),
            P("gx", ("gy", "gz"), None),
            P(None, None, "gx"),
            P("rep"),
            P(),
            P(),
            P("rep"),
        ),
        out_specs=P(("rep", "gy", "gz"), "gx"),
        check_vma=False,
    )
```
